32 devices in a mesh: grp: 4 (over y, x), key: 8 (over z, core).
Axes of the slice: x: 2, y: 2, z: 4, core: 2. Of those that a mesh axis runs over, the one named last changes fastest.
Arguments:
- tokens: bfloat16 [8, 2048, 1024], P('grp', 'key'), may hold values from -6 to 6
- token_docs: int32 [8, 2048], P('grp', 'key'), may hold values from 0 to 7, as said below
- memory_docs: int32 [8, 2048], P('grp', 'key'), may hold values from 0 to 3
- memory_resets: int32 [8], P('grp'), may hold values 0 or 1
- memory_keys: bfloat16 [8, 2048, 1024], P('grp', 'key'), may hold values from -6 to 6
- memory_values: bfloat16 [8, 2048, 1024], P('grp', 'key'), may hold values from -6 to 6
- attn_gain1: bfloat16 [1024], P(('grp', 'key')), may hold values from 0.5 to 1.5
- query_weight1: bfloat16 [1024, 1024], P(('grp', 'key')), may hold values from -0.1875 to 0.1875
- key_weight1: bfloat16 [1024, 1024], P(('grp', 'key')), may hold values from -0.1875 to 0.1875
- value_weight1: bfloat16 [1024, 1024], P(('grp', 'key')), may hold values from -0.1875 to 0.1875
- out_weight1: bfloat16 [1024, 1024], P(('grp', 'key')), may hold values from -0.75 to 0.75
- ffn_gain1: bfloat16 [1024], P(('grp', 'key')), may hold values from 0.5 to 1.5
- gate_weight1: bfloat16 [1024, 2816], P(('grp', 'key')), may hold values from -0.1875 to 0.1875
- up_weight1: bfloat16 [1024, 2816], P(('grp', 'key')), may hold values from -0.1875 to 0.1875
- down_weight1: bfloat16 [2816, 1024], P(('grp', 'key')), may hold values from -0.109375 to 0.109375
- attn_gain2: bfloat16 [1024], P(('grp', 'key')), may hold values from 0.5 to 1.5
- second_query_weight: bfloat16 [1024, 1024], P(('grp', 'key')), may hold values from -0.1875 to 0.1875
- key_weight2: bfloat16 [1024, 1024], P(('grp', 'key')), may hold values from -0.1875 to 0.1875
- value_weight2: bfloat16 [1024, 1024], P(('grp', 'key')), may hold values from -0.1875 to 0.1875
- out_weight2: bfloat16 [1024, 1024], P(('grp', 'key')), may hold values from -0.75 to 0.75
- ffn_gain2: bfloat16 [1024], P(('grp', 'key')), may hold values from 0.5 to 1.5
- gate_weight2: bfloat16 [1024, 2816], P(('grp', 'key')), may hold values from -0.1875 to 0.1875
- up_weight2: bfloat16 [1024, 2816], P(('grp', 'key')), may hold values from -0.1875 to 0.1875
- down_weight2: bfloat16 [2816, 1024], P(('grp', 'key')), may hold values from -0.109375 to 0.109375
- cotangent: bfloat16 [8, 2048, 1024], P('grp', 'key'), may hold values from -6 to 6
Outputs:
- output: bfloat16 [8, 2048, 1024], P('grp', 'key')
- grad_tokens: float32 [8, 2048, 1024], P('grp', 'key')
- grad_attn_gain1: float32 [1024], P(('grp', 'key'))
- grad_query_weight1: float32 [1024, 1024], P(('grp', 'key'))
- grad_key_weight1: float32 [1024, 1024], P(('grp', 'key'))
- grad_value_weight1: float32 [1024, 1024], P(('grp', 'key'))
- grad_out_weight1: float32 [1024, 1024], P(('grp', 'key'))
- grad_ffn_gain1: float32 [1024], P(('grp', 'key'))
- grad_gate_weight1: float32 [1024, 2816], P(('grp', 'key'))
- grad_up_weight1: float32 [1024, 2816], P(('grp', 'key'))
- grad_down_weight1: float32 [2816, 1024], P(('grp', 'key'))
- grad_attn_gain2: float32 [1024], P(('grp', 'key'))
- grad_query_weight2: float32 [1024, 1024], P(('grp', 'key'))
- grad_key_weight2: float32 [1024, 1024], P(('grp', 'key'))
- grad_value_weight2: float32 [1024, 1024], P(('grp', 'key'))
- grad_out_weight2: float32 [1024, 1024], P(('grp', 'key'))
- grad_ffn_gain2: float32 [1024], P(('grp', 'key'))
- grad_gate_weight2: float32 [1024, 2816], P(('grp', 'key'))
- grad_up_weight2: float32 [1024, 2816], P(('grp', 'key'))
- grad_down_weight2: float32 [2816, 1024], P(('grp', 'key'))
The draws below stay inside these ranges and needn't reach their ends.
Inputs may be any that keep to these rules, and one draw needn't show every extreme that they name: `token_docs`: in every segment the numbers start at 0 and rise by 0 or 1 from one token to the next; among each group's 2 consecutive segments, one holds a single document, and every other segment holds exactly 8 documents.
All inputs are finite; a program needn't handle non-finite values. No bound on the sum of `memory_resets` on one device may be relied on, other than what follows from the above.
Results may differ from the reference program's by a relative error of at most 0.03.
Values may be sent and summed in bfloat16 or wider, within the bound.
A program may use at most 512 MiB of HBM per device.

```python
import jax
import jax.numpy as jnp
from jax import lax

D = 1024
HEADS = 8
HD = 128
FF = 2816
SEG = 2048
MEM = 2048
SEGS = 2
NSEG = 8


def draw_token_docs(key, part):
    key = jax.random.fold_in(key, 7)
    start_key, pick_key = jax.random.split(key)
    row_keys = jax.random.split(start_key, NSEG)

    def row_starts(row_key):
        places = jax.random.permutation(row_key, SEG - 1) + 1
        return jnp.zeros((SEG,), jnp.int32).at[places[:7]].set(1)
    starts = jax.vmap(row_starts)(row_keys)
    groups = NSEG // SEGS
    chosen = jnp.arange(groups, dtype=jnp.int32) * SEGS + jax.random.randint(pick_key, (groups,), 0, SEGS)
    single = jnp.any(jnp.arange(NSEG, dtype=jnp.int32)[:, None] == chosen[None, :], axis=1)
    starts = jnp.where(single[:, None], 0, starts)
    return jnp.cumsum(starts, axis=1).astype(jnp.int32)


def place_ends(drawn, rng, least, top_value):
    index_at = [jax.random.randint(jax.random.fold_in(rng, axis), (), 0, length) for axis, length in enumerate(drawn.shape)]
    longest = drawn.shape.index(max(drawn.shape))
    beside = index_at[:longest] + [(index_at[longest] + 1) % drawn.shape[longest]] + index_at[longest + 1:]
    return drawn.at[tuple(index_at)].set(least).at[tuple(beside)].set(top_value)


def with_spikes(array, key, source, target, parts, factor):
    owner, partner = [(jnp.arange(array.shape[axis_at]) // (array.shape[axis_at] // parts)).reshape([-1 if axis == axis_at else 1 for axis in range(array.ndim)]) for axis_at in (source, target)]
    chosen = jax.random.permutation(key, parts)[partner]
    strong = (owner == chosen) | (owner == (partner + parts // 2) % parts)
    return jnp.where(strong, factor * array, array)


def block_scale(stream_key, extent, shards, least, largest):
    def one(position, blocks):
        steps = jax.random.uniform(jax.random.fold_in(jax.random.fold_in(stream_key, 6), position), (blocks,), jnp.float32, least / len(shards), largest / len(shards))
        return jnp.repeat(jnp.exp(steps), extent[position] // blocks).reshape((-1,) + (1,) * (len(extent) - position - 1))

    gain = one(*shards[0])
    for cut in shards[1:]:
        gain = gain * one(*cut)
    return gain


def bell_draw(rng, extent, spread, limit, cuts=(), kind=jnp.bfloat16):
    factor_of = block_scale(rng, extent, cuts, -0.22, 0.18) if cuts else 1.0
    values = jax.random.normal(rng, extent, jnp.float32) * spread * factor_of
    return jnp.minimum(jnp.maximum(values, -limit), limit).astype(kind)


def bell_draw_with(key, shape, width, bound, cuts, heavy, kind=jnp.bfloat16):
    values = width * jax.random.normal(key, shape, jnp.float32)
    if cuts:
        values = values * block_scale(key, shape, cuts, -0.22, 0.18)
    return jnp.clip(with_spikes(values, jax.random.fold_in(key, 3), *heavy), -bound, bound).astype(kind)


def setup_inputs(seed: int = 0) -> dict:
    splits = jax.random.split(jax.random.key(seed), 26)
    tokens = bell_draw_with(splits[0], (NSEG, SEG, D), 1.0, 6.0, ((0, 4), (1, 8)), (1, 2, 8, 2.0))
    token_docs = draw_token_docs(jax.random.fold_in(splits[25], 71), 0)
    memory_docs = place_ends(jax.random.randint(splits[2], (NSEG, MEM), 0, 4), jax.random.fold_in(splits[2], 1), 0, 3).astype(jnp.int32)
    memory_resets = place_ends((jax.random.randint(splits[3], (NSEG,), 0, 4) < 1).astype(jnp.int32), jax.random.fold_in(splits[3], 1), 0, 1)
    memory_keys = bell_draw(splits[4], (NSEG, MEM, D), 1.0, 6.0, ((0, 4), (1, 8)))
    memory_values = bell_draw(splits[5], (NSEG, MEM, D), 1.0, 6.0, ((0, 4), (1, 8)))
    attn_gain1 = jnp.clip(1.0 + 0.1 * jax.random.normal(splits[6], (D,), jnp.float32), 0.5, 1.5).astype(jnp.bfloat16)
    query_weight1 = bell_draw(splits[7], (D, D), D ** -0.5, 0.1875, ((0, 32),))
    key_weight1 = bell_draw(splits[8], (D, D), D ** -0.5, 0.1875, ((0, 32),))
    value_weight1 = bell_draw(splits[9], (D, D), D ** -0.5, 0.1875, ((0, 32),))
    out_weight1 = bell_draw(splits[10], (D, D), (D // 16) ** -0.5, 0.75, ((0, 32),))
    ffn_gain1 = jnp.clip(1.0 + 0.1 * jax.random.normal(splits[11], (D,), jnp.float32), 0.5, 1.5).astype(jnp.bfloat16)
    gate_weight1 = bell_draw(splits[12], (D, FF), D ** -0.5, 0.1875, ((0, 32),))
    up_weight1 = bell_draw(splits[13], (D, FF), D ** -0.5, 0.1875, ((0, 32),))
    down_weight1 = bell_draw(splits[14], (FF, D), FF ** -0.5, 0.109375, ((0, 32),))
    attn_gain2 = jnp.clip(1.0 + 0.1 * jax.random.normal(splits[15], (D,), jnp.float32), 0.5, 1.5).astype(jnp.bfloat16)
    second_query_weight = bell_draw(splits[16], (D, D), D ** -0.5, 0.1875, ((0, 32),))
    key_weight2 = bell_draw(splits[17], (D, D), D ** -0.5, 0.1875, ((0, 32),))
    value_weight2 = bell_draw(splits[18], (D, D), D ** -0.5, 0.1875, ((0, 32),))
    out_weight2 = bell_draw(splits[19], (D, D), (D // 16) ** -0.5, 0.75, ((0, 32),))
    ffn_gain2 = jnp.clip(1.0 + 0.1 * jax.random.normal(splits[20], (D,), jnp.float32), 0.5, 1.5).astype(jnp.bfloat16)
    gate_weight2 = bell_draw(splits[21], (D, FF), D ** -0.5, 0.1875, ((0, 32),))
    up_weight2 = bell_draw(splits[22], (D, FF), D ** -0.5, 0.1875, ((0, 32),))
    down_weight2 = bell_draw(splits[23], (FF, D), FF ** -0.5, 0.109375, ((0, 32),))
    cotangent = bell_draw(splits[24], (NSEG, SEG, D), 1.0, 6.0, ((0, 4), (1, 8)))
    return {"tokens": tokens, "token_docs": token_docs, "memory_docs": memory_docs, "memory_resets": memory_resets, "memory_keys": memory_keys, "memory_values": memory_values, "attn_gain1": attn_gain1, "query_weight1": query_weight1, "key_weight1": key_weight1, "value_weight1": value_weight1, "out_weight1": out_weight1, "ffn_gain1": ffn_gain1, "gate_weight1": gate_weight1, "up_weight1": up_weight1, "down_weight1": down_weight1, "attn_gain2": attn_gain2, "second_query_weight": second_query_weight, "key_weight2": key_weight2, "value_weight2": value_weight2, "out_weight2": out_weight2, "ffn_gain2": ffn_gain2, "gate_weight2": gate_weight2, "up_weight2": up_weight2, "down_weight2": down_weight2, "cotangent": cotangent}


EPS = 1e-05
NEG = -1e+30

@jax.custom_vjp
def low(v):
    return lax.optimization_barrier(v.astype(jnp.bfloat16)).astype(jnp.float32)

@jax.custom_vjp
def low_back(v):
    return v

def low_keep(v):
    return (low(v), None)

def low_pass(kept, grad):
    return (grad,)

def back_keep(v):
    return (v, None)

def back_low(kept, grad):
    return (low(grad),)
low.defvjp(low_keep, low_pass)
low_back.defvjp(back_keep, back_low)

def matmul(input_operand, weight_matrix):
    return jnp.dot(input_operand, weight_matrix, precision=lax.Precision.HIGHEST)

def rms_norm(values, gain_vec):
    return values * lax.rsqrt(lax.optimization_barrier(jnp.mean(values * values, axis=-1, keepdims=True)) + EPS) * gain_vec

def segment_attention(query, key_rows, value_rows, doc_ids, memory):
    row_count = query.shape[0]
    places = jnp.arange(row_count, dtype=jnp.int32)
    allowed = (places[None, :] <= places[:, None]) & (doc_ids[None, :] == doc_ids[:, None])
    if memory is not None:
        memory_key, memory_value, memory_doc, reset_flag = memory
        key_rows = jnp.concatenate((key_rows, memory_key), axis=0)
        value_rows = jnp.concatenate((value_rows, memory_value), axis=0)
        memory_seen = (memory_doc[None, :] == doc_ids[:, None]) & (reset_flag == 0)
        allowed = jnp.concatenate((allowed, memory_seen), axis=1)
    query_heads = query.reshape(row_count, HEADS, HD)
    key_heads = key_rows.reshape(key_rows.shape[0], HEADS, HD)
    value_heads = value_rows.reshape(value_rows.shape[0], HEADS, HD)
    raw_scores = jnp.einsum('qhd,khd->hqk', query_heads, key_heads, precision=lax.Precision.HIGHEST) * HD ** (-0.5)
    scores = jnp.where(allowed[None], low_back(raw_scores), NEG)
    row_top = lax.optimization_barrier(jnp.max(scores, axis=2, keepdims=True))
    exp_scores = jnp.where(allowed[None], jnp.exp(scores - row_top), 0.0)
    probability = exp_scores / lax.optimization_barrier(jnp.sum(exp_scores, axis=2, keepdims=True))
    weighted = jnp.einsum('hqk,khd->qhd', low(probability), value_heads, precision=lax.Precision.HIGHEST)
    return weighted.reshape(row_count, HEADS * HD)

def plain_segment(pieces):
    return segment_attention(pieces[0], pieces[1], pieces[2], pieces[3], None)

def memory_segment(pieces):
    return segment_attention(pieces[0], pieces[1], pieces[2], pieces[3], pieces[4:])

def layer(stream, params, doc_ids, memory):
    gain_a, query_w, key_w, value_w, out_w, gain_b, gate_w, up_w, down_w = params
    normed = low(rms_norm(stream, gain_a))
    query = low(low_back(matmul(normed, query_w)))
    key_rows = low(low_back(matmul(normed, key_w)))
    value_rows = low(low_back(matmul(normed, value_w)))
    if memory is None:
        attended = lax.map(jax.checkpoint(plain_segment), (query, key_rows, value_rows, doc_ids))
    else:
        attended = lax.map(jax.checkpoint(memory_segment), (query, key_rows, value_rows, doc_ids) + memory)
    attended = low(low_back(attended))
    mixed_stream = stream + low_back(matmul(attended, out_w))
    normed_ff = low(rms_norm(mixed_stream, gain_b))
    gate_value = low_back(matmul(normed_ff, gate_w))
    up_value = low_back(matmul(normed_ff, up_w))
    activated = low(gate_value * jax.nn.sigmoid(gate_value) * up_value)
    return mixed_stream + low_back(matmul(activated, down_w))

def reference(tokens, token_docs, memory_docs, memory_resets, memory_keys, memory_values, attn_gain1, query_weight1, key_weight1, value_weight1, out_weight1, ffn_gain1, gate_weight1, up_weight1, down_weight1, attn_gain2, second_query_weight, key_weight2, value_weight2, out_weight2, ffn_gain2, gate_weight2, up_weight2, down_weight2, cotangent):
    params = tuple((element.astype(jnp.float32) for element in (attn_gain1, query_weight1, key_weight1, value_weight1, out_weight1, ffn_gain1, gate_weight1, up_weight1, down_weight1, attn_gain2, second_query_weight, key_weight2, value_weight2, out_weight2, ffn_gain2, gate_weight2, up_weight2, down_weight2)))
    memory = (memory_keys.astype(jnp.float32), memory_values.astype(jnp.float32), memory_docs, memory_resets)

    def forward(stream, weights):
        middle = layer(stream, weights[:9], token_docs, None)
        return layer(middle, weights[9:], token_docs, memory)
    result, pullback = jax.vjp(forward, tokens.astype(jnp.float32), params)
    grad_tokens, grads = pullback(cotangent.astype(jnp.float32))
    return (result.astype(jnp.bfloat16), grad_tokens, grads[0], grads[1], grads[2], grads[3], grads[4], grads[5], grads[6], grads[7], grads[8], grads[9], grads[10], grads[11], grads[12], grads[13], grads[14], grads[15], grads[16], grads[17])
```

```python
import functools

import jax
import jax.numpy as jnp
from jax import lax
from jax.experimental import pallas as pl
from jax.experimental.pallas import tpu as pltpu
from jax.sharding import PartitionSpec as P

HEADS = 8


EPS = 1e-05
NEG = -1e30


def norm_forward(values, gain_vec):
    inverse = lax.rsqrt(jnp.mean(values * values, axis=-1, keepdims=True) + EPS)
    return (values * inverse * gain_vec, inverse)


def norm_backward(values, gain_vec, inverse, grad_normed):
    grad_gain = jnp.sum(grad_normed * values * inverse, axis=(0, 1))
    scaled = grad_normed * gain_vec
    grad_values = inverse * scaled - values * inverse**3 * jnp.mean(
        scaled * values, axis=-1, keepdims=True
    )
    return (grad_values, grad_gain)


def project(input_operand, weight_matrix):
    return jnp.dot(input_operand, weight_matrix, preferred_element_type=jnp.float32)


def project_back(gradient_row_block, weight_matrix):
    return jnp.einsum(
        "tzu,ku->tzk", gradient_row_block, weight_matrix, preferred_element_type=jnp.float32
    )


def outer_sum(input_arrays, gradient_reduced_precision):
    return jnp.einsum(
        "zhp,zhv->pv", input_arrays, gradient_reduced_precision, preferred_element_type=jnp.float32
    )


def split_heads(rows):
    return rows.reshape(rows.shape[0], rows.shape[1], HEADS, rows.shape[2] // HEADS)


def fetch_weights(shards):
    return (
        lax.all_gather(shards[0], ("grp", "key"), axis=0, tiled=True),
        lax.all_gather(shards[1], ("grp", "key"), axis=0, tiled=True),
        lax.all_gather(shards[2], ("grp", "key"), axis=0, tiled=True),
        lax.all_gather(shards[3], ("grp", "key"), axis=0, tiled=True),
        lax.all_gather(shards[4], ("grp", "key"), axis=0, tiled=True),
        lax.all_gather(shards[5], ("grp", "key"), axis=0, tiled=True),
        lax.all_gather(shards[6], ("grp", "key"), axis=0, tiled=True),
        lax.all_gather(shards[7], ("grp", "key"), axis=0, tiled=True),
        lax.all_gather(shards[8], ("grp", "key"), axis=0, tiled=True),
    )


def refetch_weights(shards):
    return (
        lax.all_gather(shards[0], ("grp", "key"), axis=0, tiled=True),
        lax.all_gather(shards[1], ("grp", "key"), axis=0, tiled=True),
        lax.all_gather(shards[2], ("grp", "key"), axis=0, tiled=True),
        lax.all_gather(shards[3], ("grp", "key"), axis=0, tiled=True),
        lax.all_gather(shards[4], ("grp", "key"), axis=0, tiled=True),
        lax.all_gather(shards[5], ("grp", "key"), axis=0, tiled=True),
        lax.all_gather(shards[6], ("grp", "key"), axis=0, tiled=True),
        lax.all_gather(shards[7], ("grp", "key"), axis=0, tiled=True),
        lax.all_gather(shards[8], ("grp", "key"), axis=0, tiled=True),
    )


def reduce_gradient_sums(terms):
    return (
        lax.psum_scatter(terms[0], ("grp", "key"), scatter_dimension=0, tiled=True),
        lax.psum_scatter(terms[1], ("grp", "key"), scatter_dimension=0, tiled=True),
        lax.psum_scatter(terms[2], ("grp", "key"), scatter_dimension=0, tiled=True),
        lax.psum_scatter(terms[3], ("grp", "key"), scatter_dimension=0, tiled=True),
        lax.psum_scatter(terms[4], ("grp", "key"), scatter_dimension=0, tiled=True),
        lax.psum_scatter(terms[5], ("grp", "key"), scatter_dimension=0, tiled=True),
        lax.psum_scatter(terms[6], ("grp", "key"), scatter_dimension=0, tiled=True),
        lax.psum_scatter(terms[7], ("grp", "key"), scatter_dimension=0, tiled=True),
        lax.psum_scatter(terms[8], ("grp", "key"), scatter_dimension=0, tiled=True),
    )


def head_scores(query_all, key_block, allowed):
    head_size = query_all.shape[2] // HEADS
    raw_scores = jnp.einsum(
        "sqhd,skhd->shqk",
        split_heads(query_all),
        split_heads(key_block),
        preferred_element_type=jnp.float32,
    ) * head_size ** (-0.5)
    return jnp.where(allowed[:, None], raw_scores, NEG)


def attend_forward(query_all, key_block, value_block, allowed):
    scores = head_scores(query_all, key_block, allowed)
    row_top = lax.pmax(jnp.max(scores, axis=3).astype(jnp.bfloat16), "key").astype(jnp.float32)
    exp_scores = jnp.where(allowed[:, None], jnp.exp(scores - row_top[..., None]), 0.0)
    row_total = lax.psum(jnp.sum(exp_scores, axis=3).astype(jnp.bfloat16), "key").astype(
        jnp.float32
    )
    probability = exp_scores / row_total[..., None]
    partial_value = jnp.einsum(
        "shqk,skhd->sqhd",
        probability.astype(jnp.bfloat16),
        split_heads(value_block),
        preferred_element_type=jnp.float32,
    )
    partial_value = partial_value.reshape(query_all.shape)
    attended = lax.psum_scatter(
        partial_value.astype(jnp.bfloat16), "key", scatter_dimension=1, tiled=True
    ).astype(jnp.float32)
    return (attended, row_top, row_total)


def layer_forward(stream, full_weights, allowed, extra_keys, extra_values):
    gain_a, query_w, key_w, value_w, out_w, gain_b, gate_w, up_w, down_w = full_weights
    normed, first_inverse_factor = norm_forward(stream, gain_a.astype(jnp.float32))
    normed_low = normed.astype(jnp.bfloat16)
    query_low = project(normed_low, query_w).astype(jnp.bfloat16)
    key_low = project(normed_low, key_w).astype(jnp.bfloat16)
    value_low = project(normed_low, value_w).astype(jnp.bfloat16)
    query_all = lax.all_gather(query_low, "key", axis=1, tiled=True)
    if extra_keys is None:
        key_block = key_low
        value_block = value_low
    else:
        key_block = jnp.concatenate((key_low, extra_keys), axis=1)
        value_block = jnp.concatenate((value_low, extra_values), axis=1)
    attended, row_top, row_total = attend_forward(query_all, key_block, value_block, allowed)
    attended_low = attended.astype(jnp.bfloat16)
    mixed_stream = stream + project(attended_low, out_w)
    normed_ff, inverse_b = norm_forward(mixed_stream, gain_b.astype(jnp.float32))
    normed_ff_low = normed_ff.astype(jnp.bfloat16)
    gate_value = project(normed_ff_low, gate_w)
    up_value = project(normed_ff_low, up_w)
    activated_low = (gate_value * jax.nn.sigmoid(gate_value) * up_value).astype(jnp.bfloat16)
    result = mixed_stream + project(activated_low, down_w)
    kept_state = (
        stream,
        first_inverse_factor,
        normed_low,
        key_block,
        value_block,
        query_all,
        row_top,
        row_total,
        attended_low,
        mixed_stream,
        inverse_b,
        normed_ff_low,
        gate_value,
        up_value,
        activated_low,
    )
    return (result, kept_state)


def layer_backward(grad_result, full_weights, kept_state, allowed):
    gain_a, query_w, key_w, value_w, out_w, gain_b, gate_w, up_w, down_w = full_weights
    (
        stream,
        first_inverse_factor,
        normed_low,
        key_block,
        value_block,
        query_all,
        row_top,
        row_total,
        attended_low,
        mixed_stream,
        inverse_b,
        normed_ff_low,
        gate_value,
        up_value,
        activated_low,
    ) = kept_state
    own_rows = stream.shape[1]
    branch_low = grad_result.astype(jnp.bfloat16)
    grad_down = outer_sum(activated_low, branch_low)
    grad_act = project_back(branch_low, down_w)
    sigmoid_gate = jax.nn.sigmoid(gate_value)
    grad_gate = (
        grad_act * up_value * sigmoid_gate * (1.0 + gate_value * (1.0 - sigmoid_gate))
    ).astype(jnp.bfloat16)
    grad_up_low = (grad_act * gate_value * sigmoid_gate).astype(jnp.bfloat16)
    grad_gate_w = outer_sum(normed_ff_low, grad_gate)
    grad_up_w = outer_sum(normed_ff_low, grad_up_low)
    grad_normed_ff = project_back(grad_gate, gate_w) + project_back(grad_up_low, up_w)
    grad_mixed_norm, grad_gain_b = norm_backward(
        mixed_stream, gain_b.astype(jnp.float32), inverse_b, grad_normed_ff
    )
    grad_mixed = grad_result + grad_mixed_norm
    attn_low = grad_mixed.astype(jnp.bfloat16)
    grad_out_w = outer_sum(attended_low, attn_low)
    grad_attended = project_back(attn_low, out_w).astype(jnp.bfloat16)
    grad_all = lax.all_gather(grad_attended, "key", axis=1, tiled=True)
    scores = head_scores(query_all, key_block, allowed)
    probability = (
        jnp.where(allowed[:, None], jnp.exp(scores - row_top[..., None]), 0.0)
        / row_total[..., None]
    )
    grad_heads = split_heads(grad_all)
    grad_probs = jnp.einsum(
        "sqhd,skhd->shqk", grad_heads, split_heads(value_block), preferred_element_type=jnp.float32
    )
    row_delta = lax.psum(
        jnp.sum(probability * grad_probs, axis=3).astype(jnp.bfloat16), "key"
    ).astype(jnp.float32)
    grad_scores = (probability * (grad_probs - row_delta[..., None])).astype(jnp.bfloat16)
    score_scale = (query_all.shape[2] // HEADS) ** (-0.5)
    query_part = (
        jnp.einsum(
            "shqk,skhd->sqhd",
            grad_scores,
            split_heads(key_block),
            preferred_element_type=jnp.float32,
        ).reshape(query_all.shape)
        * score_scale
    )
    grad_query = lax.psum_scatter(
        query_part.astype(jnp.bfloat16), "key", scatter_dimension=1, tiled=True
    )
    own_scores = grad_scores[..., :own_rows]
    grad_key = (
        jnp.einsum(
            "shqk,sqhd->skhd",
            own_scores,
            split_heads(query_all),
            preferred_element_type=jnp.float32,
        ).reshape(stream.shape)
        * score_scale
    ).astype(jnp.bfloat16)
    own_probs = probability.astype(jnp.bfloat16)[..., :own_rows]
    grad_value = (
        jnp.einsum("shqk,sqhd->skhd", own_probs, grad_heads, preferred_element_type=jnp.float32)
        .reshape(stream.shape)
        .astype(jnp.bfloat16)
    )
    grad_query_w = outer_sum(normed_low, grad_query)
    grad_key_w = outer_sum(normed_low, grad_key)
    grad_value_w = outer_sum(normed_low, grad_value)
    grad_normed = (
        project_back(grad_query, query_w)
        + project_back(grad_key, key_w)
        + project_back(grad_value, value_w)
    )
    grad_stream_norm, grad_gain_a = norm_backward(
        stream, gain_a.astype(jnp.float32), first_inverse_factor, grad_normed
    )
    grad_stream = grad_mixed + grad_stream_norm
    terms = (
        grad_gain_a,
        grad_query_w,
        grad_key_w,
        grad_value_w,
        grad_out_w,
        grad_gain_b,
        grad_gate_w,
        grad_up_w,
        grad_down,
    )
    return (grad_stream, terms)


def gathered_local(
    tokens,
    token_docs,
    memory_docs,
    memory_resets,
    memory_keys,
    memory_values,
    attn_gain1,
    query_weight1,
    key_weight1,
    value_weight1,
    out_weight1,
    ffn_gain1,
    gate_weight1,
    up_weight1,
    down_weight1,
    attn_gain2,
    second_query_weight,
    key_weight2,
    value_weight2,
    out_weight2,
    ffn_gain2,
    gate_weight2,
    up_weight2,
    down_weight2,
    cotangent,
):
    first_shards = (
        attn_gain1,
        query_weight1,
        key_weight1,
        value_weight1,
        out_weight1,
        ffn_gain1,
        gate_weight1,
        up_weight1,
        down_weight1,
    )
    second_shards = (
        attn_gain2,
        second_query_weight,
        key_weight2,
        value_weight2,
        out_weight2,
        ffn_gain2,
        gate_weight2,
        up_weight2,
        down_weight2,
    )
    docs_all = lax.all_gather(token_docs, "key", axis=1, tiled=True)
    own_rows = tokens.shape[1]
    query_place = jnp.arange(docs_all.shape[1], dtype=jnp.int32)
    key_place = lax.axis_index("key") * own_rows + jnp.arange(own_rows, dtype=jnp.int32)
    local_allowed = (key_place[None, None, :] <= query_place[None, :, None]) & (
        token_docs[:, None, :] == docs_all[:, :, None]
    )
    memory_allowed = (memory_docs[:, None, :] == docs_all[:, :, None]) & (
        memory_resets[:, None, None] == 0
    )
    both_allowed = jnp.concatenate((local_allowed, memory_allowed), axis=2)
    stream = tokens.astype(jnp.float32)
    first_full = fetch_weights(first_shards)
    middle, first_state = layer_forward(stream, first_full, local_allowed, None, None)
    second_full = fetch_weights(second_shards)
    result, second_state = layer_forward(
        middle, second_full, both_allowed, memory_keys, memory_values
    )
    second_full = refetch_weights(second_shards)
    grad_middle, second_terms = layer_backward(
        cotangent.astype(jnp.float32), second_full, second_state, both_allowed
    )
    second_grads = reduce_gradient_sums(second_terms)
    first_full = refetch_weights(first_shards)
    grad_stream, first_terms = layer_backward(grad_middle, first_full, first_state, local_allowed)
    first_grads = reduce_gradient_sums(first_terms)
    return (
        result.astype(jnp.bfloat16),
        grad_stream,
        first_grads[0],
        first_grads[1],
        first_grads[2],
        first_grads[3],
        first_grads[4],
        first_grads[5],
        first_grads[6],
        first_grads[7],
        first_grads[8],
        second_grads[0],
        second_grads[1],
        second_grads[2],
        second_grads[3],
        second_grads[4],
        second_grads[5],
        second_grads[6],
        second_grads[7],
        second_grads[8],
    )


MESH = pl.DeviceIdType.MESH
ANY = pl.BlockSpec(memory_space=pl.ANY)
VMEM = pl.BlockSpec(memory_space=pltpu.VMEM)
LOG2E = 1.4426950408889634
BLOCK = 256
LOCAL = 4
HEAD = 128
PAIR = 2 * HEAD
BF = jnp.bfloat16
F32 = jnp.float32


SEND = pltpu.SemaphoreType.DMA


def flip(value, change):
    return lax.rem(value + change, 2)


class Place:
    def __init__(self):
        self.grp = lax.axis_index("grp")
        self.key = lax.axis_index("key")
        self.y, self.x = self.grp // 2, lax.rem(self.grp, 2)
        self.z, self.core = self.key // 2, lax.rem(self.key, 2)
        self.rank = lax.rem(self.key, LOCAL)
        self.seg = self.key // LOCAL

    def chip(self, da, db, dz, core):
        dx = da * (1 - core) + db * core
        dy = da * core + db * (1 - core)
        z = flip(self.z // 2, dz // 2) * 2 + flip(lax.rem(self.z, 2), dz % 2)
        return flip(self.y, dy) * 2 + flip(self.x, dx), z

    def device(self, da, db, dz):
        grp, z = self.chip(da, db, dz, self.core)
        return grp, z * 2 + self.core

    def sibling(self):
        return self.grp, self.z * 2 + 1 - self.core


def remote(src, dst, send, recv, target):
    return pltpu.make_async_remote_copy(
        src_ref=src, dst_ref=dst, send_sem=send, recv_sem=recv,
        device_id=target, device_id_type=MESH,
    )


def local(src, dst, sem):
    return pltpu.make_async_copy(src, dst, sem)


def span(index, size):
    return pl.ds(pl.multiple_of(index * size, size), size)


class RowBlocks:
    def __init__(self, rows, width):
        self.shape = (rows, width)

    def whole(self, chips):
        return (chips * 2 * self.shape[0], self.shape[1])

    def at(self, ref, chip, core):
        return ref.at[span((chip[0] * LOCAL + chip[1]) * 2 + core, self.shape[0]), :]


class PairBlocks(RowBlocks):
    def whole(self, chips):
        return (chips * self.shape[0], 2 * self.shape[1])

    def at(self, ref, chip, core):
        rows, width = self.shape
        return ref.at[span(chip[0] * LOCAL + chip[1], rows), span(core, width)]


class ColumnBlocks(RowBlocks):
    def __init__(self, rows, width, part):
        self.shape = (rows, width)
        self.part = part

    def at(self, ref, chip, core):
        rows, width = self.shape
        return ref.at[
            span((chip[0] * LOCAL + chip[1]) * 2 + core, rows), pl.ds(self.part * width, width)
        ]


class Swap:
    def __init__(self, arrays, to_heads):
        self.arrays = arrays
        self.to_heads = to_heads
        if to_heads:
            rows, width = arrays[0].shape
            self.parts = width // (LOCAL * PAIR)
            self.outs = [jax.ShapeDtypeStruct((rows * LOCAL, PAIR), BF)] * self.parts
        else:
            rows = arrays[0].shape[0] // LOCAL
            self.parts = len(arrays)
            self.outs = [jax.ShapeDtypeStruct((rows, self.parts * LOCAL * PAIR), BF)]
        self.rows = rows
        self.scratch = [SEND((self.parts, LOCAL)), SEND((self.parts, LOCAL)), SEND((self.parts,))]
        self.out_specs = [ANY] * len(self.outs)

    def run(self, at, ins, outs, scratch):
        send, recv, here = scratch

        def copy(part, k):
            target = lax.rem(at.rank + k, LOCAL)
            if self.to_heads:
                src = ins[0].at[:, span(part * LOCAL + target, PAIR)]
                dst = outs[part].at[span(at.rank, self.rows), :]
            else:
                src = ins[part].at[span(target, self.rows), :]
                dst = outs[0].at[:, span(part * LOCAL + at.rank, PAIR)]
            if k == 0:
                return local(src, dst, here.at[part])
            device = (at.grp, at.seg * LOCAL + target)
            return remote(src, dst, send.at[part, k], recv.at[part, k], device)

        every = [(part, k) for part in range(self.parts) for k in (2, 3, 1, 0)]
        for part, k in every:
            copy(part, k).start()
        yield
        yield "last"
        for part, k in every:
            copy(part, k).wait()


class Rows:
    def __init__(self, array):
        segs, rows, width = array.shape
        self.arrays = [array]
        self.rows = rows
        self.outs = [jax.ShapeDtypeStruct((segs * rows, width), array.dtype)]
        self.out_specs = [ANY]
        self.scratch = [SEND((2,)), SEND((2,)), SEND(())]

    def run(self, at, ins, outs, scratch):
        (src,), (dst,) = ins, outs
        send, recv, here = scratch
        chunk = lax.rem(at.key, 2)

        def part(index):
            return dst.at[span(index, self.rows), :]

        def out(seg):
            target = seg * LOCAL + at.key // 2
            return target, remote(
                src.at[seg], part(chunk), send.at[seg], recv.at[chunk], (at.grp, target)
            )

        for seg in range(2):
            target, copy = out(seg)
            pl.when(target != at.key)(copy.start)
            pl.when(target == at.key)(local(src.at[seg], part(chunk), here).start)
        yield
        yield "last"
        for seg in range(2):
            target, copy = out(seg)
            pl.when(target != at.key)(copy.wait_send)
        for index in range(2):
            owner = 2 * at.rank + index
            copy = remote(src.at[0], part(index), send.at[0], recv.at[index], (at.grp, owner))
            pl.when(owner != at.key)(copy.wait_recv)
            pl.when(owner == at.key)(local(src.at[0], part(index), here).wait)


class Chunks:
    def __init__(self, array):
        rows, width = array.shape
        self.arrays = [array]
        self.rows = rows // 2
        self.outs = [jax.ShapeDtypeStruct((2, rows // 2, width), array.dtype)]
        self.out_specs = [ANY]
        self.scratch = [SEND((2,)), SEND((2,)), SEND(())]

    def run(self, at, ins, outs, scratch):
        (src,), (dst,) = ins, outs
        send, recv, here = scratch

        def part(index):
            return src.at[pl.ds(index * self.rows, self.rows), :]

        def out(index):
            target = 2 * at.rank + index
            return target, remote(
                part(index), dst.at[at.seg], send.at[index], recv.at[at.seg], (at.grp, target)
            )

        for index in range(2):
            target, copy = out(index)
            pl.when(target != at.key)(copy.start)
            pl.when(target == at.key)(local(part(index), dst.at[at.seg], here).start)
        yield
        yield "last"
        for index in range(2):
            target, copy = out(index)
            pl.when(target != at.key)(copy.wait_send)
        for seg in range(2):
            owner = seg * LOCAL + at.key // 2
            copy = remote(part(0), dst.at[seg], send.at[0], recv.at[seg], (at.grp, owner))
            pl.when(owner != at.key)(copy.wait_recv)
            pl.when(owner == at.key)(local(part(0), dst.at[seg], here).wait)


class Memory:
    def __init__(self, array):
        self.arrays = [array]
        self.rows = array.shape[1]
        self.outs = [jax.ShapeDtypeStruct((2 * LOCAL * self.rows, PAIR), BF)]
        self.out_specs = [ANY]
        self.scratch = [SEND((2 * LOCAL,)), SEND((2 * LOCAL,)), SEND(())]

    def run(self, at, ins, outs, scratch):
        send, recv, here = scratch

        def copy(k):
            target = lax.rem(at.key + k, 2 * LOCAL)
            src = ins[0].at[target // LOCAL, :, span(lax.rem(target, LOCAL), PAIR)]
            dst = outs[0].at[span(at.key, self.rows), :]
            if k == 0:
                return local(src, dst, here)
            return remote(src, dst, send.at[k], recv.at[k], (at.grp, target))

        for k in range(2 * LOCAL):
            copy(k).start()
        yield
        yield "last"
        for k in range(2 * LOCAL):
            copy(k).wait()


class Docs:
    def __init__(self, array):
        rows, self.width = array.shape
        self.arrays = [array]
        self.outs = [jax.ShapeDtypeStruct((rows, 2 * LOCAL * self.width), array.dtype)]
        self.out_specs = [ANY]
        self.scratch = [SEND((2 * LOCAL,)), SEND((2 * LOCAL,)), SEND(())]

    def run(self, at, ins, outs, scratch):
        send, recv, here = scratch

        def copy(k):
            target = lax.rem(at.key + k, 2 * LOCAL)
            dst = outs[0].at[:, span(at.key, self.width)]
            if k == 0:
                return local(ins[0], dst, here)
            return remote(ins[0], dst, send.at[k], recv.at[k], (at.grp, target))

        for k in range(2 * LOCAL):
            copy(k).start()
        yield
        yield "last"
        for k in range(2 * LOCAL):
            copy(k).wait()


class Sibling:
    def __init__(self, array):
        self.arrays = [array]
        self.outs = [jax.ShapeDtypeStruct(array.shape, array.dtype)]
        self.out_specs = [ANY]
        self.scratch = [SEND(()), SEND(())]

    def run(self, at, ins, outs, scratch):
        copy = remote(ins[0], outs[0], scratch[0], scratch[1], at.sibling())
        copy.start()
        yield
        yield "last"
        copy.wait()


STEPS = [(da, db, dz) for db in range(2) for da in range(2) for dz in range(4)]


class Gather:
    def __init__(self, shard, blocks):
        self.arrays = [shard]
        self.blocks = blocks
        self.outs = [jax.ShapeDtypeStruct(blocks.whole(4 * LOCAL), shard.dtype)]
        self.out_specs = [ANY]
        self.scratch = [SEND((32,)), SEND((32,)), SEND(())]

    def run(self, at, ins, outs, scratch):
        (shard,), (whole,) = ins, outs
        send, recv, here = scratch
        core = at.core

        def spot(step, of=core):
            return self.blocks.at(whole, at.chip(*step, of), of)

        def copy(step, slot, target):
            src = shard if step == (0, 0, 0) else spot(step)
            return remote(src, spot(step), send.at[slot], recv.at[slot], target)

        def along_z(dz):
            return copy((0, 0, 0), dz, at.device(0, 0, dz))

        def first(dz):
            return copy((0, 0, dz), 4 + dz, at.device(1, 0, 0))

        def second(da, dz):
            return copy((da, 0, dz), 8 + 4 * da + dz, at.device(0, 1, 0))

        def across(step):
            return copy(step, 16 + STEPS.index(step), at.sibling())

        def arrived(step, slot):
            dst = spot(step)
            remote(dst, dst, send.at[slot], recv.at[slot], at.sibling()).wait_recv()

        mine = local(shard, spot((0, 0, 0)), here)
        mine.start()
        for dz in (3, 2, 1):
            along_z(dz).start()
        first(0).start()
        second(0, 0).start()
        across((0, 0, 0)).start()
        yield
        for dz in (1, 2, 3):
            arrived((0, 0, dz), dz)
            first(dz).start()
            second(0, dz).start()
            across((0, 0, dz)).start()
        yield
        for dz in range(4):
            arrived((1, 0, dz), 4 + dz)
            second(1, dz).start()
            across((1, 0, dz)).start()
        yield
        for da in range(2):
            for dz in range(4):
                arrived((da, 1, dz), 8 + 4 * da + dz)
                across((da, 1, dz)).start()
        yield "last"
        for step in STEPS:
            dst = spot(step, 1 - core)
            slot = 16 + STEPS.index(step)
            remote(dst, dst, send.at[slot], recv.at[slot], at.sibling()).wait_recv()
        for dz in (1, 2, 3):
            along_z(dz).wait_send()
        for dz in range(4):
            first(dz).wait_send()
            for da in range(2):
                second(da, dz).wait_send()
        for step in STEPS:
            across(step).wait_send()
        mine.wait()


def add_into(dst, parts, tile):
    rows, width = dst.shape

    @pl.loop(0, width // tile)
    def _(t):
        cut = pl.ds(pl.multiple_of(t * tile, tile), tile)
        total = parts[0][:, cut].astype(F32)
        for part in parts[1:]:
            total += part[:, cut].astype(F32)
        dst[:, cut] = total.astype(dst.dtype)


class Scatter:
    def __init__(self, whole, blocks, lag=0):
        self.arrays = [whole]
        self.blocks = blocks
        self.lag = lag
        shape = blocks.shape
        self.pair = isinstance(blocks, PairBlocks)
        self.tile = 256 if shape[1] % 256 == 0 else 128
        out = (shape[0] // 2, 2 * shape[1]) if self.pair else shape
        self.outs = [jax.ShapeDtypeStruct(out, F32)]
        self.out_specs = [VMEM]
        dma = SEND
        self.scratch = [
            pltpu.VMEM((16,) + shape, BF),
            pltpu.VMEM((16,) + shape, BF),
            pltpu.VMEM((8,) + shape, BF),
            pltpu.VMEM((4,) + shape, BF),
            pltpu.VMEM((4,) + shape, BF),
            dma((16,)),
            dma((32,)),
            dma((32,)),
        ]
        if self.pair:
            self.scratch += [pltpu.VMEM(shape, F32), dma((2,))]

    def run(self, at, ins, outs, scratch):
        (whole,), (out,) = ins, outs
        own, near, from_b, from_a, from_z, load, send, recv = scratch[:8]
        core = at.core
        order = list(reversed(STEPS))

        def fetch(slot):
            src = self.blocks.at(whole, at.chip(*STEPS[slot], core), core)
            return local(src, own.at[slot], load.at[slot])

        def across(slot):
            src = self.blocks.at(whole, at.chip(*STEPS[slot], 1 - core), 1 - core)
            return remote(src, near.at[slot], send.at[slot], recv.at[slot], at.sibling())

        def second(da, dz):
            slot = STEPS.index((da, 1, dz))
            spot = 4 * da + dz
            return remote(
                own.at[slot], from_b.at[spot], send.at[16 + spot], recv.at[16 + spot],
                at.device(0, 1, 0),
            )

        def first(dz):
            slot = STEPS.index((1, 0, dz))
            return remote(
                own.at[slot], from_a.at[dz], send.at[24 + dz], recv.at[24 + dz], at.device(1, 0, 0)
            )

        def along_z(dz):
            slot = STEPS.index((0, 0, dz))
            return remote(
                own.at[slot], from_z.at[dz], send.at[28 + dz], recv.at[28 + dz], at.device(0, 0, dz)
            )

        for step in order:
            slot = STEPS.index(step)
            across(slot).start()
            fetch(slot).start()
        for _ in range(1 + self.lag):
            yield

        def settle(step, more, dst=None):
            slot = STEPS.index(step)
            fetch(slot).wait()
            across(slot).wait_recv()
            parts = [own.at[slot], near.at[slot]] + more
            add_into(own.at[slot] if dst is None else dst, parts, self.tile)

        for da in (1, 0):
            for dz in (3, 2, 1, 0):
                settle((da, 1, dz), [])
                second(da, dz).start()
        yield
        for dz in (3, 2, 1, 0):
            second(1, dz).wait_recv()
            settle((1, 0, dz), [from_b.at[4 + dz]])
            first(dz).start()
        yield
        for dz in (3, 2, 1):
            second(0, dz).wait_recv()
            first(dz).wait_recv()
            settle((0, 0, dz), [from_b.at[dz], from_a.at[dz]])
            along_z(dz).start()
        yield
        second(0, 0).wait_recv()
        first(0).wait_recv()
        for dz in (1, 2, 3):
            along_z(dz).wait_recv()
        total = scratch[8] if self.pair else out
        more = [from_b.at[0], from_a.at[0]] + [from_z.at[dz] for dz in (1, 2, 3)]
        settle((0, 0, 0), more, total)
        if self.pair:
            rows, width = self.blocks.shape
            half = rows // 2
            columns = span(core, width)
            swap = remote(
                total.at[span(1 - core, half), :], out.at[:, columns],
                scratch[9].at[0], scratch[9].at[1], at.sibling(),
            )
            swap.start()
            out[:, columns] = total[span(core, half), :]
        yield "last"
        if self.pair:
            swap.wait()
        for slot in range(16):
            across(slot).wait_send()
        for dz in range(4):
            for da in range(2):
                second(da, dz).wait_send()
            first(dz).wait_send()
            if dz:
                along_z(dz).wait_send()


def exchange(name, collective, parts, vmem=4):
    sizes = [(len(p.arrays), len(p.outs), len(p.scratch)) for p in parts]
    n_in = sum(size[0] for size in sizes)
    n_out = sum(size[1] for size in sizes)

    def kernel(*refs):
        at = Place()
        barrier = pltpu.get_barrier_semaphore()
        near = [(at.grp, lax.rem(at.key + k, 2 * LOCAL)) for k in range(1, 2 * LOCAL)]
        near += [at.device(1, 0, 0), at.device(0, 1, 0)]
        for device in near:
            pl.semaphore_signal(barrier, inc=1, device_id=device, device_id_type=MESH)
        pl.semaphore_wait(barrier, len(near))
        ins, outs, scratch = refs[:n_in], refs[n_in : n_in + n_out], refs[n_in + n_out :]
        live = []
        sums = any(isinstance(part, Scatter) for part in parts)
        for part, (i, o, s) in zip(parts, sizes):
            live.append(part.run(at, ins[:i], outs[:o], scratch[:s]))
            ins, outs, scratch = ins[i:], outs[o:], scratch[s:]
        for stage in live:
            next(stage)
        ending = []
        while live:
            for stage in list(reversed(live) if sums else live):
                if next(stage) == "last":
                    live.remove(stage)
                    ending.append(stage)
        for stage in ending:
            for _ in stage:
                pass

    outs = pl.pallas_call(
        kernel,
        name=name,
        out_shape=[o for p in parts for o in p.outs],
        in_specs=[ANY] * n_in,
        out_specs=[o for p in parts for o in p.out_specs],
        scratch_shapes=[s for p in parts for s in p.scratch],
        compiler_params=pltpu.CompilerParams(
            collective_id=collective, has_side_effects=True, vmem_limit_bytes=vmem * 2**20
        ),
    )(*[a for p in parts for a in p.arrays])
    outs = list(outs)
    return [[outs.pop(0) for _ in p.outs] for p in parts]


def dot_nt(a, b):
    return lax.dot_general(a, b, (((1,), (1,)), ((), ())), preferred_element_type=F32)


def dot_nn(a, b):
    return lax.dot_general(a, b, (((1,), (0,)), ((), ())), preferred_element_type=F32)


def heads(index):
    return pl.ds(index * HEAD, HEAD)


def block_rows(j):
    return pl.ds(pl.multiple_of(j * BLOCK, BLOCK), BLOCK)


def transpose_blocks(src, dst):
    @pl.loop(0, src.shape[0] // BLOCK)
    def _(j):
        dst[j] = src[block_rows(j), :].astype(F32).T.astype(BF)


def visible(bounds, low, high, j):
    at = lax.broadcasted_iota(jnp.int32, (BLOCK, BLOCK), 0)
    start = j * BLOCK
    return (at >= bounds[low : low + 1, :] - start) & (at < bounds[high : high + 1, :] - start)


def attend_kernel(with_memory, local_from, mem_from, mem_to, *refs):
    if with_memory:
        q, k, v, bounds, mk, mv, out, stat, vt, mvt, acc, top, total = refs
    else:
        q, k, v, bounds, out, stat, vt, acc, top, total = refs
    i = pl.program_id(0)
    scale = HEAD ** (-0.5) * LOG2E

    @pl.when(i == 0)
    def _():
        transpose_blocks(v, vt)
        if with_memory:
            transpose_blocks(mv, mvt)

    acc[...] = jnp.zeros_like(acc)
    top[...] = jnp.full_like(top, NEG)
    total[...] = jnp.zeros_like(total)

    def run(keys, values_t, low, high):
        def body(j, _):
            seen = visible(bounds, low, high, j)
            for h in range(2):
                scores = dot_nt(keys[block_rows(j), heads(h)], q[:, heads(h)]) * scale
                scores = jnp.where(seen, scores, NEG)
                old = top[h : h + 1, :]
                new = jnp.maximum(old, jnp.max(scores, axis=0, keepdims=True))
                probs = jnp.exp2(scores - new)
                shrink = jnp.exp2(old - new)
                top[h : h + 1, :] = new
                total[h : h + 1, :] = total[h : h + 1, :] * shrink + jnp.sum(
                    probs, axis=0, keepdims=True
                )
                acc[heads(h), :] = acc[heads(h), :] * shrink + dot_nn(
                    values_t[j, heads(h), :], probs.astype(BF)
                )
            return 0

        return body

    lax.fori_loop(local_from[i], i + 1, run(k, vt, 0, 1), 0)
    if with_memory:
        lax.fori_loop(mem_from[i], mem_to[i], run(mk, mvt, 2, 3), 0)
    for h in range(2):
        share = total[h : h + 1, :]
        out[:, heads(h)] = (acc[heads(h), :] / share).T.astype(BF)
        stat[h : h + 1, :] = top[h : h + 1, :] + jnp.log2(share)
    stat[2:, :] = jnp.zeros_like(stat[2:, :])


def attend(q, k, v, memory, bounds, ranges):
    rows = q.shape[0]
    blocks = rows // BLOCK
    row_block = pl.BlockSpec((BLOCK, PAIR), lambda i, *_: (i, 0))
    lane_block = pl.BlockSpec((8, BLOCK), lambda i, *_: (0, i))
    operands = [q, k, v, bounds]
    in_specs = [row_block, VMEM, VMEM, lane_block]
    scratch = [pltpu.VMEM((blocks, PAIR, BLOCK), BF)]
    if memory is not None:
        operands += [memory[0], memory[1]]
        in_specs += [VMEM, VMEM]
        scratch += [pltpu.VMEM((memory[1].shape[0] // BLOCK, PAIR, BLOCK), BF)]
    return pl.pallas_call(
        functools.partial(attend_kernel, memory is not None),
        name="attend",
        grid_spec=pltpu.PrefetchScalarGridSpec(
            num_scalar_prefetch=3,
            grid=(blocks,),
            in_specs=in_specs,
            out_specs=(row_block, lane_block),
            scratch_shapes=scratch
            + [
                pltpu.VMEM((PAIR, BLOCK), F32),
                pltpu.VMEM((8, BLOCK), F32),
                pltpu.VMEM((8, BLOCK), F32),
            ],
        ),
        out_shape=(
            jax.ShapeDtypeStruct((rows, PAIR), BF),
            jax.ShapeDtypeStruct((8, rows), F32),
        ),
        compiler_params=pltpu.CompilerParams(vmem_limit_bytes=48 * 2**20),
    )(*ranges, *operands)


def attend_back_kernel(with_memory, local_from, mem_from, mem_to, *refs):
    if with_memory:
        (q, go, o, stat, bounds, k, v, mk, mv, gq, gk, gv, kt, mkt, delta, gq_t, gk_sum, gv_sum) = refs
    else:
        (q, go, o, stat, bounds, k, v, gq, gk, gv, kt, delta, gq_t, gk_sum, gv_sum) = refs
    i = pl.program_id(0)
    unit = HEAD ** (-0.5)
    scale = unit * LOG2E

    @pl.when(i == 0)
    def _():
        transpose_blocks(k, kt)
        gk_sum[...] = jnp.zeros_like(gk_sum)
        gv_sum[...] = jnp.zeros_like(gv_sum)
        if with_memory:
            transpose_blocks(mk, mkt)

    for h in range(2):
        both = go[:, heads(h)].astype(F32) * o[:, heads(h)].astype(F32)
        delta[h : h + 1, :] = jnp.sum(both.T, axis=0, keepdims=True)
    gq_t[...] = jnp.zeros_like(gq_t)

    def run(keys, values, keys_t, low, high, own):
        def body(j, _):
            seen = visible(bounds, low, high, j)
            for h in range(2):
                query, grad = q[:, heads(h)], go[:, heads(h)]
                scores = dot_nt(keys[block_rows(j), heads(h)], query) * scale
                probs = jnp.where(seen, jnp.exp2(scores - stat[h : h + 1, :]), 0.0)
                grad_probs = dot_nt(values[block_rows(j), heads(h)], grad)
                grad_scores = (probs * (grad_probs - delta[h : h + 1, :])).astype(BF)
                gq_t[heads(h), :] += dot_nn(keys_t[j, heads(h), :], grad_scores)
                if own:
                    gv_sum[block_rows(j), heads(h)] += dot_nn(probs.astype(BF), grad)
                    gk_sum[block_rows(j), heads(h)] += dot_nn(grad_scores, query)
            return 0

        return body

    lax.fori_loop(local_from[i], i + 1, run(k, v, kt, 0, 1, True), 0)
    if with_memory:
        lax.fori_loop(mem_from[i], mem_to[i], run(mk, mv, mkt, 2, 3, False), 0)
    gq[...] = (gq_t[...] * unit).T.astype(BF)

    @pl.when(i == pl.num_programs(0) - 1)
    def _():
        gk[...] = (gk_sum[...] * unit).astype(BF)
        gv[...] = gv_sum[...].astype(BF)


def attend_back(q, k, v, memory, bounds, ranges, out, stat, grad):
    rows = q.shape[0]
    blocks = rows // BLOCK
    row_block = pl.BlockSpec((BLOCK, PAIR), lambda i, *_: (i, 0))
    lane_block = pl.BlockSpec((8, BLOCK), lambda i, *_: (0, i))
    operands = [q, grad, out, stat, bounds, k, v]
    in_specs = [row_block, row_block, row_block, lane_block, lane_block, VMEM, VMEM]
    scratch = [pltpu.VMEM((blocks, PAIR, BLOCK), BF)]
    if memory is not None:
        operands += [memory[0], memory[1]]
        in_specs += [VMEM, VMEM]
        scratch += [pltpu.VMEM((memory[0].shape[0] // BLOCK, PAIR, BLOCK), BF)]
    whole = jax.ShapeDtypeStruct((rows, PAIR), BF)
    return pl.pallas_call(
        functools.partial(attend_back_kernel, memory is not None),
        name="attend_back",
        grid_spec=pltpu.PrefetchScalarGridSpec(
            num_scalar_prefetch=3,
            grid=(blocks,),
            in_specs=in_specs,
            out_specs=(row_block, VMEM, VMEM),
            scratch_shapes=scratch
            + [
                pltpu.VMEM((8, BLOCK), F32),
                pltpu.VMEM((PAIR, BLOCK), F32),
                pltpu.VMEM((rows, PAIR), F32),
                pltpu.VMEM((rows, PAIR), F32),
            ],
        ),
        out_shape=(whole, whole, whole),
        compiler_params=pltpu.CompilerParams(vmem_limit_bytes=48 * 2**20),
    )(*ranges, *operands)


def count(compared):
    return jnp.sum(compared.astype(jnp.int32), axis=1)


def mask_ranges(docs, mem_docs, reset):
    rows = docs.shape[0]
    entries = mem_docs.shape[0]
    at = jnp.arange(rows, dtype=jnp.int32)
    start = count(docs[None, :] < docs[:, None])
    mem_low = count(mem_docs[None, :] < docs[:, None])
    mem_high = count(mem_docs[None, :] <= docs[:, None])
    mem_low = jnp.where(reset == 0, mem_low, 0)
    mem_high = jnp.where(reset == 0, mem_high, 0)
    zero = jnp.zeros_like(start)
    bounds = jnp.stack((start, at + 1, mem_low, mem_high, zero, zero, zero, zero))

    def per_block(values):
        return values.reshape(rows // BLOCK, BLOCK)

    local_from = jnp.min(per_block(start), axis=1) // BLOCK
    some = mem_high > mem_low
    first = jnp.min(per_block(jnp.where(some, mem_low, entries)), axis=1)
    last = jnp.max(per_block(jnp.where(some, mem_high, 0)), axis=1)
    mem_from = first // BLOCK
    mem_to = jnp.maximum((last + BLOCK - 1) // BLOCK, mem_from)
    return bounds, (local_from, mem_from, mem_to)


def sort_memory(memory, mem_docs):
    entries = mem_docs.shape[0]
    at = jnp.arange(entries, dtype=jnp.int32)
    before = (mem_docs[None, :] < mem_docs[:, None]) | (
        (mem_docs[None, :] == mem_docs[:, None]) & (at[None, :] < at[:, None])
    )
    rank = count(before)
    moved = (rank[None, :] == at[:, None]).astype(BF)
    return tuple(
        jnp.dot(moved, memory[index], preferred_element_type=F32).astype(BF) for index in range(2)
    )


def columns(matrix, sizes):
    pieces, at = [], 0
    for size in sizes:
        pieces.append(matrix[:, at : at + size])
        at += size
    return pieces


def dot_tn(a, b):
    return lax.dot_general(a, b, (((0,), (0,)), ((), ())), preferred_element_type=F32)


def norm_rows(values, gain):
    inverse = lax.rsqrt(jnp.mean(values * values, axis=-1, keepdims=True) + EPS)
    return (values * inverse * gain).astype(BF), inverse


def norm_rows_back(values, gain, inverse, grad):
    grad_gain = jnp.sum(grad * values * inverse, axis=0)
    scaled = grad * gain
    mean = jnp.mean(scaled * values, axis=-1, keepdims=True)
    return inverse * scaled - values * inverse**3 * mean, grad_gain


def layer(stream, qkv_w, gains, steps, memory, bounds, ranges):
    gain_a, gain_b = gains
    normed, inverse_a = norm_rows(stream, gain_a)
    qkv = jnp.dot(normed, qkv_w, preferred_element_type=F32).astype(BF)
    q, k, v = steps[0](qkv)
    out, stat = attend(q, k, v, memory() if memory else None, bounds, ranges)
    attended, out_w, gate_up_w, down_w = steps[1](out)
    ff = down_w.shape[0]
    mixed = stream + jnp.dot(attended, out_w, preferred_element_type=F32)
    normed_ff, inverse_b = norm_rows(mixed, gain_b)
    gate_up = jnp.dot(normed_ff, gate_up_w, preferred_element_type=F32)
    gate, up = gate_up[:, :ff], gate_up[:, ff:]
    activated = (gate * jax.nn.sigmoid(gate) * up).astype(BF)
    result = mixed + jnp.dot(activated, down_w, preferred_element_type=F32)
    weights = (gain_a, qkv_w, out_w, gain_b, gate_up_w, down_w)
    kept = (stream, inverse_a, normed, q, k, v, out, stat, attended, mixed, inverse_b, normed_ff, gate, up, activated)
    return result, weights, kept


def ffn_back(grad_new, weights, kept):
    gain_a, qkv_w, out_w, gain_b, gate_up_w, down_w = weights
    attended, mixed, inverse_b, normed_ff, gate, up, activated = kept[8:]
    branch = grad_new.astype(BF)
    grad_down = dot_tn(activated, branch).astype(BF)
    grad_act = dot_nt(branch, down_w)
    sig = jax.nn.sigmoid(gate)
    grad_gate = (grad_act * up * sig * (1.0 + gate * (1.0 - sig))).astype(BF)
    grad_up = (grad_act * gate * sig).astype(BF)
    grad_gate_up = jnp.concatenate((grad_gate, grad_up), axis=1)
    grad_gate_up_w = dot_tn(normed_ff, grad_gate_up).astype(BF)
    grad_normed_ff = dot_nt(grad_gate_up, gate_up_w)
    back, grad_gain_b = norm_rows_back(mixed, gain_b, inverse_b, grad_normed_ff)
    grad_mixed = grad_new + back
    attn = grad_mixed.astype(BF)
    grad_out_w = dot_tn(attended, attn).astype(BF)
    grad_attended = dot_nt(attn, out_w).astype(BF)
    return grad_mixed, grad_attended, grad_out_w, grad_gain_b, grad_gate_up_w, grad_down


def projections_back(grad_mixed, grad_qkv, weights, kept):
    gain_a, qkv_w = weights[:2]
    stream, inverse_a, normed = kept[:3]
    grad_qkv_w = dot_tn(normed, grad_qkv).astype(BF)
    grad_normed = dot_nt(grad_qkv, qkv_w)
    back, grad_gain_a = norm_rows_back(stream, gain_a, inverse_a, grad_normed)
    return grad_mixed + back, grad_gain_a, grad_qkv_w


def gain_columns(gains):
    stacked = jnp.stack(gains, axis=1)
    return jnp.pad(stacked, ((0, 0), (0, HEAD - len(gains))))


def pair_rows(own, other, core):
    rows, width = own.shape
    both = jnp.where(core == 0, jnp.stack((own, other)), jnp.stack((other, own)))
    return lax.dynamic_slice_in_dim(both.reshape(2 * rows, width), core * (width // 2), width // 2, 1)


def head_local(
    tokens, token_docs, memory_docs, memory_resets, memory_keys, memory_values,
    attn_gain1, query_weight1, key_weight1, value_weight1, out_weight1,
    ffn_gain1, gate_weight1, up_weight1, down_weight1,
    attn_gain2, second_query_weight, key_weight2, value_weight2, out_weight2,
    ffn_gain2, gate_weight2, up_weight2, down_weight2, cotangent,
):
    count, width = query_weight1.shape
    ff = gate_weight1.shape[1]
    each = down_weight1.shape[0]
    core = lax.rem(lax.axis_index("key"), 2)
    seg = lax.axis_index("key") // LOCAL
    gains = gain_columns((attn_gain1, ffn_gain1, attn_gain2, ffn_gain2))
    qkv1 = jnp.concatenate((query_weight1, key_weight1, value_weight1), axis=1)
    qkv2 = jnp.concatenate((second_query_weight, key_weight2, value_weight2), axis=1)
    gate_up1 = jnp.concatenate((gate_weight1, up_weight1), axis=1)
    gate_up2 = jnp.concatenate((gate_weight2, up_weight2), axis=1)
    downs = jnp.concatenate((down_weight1, down_weight2), axis=0)
    docs = jnp.concatenate((token_docs, memory_docs), axis=0)
    pairs = PairBlocks(2 * each, width // 2)

    def own(matrix):
        return RowBlocks(count, matrix.shape[1])

    def gather(matrix):
        return Gather(matrix, own(matrix))

    (rows,), (docs,), (other,), (qkv1_w,), (gains,) = exchange(
        "bring_tokens", 1,
        [Rows(tokens), Docs(docs), Sibling(downs), gather(qkv1), gather(gains)],
    )
    down1 = pair_rows(down_weight1, other[:each], core)
    down2 = pair_rows(down_weight2, other[each:], core)
    own_docs = lax.dynamic_index_in_dim(docs, seg, 0, keepdims=False)
    own_mem_docs = lax.dynamic_index_in_dim(docs, seg + 2, 0, keepdims=False)
    reset = lax.dynamic_index_in_dim(memory_resets, seg, 0, keepdims=False)
    bounds, ranges = mask_ranges(own_docs, own_mem_docs, reset)
    gains = gains[:, :4].astype(F32)
    held = {}

    def heads1(qkv):
        swapped, (held["out1"],), (held["gu1"],), (held["down1"],), (mk,), (mv,) = exchange(
            "to_heads_1", 2,
            [Swap([qkv], True), gather(out_weight1), gather(gate_up1), Gather(down1, pairs),
             Memory(memory_keys), Memory(memory_values)],
        )
        held["memory"] = sort_memory((mk, mv), own_mem_docs)
        return swapped

    def rows1(out):
        (attended,), (held["qkv2"],) = exchange(
            "to_rows_1", 3, [Swap([out], False), gather(qkv2)]
        )
        return attended, held["out1"], held["gu1"], held["down1"]

    def heads2(qkv):
        swapped, (held["out2"],), (held["gu2"],) = exchange(
            "to_heads_2", 4, [Swap([qkv], True), gather(out_weight2), gather(gate_up2)]
        )
        return swapped

    def rows2(out):
        (attended,), (down,), (held["cot"],) = exchange(
            "to_rows_2", 5, [Swap([out], False), Gather(down2, pairs), Rows(cotangent)]
        )
        return attended, held["out2"], held["gu2"], down

    middle, weights1, kept1 = layer(
        rows.astype(F32), qkv1_w, (gains[:, 0], gains[:, 1]), (heads1, rows1), None, bounds, ranges
    )
    result, weights2, kept2 = layer(
        middle, held["qkv2"], (gains[:, 2], gains[:, 3]), (heads2, rows2),
        lambda: held["memory"], bounds, ranges,
    )

    def part(matrix, index, size):
        return ColumnBlocks(count, size, index)

    grad_mixed, grad_att, out_g2, gain_b2, gate_up_g2, down_g2 = ffn_back(
        held["cot"].astype(F32), weights2, kept2
    )
    (grad_out,), (output,), (gate_s2,), (up_s2,) = exchange(
        "back_to_heads_2", 6,
        [Swap([grad_att], True), Chunks(result.astype(BF)),
         Scatter(gate_up_g2, ColumnBlocks(count, ff, 0)),
         Scatter(gate_up_g2, ColumnBlocks(count, ff, 1), 1)],
        40,
    )
    q, k, v, out, stat = kept2[3:8]
    grads = attend_back(q, k, v, held["memory"], bounds, ranges, out, stat, grad_out)
    (grad_qkv,), (down_s2,), (out_s2,) = exchange(
        "back_to_rows_2", 7,
        [Swap(list(grads), False), Scatter(down_g2, pairs), Scatter(out_g2, own(out_g2), 1)],
        40,
    )
    grad_middle, gain_a2, qkv_g2 = projections_back(grad_mixed, grad_qkv, weights2, kept2)

    grad_mixed, grad_att, out_g1, gain_b1, gate_up_g1, down_g1 = ffn_back(
        grad_middle, weights1, kept1
    )
    (grad_out,), (gate_s1,), (up_s1,), (qkv_s2,) = exchange(
        "back_to_heads_1", 8,
        [Swap([grad_att], True),
         Scatter(gate_up_g1, ColumnBlocks(count, ff, 0)),
         Scatter(gate_up_g1, ColumnBlocks(count, ff, 1), 1),
         Scatter(qkv_g2, own(qkv_g2), 2)],
        44,
    )
    q, k, v, out, stat = kept1[3:8]
    grads = attend_back(q, k, v, None, bounds, ranges, out, stat, grad_out)
    (grad_qkv,), (down_s1,), (out_s1,) = exchange(
        "back_to_rows_1", 9,
        [Swap(list(grads), False), Scatter(down_g1, pairs), Scatter(out_g1, own(out_g1), 1)],
        40,
    )
    grad_rows, gain_a1, qkv_g1 = projections_back(grad_mixed, grad_qkv, weights1, kept1)
    gain_grads = gain_columns((gain_a1, gain_b1, gain_a2, gain_b2)).astype(BF)
    (grad_tokens,), (q_s1,), (k_s1,), (v_s1,), (gain_s,) = exchange(
        "back_to_owners", 10,
        [Chunks(grad_rows.astype(BF))]
        + [Scatter(qkv_g1, ColumnBlocks(count, width, i), i) for i in range(3)]
        + [Scatter(gain_grads, own(gain_grads), 2)],
        40,
    )
    q_s2, k_s2, v_s2 = columns(qkv_s2, (width,) * 3)
    return (
        output, grad_tokens.astype(F32),
        gain_s[:, 0], q_s1, k_s1, v_s1, out_s1, gain_s[:, 1], gate_s1, up_s1, down_s1,
        gain_s[:, 2], q_s2, k_s2, v_s2, out_s2, gain_s[:, 3], gate_s2, up_s2, down_s2,
    )


def solution(mesh):
    in_specs = (
        P("grp", "key", None),
        P("grp", "key"),
        P("grp", "key"),
        P("grp"),
        P("grp", "key", None),
        P("grp", "key", None),
        P(("grp", "key")),
        P(("grp", "key"), None),
        P(("grp", "key"), None),
        P(("grp", "key"), None),
        P(("grp", "key"), None),
        P(("grp", "key")),
        P(("grp", "key"), None),
        P(("grp", "key"), None),
        P(("grp", "key"), None),
        P(("grp", "key")),
        P(("grp", "key"), None),
        P(("grp", "key"), None),
        P(("grp", "key"), None),
        P(("grp", "key"), None),
        P(("grp", "key")),
        P(("grp", "key"), None),
        P(("grp", "key"), None),
        P(("grp", "key"), None),
        P("grp", "key", None),
    )
    out_specs = (
        P("grp", "key", None),
        P("grp", "key", None),
        P(("grp", "key")),
        P(("grp", "key"), None),
        P(("grp", "key"), None),
        P(("grp", "key"), None),
        P(("grp", "key"), None),
        P(("grp", "key")),
        P(("grp", "key"), None),
        P(("grp", "key"), None),
        P(("grp", "key"), None),
        P(("grp", "key")),
        P(("grp", "key"), None),
        P(("grp", "key"), None),
        P(("grp", "key"), None),
        P(("grp", "key"), None),
        P(("grp", "key")),
        P(("grp", "key"), None),
        P(("grp", "key"), None),
        P(("grp", "key"), None),
    )
    body = head_local if mesh.shape["key"] == HEADS else gathered_local
    return jax.shard_map(body, mesh=mesh, in_specs=in_specs, out_specs=out_specs, check_vma=False)
```

```python
import functools

import jax
import jax.numpy as jnp
from jax import lax
from jax.experimental import pallas as pl
from jax.experimental.pallas import tpu as pltpu
from jax.sharding import PartitionSpec as P

HEADS = 8


EPS = 1e-05
NEG = -1e30


def norm_forward(values, gain_vec):
    inverse = lax.rsqrt(jnp.mean(values * values, axis=-1, keepdims=True) + EPS)
    return (values * inverse * gain_vec, inverse)


def norm_backward(values, gain_vec, inverse, grad_normed):
    grad_gain = jnp.sum(grad_normed * values * inverse, axis=(0, 1))
    scaled = grad_normed * gain_vec
    grad_values = inverse * scaled - values * inverse**3 * jnp.mean(
        scaled * values, axis=-1, keepdims=True
    )
    return (grad_values, grad_gain)


def project(input_operand, weight_matrix):
    return jnp.dot(input_operand, weight_matrix, preferred_element_type=jnp.float32)


def project_back(gradient_row_block, weight_matrix):
    return jnp.einsum(
        "tzu,ku->tzk", gradient_row_block, weight_matrix, preferred_element_type=jnp.float32
    )


def outer_sum(input_arrays, gradient_reduced_precision):
    return jnp.einsum(
        "zhp,zhv->pv", input_arrays, gradient_reduced_precision, preferred_element_type=jnp.float32
    )


def split_heads(rows):
    return rows.reshape(rows.shape[0], rows.shape[1], HEADS, rows.shape[2] // HEADS)


def fetch_weights(shards):
    return (
        lax.all_gather(shards[0], ("grp", "key"), axis=0, tiled=True),
        lax.all_gather(shards[1], ("grp", "key"), axis=0, tiled=True),
        lax.all_gather(shards[2], ("grp", "key"), axis=0, tiled=True),
        lax.all_gather(shards[3], ("grp", "key"), axis=0, tiled=True),
        lax.all_gather(shards[4], ("grp", "key"), axis=0, tiled=True),
        lax.all_gather(shards[5], ("grp", "key"), axis=0, tiled=True),
        lax.all_gather(shards[6], ("grp", "key"), axis=0, tiled=True),
        lax.all_gather(shards[7], ("grp", "key"), axis=0, tiled=True),
        lax.all_gather(shards[8], ("grp", "key"), axis=0, tiled=True),
    )


def refetch_weights(shards):
    return (
        lax.all_gather(shards[0], ("grp", "key"), axis=0, tiled=True),
        lax.all_gather(shards[1], ("grp", "key"), axis=0, tiled=True),
        lax.all_gather(shards[2], ("grp", "key"), axis=0, tiled=True),
        lax.all_gather(shards[3], ("grp", "key"), axis=0, tiled=True),
        lax.all_gather(shards[4], ("grp", "key"), axis=0, tiled=True),
        lax.all_gather(shards[5], ("grp", "key"), axis=0, tiled=True),
        lax.all_gather(shards[6], ("grp", "key"), axis=0, tiled=True),
        lax.all_gather(shards[7], ("grp", "key"), axis=0, tiled=True),
        lax.all_gather(shards[8], ("grp", "key"), axis=0, tiled=True),
    )


def reduce_gradient_sums(terms):
    return (
        lax.psum_scatter(terms[0], ("grp", "key"), scatter_dimension=0, tiled=True),
        lax.psum_scatter(terms[1], ("grp", "key"), scatter_dimension=0, tiled=True),
        lax.psum_scatter(terms[2], ("grp", "key"), scatter_dimension=0, tiled=True),
        lax.psum_scatter(terms[3], ("grp", "key"), scatter_dimension=0, tiled=True),
        lax.psum_scatter(terms[4], ("grp", "key"), scatter_dimension=0, tiled=True),
        lax.psum_scatter(terms[5], ("grp", "key"), scatter_dimension=0, tiled=True),
        lax.psum_scatter(terms[6], ("grp", "key"), scatter_dimension=0, tiled=True),
        lax.psum_scatter(terms[7], ("grp", "key"), scatter_dimension=0, tiled=True),
        lax.psum_scatter(terms[8], ("grp", "key"), scatter_dimension=0, tiled=True),
    )


def head_scores(query_all, key_block, allowed):
    head_size = query_all.shape[2] // HEADS
    raw_scores = jnp.einsum(
        "sqhd,skhd->shqk",
        split_heads(query_all),
        split_heads(key_block),
        preferred_element_type=jnp.float32,
    ) * head_size ** (-0.5)
    return jnp.where(allowed[:, None], raw_scores, NEG)


def attend_forward(query_all, key_block, value_block, allowed):
    scores = head_scores(query_all, key_block, allowed)
    row_top = lax.pmax(jnp.max(scores, axis=3).astype(jnp.bfloat16), "key").astype(jnp.float32)
    exp_scores = jnp.where(allowed[:, None], jnp.exp(scores - row_top[..., None]), 0.0)
    row_total = lax.psum(jnp.sum(exp_scores, axis=3).astype(jnp.bfloat16), "key").astype(
        jnp.float32
    )
    probability = exp_scores / row_total[..., None]
    partial_value = jnp.einsum(
        "shqk,skhd->sqhd",
        probability.astype(jnp.bfloat16),
        split_heads(value_block),
        preferred_element_type=jnp.float32,
    )
    partial_value = partial_value.reshape(query_all.shape)
    attended = lax.psum_scatter(
        partial_value.astype(jnp.bfloat16), "key", scatter_dimension=1, tiled=True
    ).astype(jnp.float32)
    return (attended, row_top, row_total)


def layer_forward(stream, full_weights, allowed, extra_keys, extra_values):
    gain_a, query_w, key_w, value_w, out_w, gain_b, gate_w, up_w, down_w = full_weights
    normed, first_inverse_factor = norm_forward(stream, gain_a.astype(jnp.float32))
    normed_low = normed.astype(jnp.bfloat16)
    query_low = project(normed_low, query_w).astype(jnp.bfloat16)
    key_low = project(normed_low, key_w).astype(jnp.bfloat16)
    value_low = project(normed_low, value_w).astype(jnp.bfloat16)
    query_all = lax.all_gather(query_low, "key", axis=1, tiled=True)
    if extra_keys is None:
        key_block = key_low
        value_block = value_low
    else:
        key_block = jnp.concatenate((key_low, extra_keys), axis=1)
        value_block = jnp.concatenate((value_low, extra_values), axis=1)
    attended, row_top, row_total = attend_forward(query_all, key_block, value_block, allowed)
    attended_low = attended.astype(jnp.bfloat16)
    mixed_stream = stream + project(attended_low, out_w)
    normed_ff, inverse_b = norm_forward(mixed_stream, gain_b.astype(jnp.float32))
    normed_ff_low = normed_ff.astype(jnp.bfloat16)
    gate_value = project(normed_ff_low, gate_w)
    up_value = project(normed_ff_low, up_w)
    activated_low = (gate_value * jax.nn.sigmoid(gate_value) * up_value).astype(jnp.bfloat16)
    result = mixed_stream + project(activated_low, down_w)
    kept_state = (
        stream,
        first_inverse_factor,
        normed_low,
        key_block,
        value_block,
        query_all,
        row_top,
        row_total,
        attended_low,
        mixed_stream,
        inverse_b,
        normed_ff_low,
        gate_value,
        up_value,
        activated_low,
    )
    return (result, kept_state)


def layer_backward(grad_result, full_weights, kept_state, allowed):
    gain_a, query_w, key_w, value_w, out_w, gain_b, gate_w, up_w, down_w = full_weights
    (
        stream,
        first_inverse_factor,
        normed_low,
        key_block,
        value_block,
        query_all,
        row_top,
        row_total,
        attended_low,
        mixed_stream,
        inverse_b,
        normed_ff_low,
        gate_value,
        up_value,
        activated_low,
    ) = kept_state
    own_rows = stream.shape[1]
    branch_low = grad_result.astype(jnp.bfloat16)
    grad_down = outer_sum(activated_low, branch_low)
    grad_act = project_back(branch_low, down_w)
    sigmoid_gate = jax.nn.sigmoid(gate_value)
    grad_gate = (
        grad_act * up_value * sigmoid_gate * (1.0 + gate_value * (1.0 - sigmoid_gate))
    ).astype(jnp.bfloat16)
    grad_up_low = (grad_act * gate_value * sigmoid_gate).astype(jnp.bfloat16)
    grad_gate_w = outer_sum(normed_ff_low, grad_gate)
    grad_up_w = outer_sum(normed_ff_low, grad_up_low)
    grad_normed_ff = project_back(grad_gate, gate_w) + project_back(grad_up_low, up_w)
    grad_mixed_norm, grad_gain_b = norm_backward(
        mixed_stream, gain_b.astype(jnp.float32), inverse_b, grad_normed_ff
    )
    grad_mixed = grad_result + grad_mixed_norm
    attn_low = grad_mixed.astype(jnp.bfloat16)
    grad_out_w = outer_sum(attended_low, attn_low)
    grad_attended = project_back(attn_low, out_w).astype(jnp.bfloat16)
    grad_all = lax.all_gather(grad_attended, "key", axis=1, tiled=True)
    scores = head_scores(query_all, key_block, allowed)
    probability = (
        jnp.where(allowed[:, None], jnp.exp(scores - row_top[..., None]), 0.0)
        / row_total[..., None]
    )
    grad_heads = split_heads(grad_all)
    grad_probs = jnp.einsum(
        "sqhd,skhd->shqk", grad_heads, split_heads(value_block), preferred_element_type=jnp.float32
    )
    row_delta = lax.psum(
        jnp.sum(probability * grad_probs, axis=3).astype(jnp.bfloat16), "key"
    ).astype(jnp.float32)
    grad_scores = (probability * (grad_probs - row_delta[..., None])).astype(jnp.bfloat16)
    score_scale = (query_all.shape[2] // HEADS) ** (-0.5)
    query_part = (
        jnp.einsum(
            "shqk,skhd->sqhd",
            grad_scores,
            split_heads(key_block),
            preferred_element_type=jnp.float32,
        ).reshape(query_all.shape)
        * score_scale
    )
    grad_query = lax.psum_scatter(
        query_part.astype(jnp.bfloat16), "key", scatter_dimension=1, tiled=True
    )
    own_scores = grad_scores[..., :own_rows]
    grad_key = (
        jnp.einsum(
            "shqk,sqhd->skhd",
            own_scores,
            split_heads(query_all),
            preferred_element_type=jnp.float32,
        ).reshape(stream.shape)
        * score_scale
    ).astype(jnp.bfloat16)
    own_probs = probability.astype(jnp.bfloat16)[..., :own_rows]
    grad_value = (
        jnp.einsum("shqk,sqhd->skhd", own_probs, grad_heads, preferred_element_type=jnp.float32)
        .reshape(stream.shape)
        .astype(jnp.bfloat16)
    )
    grad_query_w = outer_sum(normed_low, grad_query)
    grad_key_w = outer_sum(normed_low, grad_key)
    grad_value_w = outer_sum(normed_low, grad_value)
    grad_normed = (
        project_back(grad_query, query_w)
        + project_back(grad_key, key_w)
        + project_back(grad_value, value_w)
    )
    grad_stream_norm, grad_gain_a = norm_backward(
        stream, gain_a.astype(jnp.float32), first_inverse_factor, grad_normed
    )
    grad_stream = grad_mixed + grad_stream_norm
    terms = (
        grad_gain_a,
        grad_query_w,
        grad_key_w,
        grad_value_w,
        grad_out_w,
        grad_gain_b,
        grad_gate_w,
        grad_up_w,
        grad_down,
    )
    return (grad_stream, terms)


def gathered_local(
    tokens,
    token_docs,
    memory_docs,
    memory_resets,
    memory_keys,
    memory_values,
    attn_gain1,
    query_weight1,
    key_weight1,
    value_weight1,
    out_weight1,
    ffn_gain1,
    gate_weight1,
    up_weight1,
    down_weight1,
    attn_gain2,
    second_query_weight,
    key_weight2,
    value_weight2,
    out_weight2,
    ffn_gain2,
    gate_weight2,
    up_weight2,
    down_weight2,
    cotangent,
):
    first_shards = (
        attn_gain1,
        query_weight1,
        key_weight1,
        value_weight1,
        out_weight1,
        ffn_gain1,
        gate_weight1,
        up_weight1,
        down_weight1,
    )
    second_shards = (
        attn_gain2,
        second_query_weight,
        key_weight2,
        value_weight2,
        out_weight2,
        ffn_gain2,
        gate_weight2,
        up_weight2,
        down_weight2,
    )
    docs_all = lax.all_gather(token_docs, "key", axis=1, tiled=True)
    own_rows = tokens.shape[1]
    query_place = jnp.arange(docs_all.shape[1], dtype=jnp.int32)
    key_place = lax.axis_index("key") * own_rows + jnp.arange(own_rows, dtype=jnp.int32)
    local_allowed = (key_place[None, None, :] <= query_place[None, :, None]) & (
        token_docs[:, None, :] == docs_all[:, :, None]
    )
    memory_allowed = (memory_docs[:, None, :] == docs_all[:, :, None]) & (
        memory_resets[:, None, None] == 0
    )
    both_allowed = jnp.concatenate((local_allowed, memory_allowed), axis=2)
    stream = tokens.astype(jnp.float32)
    first_full = fetch_weights(first_shards)
    middle, first_state = layer_forward(stream, first_full, local_allowed, None, None)
    second_full = fetch_weights(second_shards)
    result, second_state = layer_forward(
        middle, second_full, both_allowed, memory_keys, memory_values
    )
    second_full = refetch_weights(second_shards)
    grad_middle, second_terms = layer_backward(
        cotangent.astype(jnp.float32), second_full, second_state, both_allowed
    )
    second_grads = reduce_gradient_sums(second_terms)
    first_full = refetch_weights(first_shards)
    grad_stream, first_terms = layer_backward(grad_middle, first_full, first_state, local_allowed)
    first_grads = reduce_gradient_sums(first_terms)
    return (
        result.astype(jnp.bfloat16),
        grad_stream,
        first_grads[0],
        first_grads[1],
        first_grads[2],
        first_grads[3],
        first_grads[4],
        first_grads[5],
        first_grads[6],
        first_grads[7],
        first_grads[8],
        second_grads[0],
        second_grads[1],
        second_grads[2],
        second_grads[3],
        second_grads[4],
        second_grads[5],
        second_grads[6],
        second_grads[7],
        second_grads[8],
    )


MESH = pl.DeviceIdType.MESH
ANY = pl.BlockSpec(memory_space=pl.ANY)
VMEM = pl.BlockSpec(memory_space=pltpu.VMEM)
LOG2E = 1.4426950408889634
BLOCK = 512
QUERIES = 512
LOCAL = 4
HEAD = 128
PAIR = 2 * HEAD
BF = jnp.bfloat16
F32 = jnp.float32


SEND = pltpu.SemaphoreType.DMA


def flip(value, change):
    return lax.rem(value + change, 2)


class Place:
    def __init__(self):
        self.grp = lax.axis_index("grp")
        self.key = lax.axis_index("key")
        self.y, self.x = self.grp // 2, lax.rem(self.grp, 2)
        self.z, self.core = self.key // 2, lax.rem(self.key, 2)
        self.rank = lax.rem(self.key, LOCAL)
        self.seg = self.key // LOCAL

    def chip(self, da, db, dz, core):
        dx = da * (1 - core) + db * core
        dy = da * core + db * (1 - core)
        z = flip(self.z // 2, dz // 2) * 2 + flip(lax.rem(self.z, 2), lax.rem(dz, 2))
        return flip(self.y, dy) * 2 + flip(self.x, dx), z

    def device(self, da, db, dz):
        grp, z = self.chip(da, db, dz, self.core)
        return grp, z * 2 + self.core

    def sibling(self):
        return self.grp, self.z * 2 + 1 - self.core


def remote(src, dst, send, recv, target):
    return pltpu.make_async_remote_copy(
        src_ref=src, dst_ref=dst, send_sem=send, recv_sem=recv,
        device_id=target, device_id_type=MESH,
    )


def local(src, dst, sem):
    return pltpu.make_async_copy(src, dst, sem)


def span(index, size):
    return pl.ds(pl.multiple_of(index * size, size), size)


class RowBlocks:
    def __init__(self, rows, width):
        self.shape = (rows, width)

    def whole(self, chips):
        return (chips * 2 * self.shape[0], self.shape[1])

    def at(self, ref, chip, core):
        return ref.at[span((chip[0] * LOCAL + chip[1]) * 2 + core, self.shape[0]), :]


class PairBlocks(RowBlocks):
    def whole(self, chips):
        return (chips * self.shape[0], 2 * self.shape[1])

    def at(self, ref, chip, core):
        rows, width = self.shape
        return ref.at[span(chip[0] * LOCAL + chip[1], rows), span(core, width)]


class ColumnBlocks(RowBlocks):
    def __init__(self, rows, width, part):
        self.shape = (rows, width)
        self.part = part

    def at(self, ref, chip, core):
        rows, width = self.shape
        return ref.at[
            span((chip[0] * LOCAL + chip[1]) * 2 + core, rows), pl.ds(self.part * width, width)
        ]


class Swap:
    def __init__(self, arrays, to_heads):
        self.arrays = arrays
        self.to_heads = to_heads
        if to_heads:
            rows, width = arrays[0].shape
            self.parts = width // (LOCAL * PAIR)
            self.outs = [jax.ShapeDtypeStruct((rows * LOCAL, PAIR), BF)] * self.parts
        else:
            rows = arrays[0].shape[0] // LOCAL
            self.parts = len(arrays)
            self.outs = [jax.ShapeDtypeStruct((rows, self.parts * LOCAL * PAIR), BF)]
        self.rows = rows
        self.scratch = [SEND((self.parts, LOCAL)), SEND((self.parts, LOCAL)), SEND((self.parts,))]
        self.out_specs = [ANY] * len(self.outs)

    def run(self, at, ins, outs, scratch):
        send, recv, here = scratch

        def copy(part, k):
            target = lax.rem(at.rank + k, LOCAL)
            if self.to_heads:
                src = ins[0].at[:, span(part * LOCAL + target, PAIR)]
                dst = outs[part].at[span(at.rank, self.rows), :]
            else:
                src = ins[part].at[span(target, self.rows), :]
                dst = outs[0].at[:, span(part * LOCAL + at.rank, PAIR)]
            if k == 0:
                return local(src, dst, here.at[part])
            device = (at.grp, at.seg * LOCAL + target)
            return remote(src, dst, send.at[part, k], recv.at[part, k], device)

        every = [(part, k) for part in range(self.parts) for k in (2, 3, 1, 0)]
        for part, k in every:
            copy(part, k).start()
        yield
        yield "last"
        for part, k in every:
            copy(part, k).wait()


class Rows:
    def __init__(self, array):
        segs, rows, width = array.shape
        self.arrays = [array]
        self.rows = rows
        self.outs = [jax.ShapeDtypeStruct((segs * rows, width), array.dtype)]
        self.out_specs = [ANY]
        self.scratch = [SEND((2,)), SEND((2,)), SEND(())]

    def run(self, at, ins, outs, scratch):
        (src,), (dst,) = ins, outs
        send, recv, here = scratch
        chunk = lax.rem(at.key, 2)

        def part(index):
            return dst.at[span(index, self.rows), :]

        def out(seg):
            target = seg * LOCAL + at.key // 2
            return target, remote(
                src.at[seg], part(chunk), send.at[seg], recv.at[chunk], (at.grp, target)
            )

        for seg in range(2):
            target, copy = out(seg)
            pl.when(target != at.key)(copy.start)
            pl.when(target == at.key)(local(src.at[seg], part(chunk), here).start)
        yield
        yield "last"
        for seg in range(2):
            target, copy = out(seg)
            pl.when(target != at.key)(copy.wait_send)
        for index in range(2):
            owner = 2 * at.rank + index
            copy = remote(src.at[0], part(index), send.at[0], recv.at[index], (at.grp, owner))
            pl.when(owner != at.key)(copy.wait_recv)
            pl.when(owner == at.key)(local(src.at[0], part(index), here).wait)


class Chunks:
    def __init__(self, array):
        rows, width = array.shape
        self.arrays = [array]
        self.rows = rows // 2
        self.outs = [jax.ShapeDtypeStruct((2, rows // 2, width), array.dtype)]
        self.out_specs = [ANY]
        self.scratch = [SEND((2,)), SEND((2,)), SEND(())]

    def run(self, at, ins, outs, scratch):
        (src,), (dst,) = ins, outs
        send, recv, here = scratch

        def part(index):
            return src.at[pl.ds(index * self.rows, self.rows), :]

        def out(index):
            target = 2 * at.rank + index
            return target, remote(
                part(index), dst.at[at.seg], send.at[index], recv.at[at.seg], (at.grp, target)
            )

        for index in range(2):
            target, copy = out(index)
            pl.when(target != at.key)(copy.start)
            pl.when(target == at.key)(local(part(index), dst.at[at.seg], here).start)
        yield
        yield "last"
        for index in range(2):
            target, copy = out(index)
            pl.when(target != at.key)(copy.wait_send)
        for seg in range(2):
            owner = seg * LOCAL + at.key // 2
            copy = remote(part(0), dst.at[seg], send.at[0], recv.at[seg], (at.grp, owner))
            pl.when(owner != at.key)(copy.wait_recv)
            pl.when(owner == at.key)(local(part(0), dst.at[seg], here).wait)


class Memory:
    def __init__(self, array):
        self.arrays = [array]
        self.rows = array.shape[1]
        self.outs = [jax.ShapeDtypeStruct((2 * LOCAL * self.rows, PAIR), BF)]
        self.out_specs = [ANY]
        self.scratch = [SEND((2 * LOCAL,)), SEND((2 * LOCAL,)), SEND(())]

    def run(self, at, ins, outs, scratch):
        send, recv, here = scratch

        def copy(k):
            target = lax.rem(at.key + k, 2 * LOCAL)
            src = ins[0].at[target // LOCAL, :, span(lax.rem(target, LOCAL), PAIR)]
            dst = outs[0].at[span(at.key, self.rows), :]
            if k == 0:
                return local(src, dst, here)
            return remote(src, dst, send.at[k], recv.at[k], (at.grp, target))

        for k in range(2 * LOCAL):
            copy(k).start()
        yield
        yield "last"
        for k in range(2 * LOCAL):
            copy(k).wait()


class Docs:
    def __init__(self, array):
        rows, self.width = array.shape
        self.arrays = [array]
        self.outs = [jax.ShapeDtypeStruct((rows, 2 * LOCAL * self.width), array.dtype)]
        self.out_specs = [ANY]
        self.scratch = [SEND((2 * LOCAL,)), SEND((2 * LOCAL,)), SEND(())]

    def run(self, at, ins, outs, scratch):
        send, recv, here = scratch

        def copy(k):
            target = lax.rem(at.key + k, 2 * LOCAL)
            dst = outs[0].at[:, span(at.key, self.width)]
            if k == 0:
                return local(ins[0], dst, here)
            return remote(ins[0], dst, send.at[k], recv.at[k], (at.grp, target))

        for k in range(2 * LOCAL):
            copy(k).start()
        yield
        yield "last"
        for k in range(2 * LOCAL):
            copy(k).wait()


class Sibling:
    def __init__(self, array):
        self.arrays = [array]
        self.outs = [jax.ShapeDtypeStruct(array.shape, array.dtype)]
        self.out_specs = [ANY]
        self.scratch = [SEND(()), SEND(())]

    def run(self, at, ins, outs, scratch):
        copy = remote(ins[0], outs[0], scratch[0], scratch[1], at.sibling())
        copy.start()
        yield
        yield "last"
        copy.wait()


STEPS = [(da, db, dz) for db in range(2) for da in range(2) for dz in range(4)]


class Gather:
    def __init__(self, shard, blocks):
        self.arrays = [shard]
        self.blocks = blocks
        self.outs = [jax.ShapeDtypeStruct(blocks.whole(4 * LOCAL), shard.dtype)]
        self.out_specs = [ANY]
        self.scratch = [SEND((36,)), SEND((36,)), SEND(())]

    def run(self, at, ins, outs, scratch):
        (shard,), (whole,) = ins, outs
        send, recv, here = scratch
        core = at.core

        def spot(step, of=core):
            return self.blocks.at(whole, at.chip(*step, of), of)

        def copy(step, slot, target):
            mine = isinstance(step[2], int) and step == (0, 0, 0)
            src = shard if mine else spot(step)
            return remote(src, spot(step), send.at[slot], recv.at[slot], target)

        def cross(step):
            da, db, dz = step
            return 20 + 8 * db + 4 * da + dz

        def first(dz):
            return copy((0, 0, dz), 8 + dz, at.device(1, 0, 0))

        def second(da, dz):
            return copy((da, 0, dz), 12 + 4 * da + dz, at.device(0, 1, 0))

        def across(step):
            return copy(step, cross(step), at.sibling())

        def arrived(step, slot):
            dst = spot(step)
            remote(dst, dst, send.at[slot], recv.at[slot], at.sibling()).wait_recv()

        inner = flip(at.z // 2, lax.rem(at.z, 2))
        near, turns = at.device(0, 0, 1), (1, 2 + inner, 3 - inner)
        far = at.device(0, 0, 3)
        inside = pl.when(inner == 1)

        def along_z(index):
            if index == 0:
                return remote(shard, spot((0, 0, 0)), send.at[0], recv.at[1], near)
            if index == 1:
                return remote(shard, spot((0, 0, 0)), send.at[1], recv.at[3], far)
            step, slot, device = {
                2: ((0, 0, 1), 2, far), 3: ((0, 0, 3), 2, near), 4: ((0, 0, 2), 3, near)
            }[index]
            return remote(spot(step), spot(step), send.at[index], recv.at[slot], device)

        mine = local(shard, spot((0, 0, 0)), here)
        mine.start()
        along_z(0).start()
        inside(along_z(1).start)
        first(0).start()
        second(0, 0).start()
        across((0, 0, 0)).start()
        yield
        for turn, dz in enumerate(turns):
            arrived((0, 0, dz), dz)
            inside(along_z((2, 3, 4)[turn]).start)
            first(dz).start()
            second(0, dz).start()
            across((0, 0, dz)).start()
        yield
        for dz in (0,) + turns:
            arrived((1, 0, dz), 8 + dz)
            second(1, dz).start()
            across((1, 0, dz)).start()
        yield
        for da in range(2):
            for dz in (0,) + turns:
                arrived((da, 1, dz), 12 + 4 * da + dz)
                across((da, 1, dz)).start()
        yield "last"
        for step in STEPS:
            dst = spot(step, 1 - core)
            slot = cross(step)
            remote(dst, dst, send.at[slot], recv.at[slot], at.sibling()).wait_recv()
        along_z(0).wait_send()
        for index in range(1, 5):
            inside(along_z(index).wait_send)
        for dz in range(4):
            first(dz).wait_send()
            for da in range(2):
                second(da, dz).wait_send()
        for step in STEPS:
            across(step).wait_send()
        mine.wait()


def add_into(dst, parts, tile):
    rows, width = dst.shape

    @pl.loop(0, width // tile)
    def _(t):
        cut = pl.ds(pl.multiple_of(t * tile, tile), tile)
        total = parts[0][:, cut].astype(F32)
        for part in parts[1:]:
            total += part[:, cut].astype(F32)
        dst[:, cut] = total.astype(dst.dtype)


class Assemble:
    def __init__(self, groups, blocks):
        self.arrays = list(groups)
        self.blocks = blocks
        self.outs = [jax.ShapeDtypeStruct(b.whole(4 * LOCAL), groups[0].dtype) for b in blocks]
        self.out_specs = [ANY] * len(blocks)
        n = len(blocks)
        self.scratch = [SEND((n, 16)), SEND((n, 16)), SEND((n, 16))]

    def run(self, at, ins, outs, scratch):
        send, recv, here = scratch

        def each():
            begin = 0
            for index, blocks in enumerate(self.blocks):
                for slot in range(16):
                    yield index, slot, pl.ds(begin, blocks.shape[1])
                begin += blocks.shape[1]

        def spot(index, slot, core):
            return self.blocks[index].at(outs[index], at.chip(*STEPS[slot], core), core)

        def copies(index, slot, cut):
            src = ins[slot // 4].at[slot % 4, :, cut]
            dst = spot(index, slot, at.core)
            return remote(
                src, dst, send.at[index, slot], recv.at[index, slot], at.sibling()
            ), local(src, dst, here.at[index, slot])

        for spec in each():
            for copy in copies(*spec):
                copy.start()
        yield
        yield "last"
        for index, slot, cut in each():
            across, own = copies(index, slot, cut)
            across.wait_send()
            own.wait()
            dst = spot(index, slot, 1 - at.core)
            remote(dst, dst, send.at[index, slot], recv.at[index, slot], at.sibling()).wait_recv()


PACK = 16


class CoreSums:
    def __init__(self, *wholes):
        self.arrays = [whole for whole, _ in wholes]
        self.blocks = [blocks for _, blocks in wholes]
        shapes = [blocks.shape for blocks in self.blocks]
        self.width = sum(rows // PACK * width for rows, width in shapes)
        self.outs = [jax.ShapeDtypeStruct((n, PACK, self.width), BF) for n in (4, 4, 8)]
        self.out_specs = [ANY] * 3
        n = len(shapes)
        self.scratch = [pltpu.VMEM((16,) + shape, BF) for shape in shapes] * 2
        self.scratch += [pltpu.VMEM((16, PACK, self.width), BF)]
        self.scratch += [SEND((n, 16)), SEND((n, 16)), SEND((n, 16)), SEND((16,))]

    def run(self, at, ins, outs, scratch):
        n = len(ins)
        own, near, packed = scratch[:n], scratch[n : 2 * n], scratch[2 * n]
        load, send, recv, store = scratch[2 * n + 1 :]

        def chip(slot, core):
            return at.chip(lax.rem(slot // 4, 2), slot // 8, lax.rem(slot, 4), core)

        def fetch(index, slot):
            src = self.blocks[index].at(ins[index], chip(slot, at.core), at.core)
            return local(src, own[index].at[slot], load.at[index, slot])

        def across(index, slot):
            other = 1 - at.core
            src = self.blocks[index].at(ins[index], chip(slot, other), other)
            return remote(
                src, near[index].at[slot], send.at[index, slot], recv.at[index, slot], at.sibling()
            )

        def keep(slot, group, first):
            return local(packed.at[slot], outs[group].at[slot - first], store.at[slot])

        @pl.loop(0, 16)
        def _(turn):
            for index in range(n):
                across(index, 15 - turn).start()
                fetch(index, 15 - turn).start()

        yield
        groups = ((2, 8, 8), (1, 4, 4), (0, 0, 4))
        for group, first, count in groups:

            @pl.loop(0, count)
            def _(turn):
                slot = first + count - 1 - turn
                begin = 0
                for index in range(n):
                    fetch(index, slot).wait()
                    across(index, slot).wait_recv()
                    rows, width = self.blocks[index].shape
                    for part in range(rows // PACK):
                        cut = pl.ds(part * PACK, PACK)
                        add_into(
                            packed.at[slot, :, pl.ds(begin, width)],
                            [own[index].at[slot, cut, :], near[index].at[slot, cut, :]],
                            512,
                        )
                        begin += width
                keep(slot, group, first).start()

            yield
        yield "last"
        for group, first, count in groups:

            @pl.loop(0, count)
            def _(turn):
                slot = first + count - 1 - turn
                for index in range(n):
                    across(index, slot).wait_send()
                keep(slot, group, first).wait()


def unpack(total, shapes):
    blocks, begin = [], 0
    for rows, width in shapes:
        parts = rows // PACK
        cut = total[:, begin : begin + parts * width].reshape(PACK, parts, width)
        blocks.append(cut.transpose(1, 0, 2).reshape(rows, width))
        begin += parts * width
    return blocks


class Scatter:
    def __init__(self, whole, blocks, turn=0):
        self.arrays = [whole]
        self.blocks = blocks
        self.turn = turn
        shape = blocks.shape
        self.pair = isinstance(blocks, PairBlocks)
        self.tile = 256 if shape[1] % 256 == 0 else 128
        out = (shape[0] // 2, 2 * shape[1]) if self.pair else shape
        self.outs = [jax.ShapeDtypeStruct(out, F32)]
        self.out_specs = [VMEM]
        dma = SEND
        self.scratch = [
            pltpu.VMEM((16,) + shape, BF),
            pltpu.VMEM((16,) + shape, BF),
            pltpu.VMEM((8,) + shape, BF),
            pltpu.VMEM((4,) + shape, BF),
            pltpu.VMEM((4,) + shape, BF),
            dma((16,)),
            dma((32,)),
            dma((32,)),
        ]
        if self.pair:
            self.scratch += [pltpu.VMEM(shape, F32), dma((2,))]

    def run(self, at, ins, outs, scratch):
        (whole,), (out,) = ins, outs
        own, near, from_b, from_a, from_z, load, send, recv = scratch[:8]
        core = at.core
        order = list(reversed(STEPS))

        def fetch(slot):
            src = self.blocks.at(whole, at.chip(*STEPS[slot], core), core)
            return local(src, own.at[slot], load.at[slot])

        def across(slot):
            src = self.blocks.at(whole, at.chip(*STEPS[slot], 1 - core), 1 - core)
            return remote(src, near.at[slot], send.at[slot], recv.at[slot], at.sibling())

        def second(da, dz):
            slot = STEPS.index((da, 1, dz))
            spot = 4 * da + dz
            return remote(
                own.at[slot], from_b.at[spot], send.at[16 + spot], recv.at[16 + spot],
                at.device(0, 1, 0),
            )

        def first(dz):
            slot = STEPS.index((1, 0, dz))
            return remote(
                own.at[slot], from_a.at[dz], send.at[24 + dz], recv.at[24 + dz], at.device(1, 0, 0)
            )

        def along_z(dz):
            slot = STEPS.index((0, 0, dz))
            return remote(
                own.at[slot], from_z.at[dz], send.at[28 + dz], recv.at[28 + dz], at.device(0, 0, dz)
            )

        for step in order:
            slot = STEPS.index(step)
            across(slot).start()
            fetch(slot).start()
        for _ in range(1 + self.turn):
            yield

        def settle(step, more, dst=None):
            slot = STEPS.index(step)
            fetch(slot).wait()
            across(slot).wait_recv()
            parts = [own.at[slot], near.at[slot]] + more
            add_into(own.at[slot] if dst is None else dst, parts, self.tile)

        for da in (1, 0):
            for dz in (3, 2, 1, 0):
                settle((da, 1, dz), [])
                second(da, dz).start()
        yield
        for dz in (3, 2, 1, 0):
            second(1, dz).wait_recv()
            settle((1, 0, dz), [from_b.at[4 + dz]])
            first(dz).start()
        yield
        for dz in (3, 2, 1):
            second(0, dz).wait_recv()
            first(dz).wait_recv()
            settle((0, 0, dz), [from_b.at[dz], from_a.at[dz]])
            along_z(dz).start()
        yield
        second(0, 0).wait_recv()
        first(0).wait_recv()
        for dz in (1, 2, 3):
            along_z(dz).wait_recv()
        total = scratch[8] if self.pair else out
        more = [from_b.at[0], from_a.at[0]] + [from_z.at[dz] for dz in (1, 2, 3)]
        settle((0, 0, 0), more, total)
        if self.pair:
            rows, width = self.blocks.shape
            half = rows // 2
            columns = span(core, width)
            swap = remote(
                total.at[span(1 - core, half), :], out.at[:, columns],
                scratch[9].at[0], scratch[9].at[1], at.sibling(),
            )
            swap.start()
            out[:, columns] = total[span(core, half), :]
        yield "last"
        if self.pair:
            swap.wait()
        for slot in range(16):
            across(slot).wait_send()
        for dz in range(4):
            for da in range(2):
                second(da, dz).wait_send()
            first(dz).wait_send()
            if dz:
                along_z(dz).wait_send()


def later(part, steps=2):
    part.wait = steps
    return part


def staged(part, *refs):
    for _ in range(getattr(part, "wait", 0)):
        yield
    yield from part.run(*refs)


def exchange(name, collective, parts, vmem=4):
    sizes = [(len(p.arrays), len(p.outs), len(p.scratch)) for p in parts]
    n_in = sum(size[0] for size in sizes)
    n_out = sum(size[1] for size in sizes)

    def kernel(*refs):
        at = Place()
        barrier = pltpu.get_barrier_semaphore()
        near = [(at.grp, lax.rem(at.key + k, 2 * LOCAL)) for k in range(1, 2 * LOCAL)]
        near += [at.device(1, 0, 0), at.device(0, 1, 0)]
        for device in near:
            pl.semaphore_signal(barrier, inc=1, device_id=device, device_id_type=MESH)
        pl.semaphore_wait(barrier, len(near))
        ins, outs, scratch = refs[:n_in], refs[n_in : n_in + n_out], refs[n_in + n_out :]
        live = []
        sums = any(isinstance(part, Scatter) for part in parts)
        for part, (i, o, s) in zip(parts, sizes):
            live.append(staged(part, at, ins[:i], outs[:o], scratch[:s]))
            ins, outs, scratch = ins[i:], outs[o:], scratch[s:]
        for stage in live:
            next(stage)
        ending = []
        while live:
            for stage in list(reversed(live) if sums else live):
                if next(stage) == "last":
                    live.remove(stage)
                    ending.append(stage)
        for stage in ending:
            for _ in stage:
                pass

    outs = pl.pallas_call(
        kernel,
        name=name,
        out_shape=[o for p in parts for o in p.outs],
        in_specs=[ANY] * n_in,
        out_specs=[o for p in parts for o in p.out_specs],
        scratch_shapes=[s for p in parts for s in p.scratch],
        compiler_params=pltpu.CompilerParams(
            collective_id=collective, has_side_effects=True, vmem_limit_bytes=vmem * 2**20
        ),
    )(*[a for p in parts for a in p.arrays])
    outs = list(outs)
    return [[outs.pop(0) for _ in p.outs] for p in parts]


def hop(values, change):
    pairs = []
    for y in range(2):
        for x in range(2):
            for z in range(LOCAL):
                for core in range(2):
                    to = [y, x, z, core]
                    if change in ("a", "b"):
                        to[1 if (change == "a") == (core == 0) else 0] ^= 1
                    elif change == "core":
                        to[3] ^= 1
                    else:
                        to[2] ^= change
                    number = [((v[0] * 2 + v[1]) * LOCAL + v[2]) * 2 + v[3] for v in ([y, x, z, core], to)]
                    pairs.append(tuple(number))
    return lax.ppermute(values, ("grp", "key"), pairs)


def column_hop(values, pairs):
    size = 2 * LOCAL
    every = [(g * size + s, g * size + t) for g in range(4) for s, t in pairs]
    return lax.ppermute(values, ("grp", "key"), every)


def join(value, others):
    return lax.optimization_barrier((value, others))


def gather_column(shard):
    return jnp.stack([shard] + [hop(shard, dz) for dz in (1, 2, 3)])


def add(*terms):
    return sum(term.astype(F32) for term in terms)


def scatter_second(sums):
    here, first, second = sums
    return here, first, hop(second, "b")


def scatter_first(sums):
    here, first, got = sums
    return here, got, hop(add(first, got[4:]).astype(BF), "a")


def scatter_z(sums):
    here, got, more = sums
    total = add(here, got[:4], more)
    low = total[1:].astype(BF)
    return [total[0]] + [hop(low[dz - 1], dz) for dz in (1, 2, 3)]


def scatter_end(sums):
    return add(*sums)


def rows_hops(chunks):
    odd = lax.rem(lax.axis_index("key"), 2) == 1
    size = 2 * LOCAL
    same = [(j, j // 2 + LOCAL * (j % 2)) for j in range(size)]
    cross = [(j, j // 2 + LOCAL * (1 - j % 2)) for j in range(size)]
    one = column_hop(jnp.where(odd, chunks[1], chunks[0]), same)
    two = column_hop(jnp.where(odd, chunks[0], chunks[1]), cross)
    upper = lax.axis_index("key") >= LOCAL
    return jnp.concatenate((jnp.where(upper, two, one), jnp.where(upper, one, two)))


def chunk_hops(rows):
    half = rows.shape[0] // 2
    odd = lax.rem(lax.axis_index("key"), 2) == 1
    upper = lax.axis_index("key") >= LOCAL
    size = 2 * LOCAL
    same = [(j // 2 + LOCAL * (j % 2), j) for j in range(size)]
    cross = [(j // 2 + LOCAL * (1 - j % 2), j) for j in range(size)]
    one = column_hop(jnp.where(upper, rows[half:], rows[:half]), same)
    two = column_hop(jnp.where(upper, rows[:half], rows[half:]), cross)
    return jnp.stack((jnp.where(odd, two, one), jnp.where(odd, one, two)))


def dot_nt(a, b):
    return lax.dot_general(a, b, (((1,), (1,)), ((), ())), preferred_element_type=F32)


def dot_nn(a, b):
    return lax.dot_general(a, b, (((1,), (0,)), ((), ())), preferred_element_type=F32)


def heads(index):
    return pl.ds(index * HEAD, HEAD)


def block_rows(j):
    return pl.ds(pl.multiple_of(j * BLOCK, BLOCK), BLOCK)


def transpose_blocks(src, dst):
    @pl.loop(0, src.shape[0] // BLOCK)
    def _(j):
        dst[j] = src[block_rows(j), :].astype(F32).T.astype(BF)


def visible(bounds, low, high, j):
    at = lax.broadcasted_iota(jnp.int32, (BLOCK, QUERIES), 0)
    start = j * BLOCK
    return (at >= bounds[low : low + 1, :] - start) & (at < bounds[high : high + 1, :] - start)


def fold(values):
    return values.reshape(values.shape[0] // 8, 8, values.shape[1])


def each_block(ranges, i, with_memory, local_body, memory_body):
    begin, full, diagonal, end = (ranges[i, k] for k in range(4))
    lax.fori_loop(begin, full, local_body(True), 0)
    lax.fori_loop(full, diagonal, local_body(False), 0)
    lax.fori_loop(diagonal, end, local_body(True), 0)
    if with_memory:
        begin, full, rest, end = (ranges[i, k] for k in range(4, 8))
        lax.fori_loop(begin, full, memory_body(True), 0)
        lax.fori_loop(full, rest, memory_body(False), 0)
        lax.fori_loop(rest, end, memory_body(True), 0)


def attend_kernel(with_memory, ranges, *refs):
    if with_memory:
        q, k, v, bounds, mk, mv, out, stat, vt, mvt, scores, acc, top, total = refs
    else:
        q, k, v, bounds, out, stat, vt, scores, acc, top, total = refs
        mk = mvt = None
    i = pl.program_id(0)
    scale = HEAD ** (-0.5) * LOG2E
    blocks = vt.shape[0]

    @pl.when(i == 0)
    def _():
        transpose_blocks(v, vt)
        if with_memory:
            transpose_blocks(mv, mvt)

    acc[...] = jnp.zeros_like(acc)
    top[...] = jnp.full_like(top, NEG)
    total[...] = jnp.zeros_like(total)

    def scan(keys, first, low):
        def run(masked):
            def body(j, _):
                for h in range(2):
                    part = dot_nt(keys[block_rows(j), heads(h)], q[:, heads(h)])
                    if masked:
                        part = jnp.where(visible(bounds, low, low + 1, j), part, NEG)
                    scores[h, first + j] = part
                    top[h] = jnp.maximum(top[h], jnp.max(fold(part), axis=0))
                return 0

            return body

        return run

    each_block(ranges, i, with_memory, scan(k, 0, 0), scan(mk, blocks, 2))
    tops = [jnp.max(top[h], axis=0, keepdims=True) * scale for h in range(2)]

    def take(values_t, first):
        def run(masked):
            def body(j, _):
                for h in range(2):
                    probs = jnp.exp2(scores[h, first + j] * scale - tops[h])
                    total[h] += jnp.sum(fold(probs), axis=0)
                    acc[heads(h), :] += dot_nn(values_t[j, heads(h), :], probs.astype(BF))
                return 0

            return body

        return run

    lax.fori_loop(ranges[i, 0], ranges[i, 3], take(vt, 0)(False), 0)
    if with_memory:
        lax.fori_loop(ranges[i, 4], ranges[i, 7], take(mvt, blocks)(False), 0)
    for h in range(2):
        share = jnp.sum(total[h], axis=0, keepdims=True)
        out[:, heads(h)] = (acc[heads(h), :] / share).T.astype(BF)
        stat[h : h + 1, :] = tops[h] + jnp.log2(share)
    stat[2:, :] = jnp.zeros_like(stat[2:, :])


def attend(q, k, v, memory, bounds, ranges):
    rows = q.shape[0]
    blocks = rows // BLOCK
    row_block = pl.BlockSpec((QUERIES, PAIR), lambda i, *_: (i, 0))
    lane_block = pl.BlockSpec((8, QUERIES), lambda i, *_: (0, i))
    operands = [q, k, v, bounds]
    in_specs = [row_block, VMEM, VMEM, lane_block]
    scratch = [pltpu.VMEM((blocks, PAIR, BLOCK), BF)]
    if memory is not None:
        operands += [memory[0], memory[1]]
        in_specs += [VMEM, VMEM]
        more = memory[1].shape[0] // BLOCK
        scratch += [pltpu.VMEM((more, PAIR, BLOCK), BF)]
        blocks += more
    return pl.pallas_call(
        functools.partial(attend_kernel, memory is not None),
        name="attend",
        grid_spec=pltpu.PrefetchScalarGridSpec(
            num_scalar_prefetch=1,
            grid=(rows // QUERIES,),
            in_specs=in_specs,
            out_specs=(row_block, lane_block),
            scratch_shapes=scratch
            + [
                pltpu.VMEM((2, blocks, BLOCK, QUERIES), F32),
                pltpu.VMEM((PAIR, QUERIES), F32),
                pltpu.VMEM((2, 8, QUERIES), F32),
                pltpu.VMEM((2, 8, QUERIES), F32),
            ],
        ),
        out_shape=(
            jax.ShapeDtypeStruct((rows, PAIR), BF),
            jax.ShapeDtypeStruct((8, rows), F32),
        ),
        compiler_params=pltpu.CompilerParams(vmem_limit_bytes=48 * 2**20),
    )(ranges, *operands)


def attend_back_kernel(with_memory, ranges, *refs):
    if with_memory:
        (q, go, o, stat, bounds, k, v, mk, mv, gq, gk, gv, kt, mkt, delta, gq_t, gk_sum, gv_sum) = refs
    else:
        (q, go, o, stat, bounds, k, v, gq, gk, gv, kt, delta, gq_t, gk_sum, gv_sum) = refs
        mk = mv = mkt = None
    i = pl.program_id(0)
    unit = HEAD ** (-0.5)
    scale = unit * LOG2E

    @pl.when(i == 0)
    def _():
        transpose_blocks(k, kt)
        gk_sum[...] = jnp.zeros_like(gk_sum)
        gv_sum[...] = jnp.zeros_like(gv_sum)
        if with_memory:
            transpose_blocks(mk, mkt)

    for h in range(2):
        both = go[:, heads(h)].astype(F32) * o[:, heads(h)].astype(F32)
        delta[h : h + 1, :] = jnp.sum(both.T, axis=0, keepdims=True)
    gq_t[...] = jnp.zeros_like(gq_t)

    def step(keys, values, keys_t, low, own):
        def run(masked):
            def body(j, _):
                for h in range(2):
                    query, grad = q[:, heads(h)], go[:, heads(h)]
                    scores = dot_nt(keys[block_rows(j), heads(h)], query) * scale
                    probs = jnp.exp2(scores - stat[h : h + 1, :])
                    if masked:
                        probs = jnp.where(visible(bounds, low, low + 1, j), probs, 0.0)
                    grad_probs = dot_nt(values[block_rows(j), heads(h)], grad)
                    grad_scores = (probs * (grad_probs - delta[h : h + 1, :])).astype(BF)
                    gq_t[heads(h), :] += dot_nn(keys_t[j, heads(h), :], grad_scores)
                    if own:
                        gv_sum[block_rows(j), heads(h)] += dot_nn(probs.astype(BF), grad)
                        gk_sum[block_rows(j), heads(h)] += dot_nn(grad_scores, query)
                return 0

            return body

        return run

    each_block(ranges, i, with_memory, step(k, v, kt, 0, True), step(mk, mv, mkt, 2, False))
    gq[...] = (gq_t[...] * unit).T.astype(BF)

    @pl.when(i == pl.num_programs(0) - 1)
    def _():
        gk[...] = (gk_sum[...] * unit).astype(BF)
        gv[...] = gv_sum[...].astype(BF)


def attend_back(q, k, v, memory, bounds, ranges, out, stat, grad):
    rows = q.shape[0]
    blocks = rows // BLOCK
    row_block = pl.BlockSpec((QUERIES, PAIR), lambda i, *_: (i, 0))
    lane_block = pl.BlockSpec((8, QUERIES), lambda i, *_: (0, i))
    operands = [q, grad, out, stat, bounds, k, v]
    in_specs = [row_block, row_block, row_block, lane_block, lane_block, VMEM, VMEM]
    scratch = [pltpu.VMEM((blocks, PAIR, BLOCK), BF)]
    if memory is not None:
        operands += [memory[0], memory[1]]
        in_specs += [VMEM, VMEM]
        scratch += [pltpu.VMEM((memory[0].shape[0] // BLOCK, PAIR, BLOCK), BF)]
    whole = jax.ShapeDtypeStruct((rows, PAIR), BF)
    return pl.pallas_call(
        functools.partial(attend_back_kernel, memory is not None),
        name="attend_back",
        grid_spec=pltpu.PrefetchScalarGridSpec(
            num_scalar_prefetch=1,
            grid=(rows // QUERIES,),
            in_specs=in_specs,
            out_specs=(row_block, VMEM, VMEM),
            scratch_shapes=scratch
            + [
                pltpu.VMEM((8, QUERIES), F32),
                pltpu.VMEM((PAIR, QUERIES), F32),
                pltpu.VMEM((rows, PAIR), F32),
                pltpu.VMEM((rows, PAIR), F32),
            ],
        ),
        out_shape=(whole, whole, whole),
        compiler_params=pltpu.CompilerParams(vmem_limit_bytes=48 * 2**20),
    )(ranges, *operands)


NUMBERS = 8


def members(docs):
    number = jnp.arange(NUMBERS, dtype=jnp.int32)
    return (docs[None, :] == number[:, None]).astype(jnp.int32)


def before(counts):
    at = jnp.arange(counts.shape[-1])
    earlier = at[:, None] < at[None, :]
    return jnp.sum(jnp.where(earlier, counts[..., :, None], 0), axis=-2)


def pick(which, table):
    return jnp.sum(which * table[:, None], axis=0)


def mask_ranges(docs, mem_docs, reset):
    rows = docs.shape[0]
    at = jnp.arange(rows, dtype=jnp.int32)
    own, other = members(docs), members(mem_docs)
    start = pick(own, before(jnp.sum(own, axis=1)))
    counts = jnp.where(reset == 0, jnp.sum(other, axis=1), 0)
    mem_low = pick(own, before(counts))
    mem_high = mem_low + pick(own, counts)
    zero = jnp.zeros_like(start)
    bounds = jnp.stack((start, at + 1, mem_low, mem_high, zero, zero, zero, zero))

    def per_block(values):
        return values.reshape(rows // QUERIES, QUERIES)

    def up(values):
        return (values + BLOCK - 1) // BLOCK

    step = QUERIES // BLOCK
    diagonal = jnp.arange(rows // QUERIES, dtype=jnp.int32) * step
    first = jnp.min(per_block(start), axis=1) // BLOCK
    full = jnp.clip(up(jnp.max(per_block(start), axis=1)), first, diagonal)
    some = mem_high > mem_low
    mem_first = jnp.min(per_block(jnp.where(some, mem_low, mem_docs.shape[0])), axis=1) // BLOCK
    mem_end = jnp.maximum(up(jnp.max(per_block(mem_high), axis=1)), mem_first)
    mem_full = jnp.clip(up(jnp.max(per_block(mem_low), axis=1)), mem_first, mem_end)
    mem_rest = jnp.clip(jnp.min(per_block(mem_high), axis=1) // BLOCK, mem_full, mem_end)
    columns = (first, full, diagonal, diagonal + step, mem_first, mem_full, mem_rest, mem_end)
    return bounds, jnp.stack(columns, axis=1)


def sort_memory(memory, mem_docs):
    entries = mem_docs.shape[0]
    which = members(mem_docs)
    lanes = which.reshape(-1, HEAD)
    at = jnp.arange(HEAD)
    earlier = (at[:, None] < at[None, :]).astype(BF)
    inside = jnp.dot(lanes.astype(BF), earlier, preferred_element_type=F32).astype(jnp.int32)
    totals = jnp.sum(lanes, axis=1).reshape(NUMBERS, -1)
    first = before(jnp.sum(totals, axis=1))[:, None] + before(totals)
    rank = inside.reshape(NUMBERS, -1, HEAD) + first[:, :, None]
    rank = jnp.sum(which * rank.reshape(NUMBERS, entries), axis=0)
    moved = (rank[None, :] == jnp.arange(entries, dtype=jnp.int32)[:, None]).astype(BF)
    return tuple(
        jnp.dot(moved, memory[index], preferred_element_type=F32).astype(BF) for index in range(2)
    )


def columns(matrix, sizes):
    pieces, at = [], 0
    for size in sizes:
        pieces.append(matrix[:, at : at + size])
        at += size
    return pieces


def dot_tn(a, b):
    return lax.dot_general(a, b, (((0,), (0,)), ((), ())), preferred_element_type=F32)


def norm_rows(values, gain):
    inverse = lax.rsqrt(jnp.mean(values * values, axis=-1, keepdims=True) + EPS)
    return (values * inverse * gain).astype(BF), inverse


def norm_rows_back(values, gain, inverse, grad):
    grad_gain = jnp.sum(grad * values * inverse, axis=0)
    scaled = grad * gain
    mean = jnp.mean(scaled * values, axis=-1, keepdims=True)
    return inverse * scaled - values * inverse**3 * mean, grad_gain


def layer(stream, qkv_w, gains, steps, memory, bounds, ranges):
    gain_a, gain_b = gains
    normed, inverse_a = norm_rows(stream, gain_a)
    qkv = jnp.dot(normed, qkv_w, preferred_element_type=F32).astype(BF)
    q, k, v = steps[0](qkv)
    out, stat = attend(q, k, v, memory() if memory else None, bounds, ranges)
    attended, out_w, gate_up_w, down_w = steps[1](out)
    ff = down_w.shape[0]
    mixed = stream + jnp.dot(attended, out_w, preferred_element_type=F32)
    normed_ff, inverse_b = norm_rows(mixed, gain_b)
    gate_up = jnp.dot(normed_ff, gate_up_w, preferred_element_type=F32)
    gate, up = gate_up[:, :ff], gate_up[:, ff:]
    activated = (gate * jax.nn.sigmoid(gate) * up).astype(BF)
    result = mixed + jnp.dot(activated, down_w, preferred_element_type=F32)
    weights = (gain_a, qkv_w, out_w, gain_b, gate_up_w, down_w)
    kept = (stream, inverse_a, normed, q, k, v, out, stat, attended, mixed, inverse_b, normed_ff, gate, up, activated)
    return result, weights, kept


def ffn_back(grad_new, weights, kept):
    gain_a, qkv_w, out_w, gain_b, gate_up_w, down_w = weights
    attended, mixed, inverse_b, normed_ff, gate, up, activated = kept[8:]
    branch = grad_new.astype(BF)
    grad_down = dot_tn(activated, branch).astype(BF)
    grad_act = dot_nt(branch, down_w)
    sig = jax.nn.sigmoid(gate)
    grad_gate = (grad_act * up * sig * (1.0 + gate * (1.0 - sig))).astype(BF)
    grad_up = (grad_act * gate * sig).astype(BF)
    grad_gate_up = jnp.concatenate((grad_gate, grad_up), axis=1)
    grad_gate_up_w = dot_tn(normed_ff, grad_gate_up).astype(BF)
    grad_normed_ff = dot_nt(grad_gate_up, gate_up_w)
    back, grad_gain_b = norm_rows_back(mixed, gain_b, inverse_b, grad_normed_ff)
    grad_mixed = grad_new + back
    attn = grad_mixed.astype(BF)
    grad_out_w = dot_tn(attended, attn).astype(BF)
    grad_attended = dot_nt(attn, out_w).astype(BF)
    return grad_mixed, grad_attended, grad_out_w, grad_gain_b, grad_gate_up_w, grad_down


def projections_back(grad_mixed, grad_qkv, weights, kept):
    gain_a, qkv_w = weights[:2]
    stream, inverse_a, normed = kept[:3]
    grad_qkv_w = dot_tn(normed, grad_qkv).astype(BF)
    grad_normed = dot_nt(grad_qkv, qkv_w)
    back, grad_gain_a = norm_rows_back(stream, gain_a, inverse_a, grad_normed)
    return grad_mixed + back, grad_gain_a, grad_qkv_w


def gain_columns(gains):
    stacked = jnp.stack(gains, axis=1)
    return jnp.pad(stacked, ((0, 0), (0, HEAD - len(gains))))


def pair_rows(own, other, core):
    rows, width = own.shape
    both = jnp.where(core == 0, jnp.stack((own, other)), jnp.stack((other, own)))
    return lax.dynamic_slice_in_dim(both.reshape(2 * rows, width), core * (width // 2), width // 2, 1)


def head_local(
    tokens, token_docs, memory_docs, memory_resets, memory_keys, memory_values,
    attn_gain1, query_weight1, key_weight1, value_weight1, out_weight1,
    ffn_gain1, gate_weight1, up_weight1, down_weight1,
    attn_gain2, second_query_weight, key_weight2, value_weight2, out_weight2,
    ffn_gain2, gate_weight2, up_weight2, down_weight2, cotangent,
):
    count, width = query_weight1.shape
    ff = gate_weight1.shape[1]
    each = down_weight1.shape[0]
    core = lax.rem(lax.axis_index("key"), 2)
    seg = lax.axis_index("key") // LOCAL
    gains = gain_columns((attn_gain1, ffn_gain1, attn_gain2, ffn_gain2))
    qkv1 = jnp.concatenate((query_weight1, key_weight1, value_weight1), axis=1)
    qkv2 = jnp.concatenate((second_query_weight, key_weight2, value_weight2), axis=1)
    gate_up1 = jnp.concatenate((gate_weight1, up_weight1), axis=1)
    gate_up2 = jnp.concatenate((gate_weight2, up_weight2), axis=1)
    downs = jnp.concatenate((down_weight1, down_weight2), axis=0)
    docs = jnp.concatenate((token_docs, memory_docs), axis=0)
    pairs = PairBlocks(2 * each, width // 2)

    def own(matrix):
        return RowBlocks(count, matrix.shape[1])

    def gather(matrix):
        return Gather(matrix, own(matrix))

    (rows,), (docs,), (other,), (qkv1_w,), (gains,) = exchange(
        "bring_tokens", 1,
        [later(Rows(tokens)), Docs(docs), Sibling(downs), gather(qkv1), gather(gains)],
    )
    down1 = pair_rows(down_weight1, other[:each], core)
    down2 = pair_rows(down_weight2, other[each:], core)
    own_docs = lax.dynamic_index_in_dim(docs, seg, 0, keepdims=False)
    own_mem_docs = lax.dynamic_index_in_dim(docs, seg + 2, 0, keepdims=False)
    reset = lax.dynamic_index_in_dim(memory_resets, seg, 0, keepdims=False)
    bounds, ranges = mask_ranges(own_docs, own_mem_docs, reset)
    gains = gains[:, :4].astype(F32)
    held = {}

    hops = {}
    rest2 = jnp.concatenate((gate_up2, out_weight2), axis=1)

    def heads1(qkv):
        swapped, (mk,), (mv,), (held["gu1"],), (held["down1"],), (held["out1"],), (held["qkv2"],) = exchange(
            "to_heads_1", 2,
            [later(Swap([qkv], True)), later(Memory(memory_keys), 3), later(Memory(memory_values), 3),
             gather(gate_up1), Gather(down1, pairs), gather(out_weight1), gather(qkv2)],
        )
        held["memory"] = mk, mv
        swapped, shards = join(swapped, (rest2, down2))
        hops["rest"] = [gather_column(shard) for shard in shards]
        return swapped

    def rows1(out):
        ((attended,),) = exchange("to_rows_1", 3, [Swap([out], False)])
        return attended, held["out1"], held["gu1"], held["down1"]

    def heads2(qkv):
        held["memory"] = sort_memory(held["memory"], own_mem_docs)
        (swapped,) = exchange("to_heads_2", 4, [Swap([qkv], True)])
        swapped, firsts = join(swapped, [group[1] for group in hops["rest"]])
        hops["rest"] = [
            (group[0], first, group[2], hop(first, "b"))
            for group, first in zip(hops["rest"], firsts)
        ]
        return swapped

    def rows2(out):
        out, (rest, down) = join(out, hops["rest"])
        (attended,), (gate_up_w, out_w), (down_w,) = exchange(
            "to_rows_2", 5,
            [Swap([out], False), Assemble(rest, [RowBlocks(count, 2 * ff), RowBlocks(count, width)]),
             Assemble(down, [pairs])],
        )
        attended, cot = join(attended, cotangent)
        hops["cot"] = rows_hops(cot)
        return attended, out_w, gate_up_w, down_w

    middle, weights1, kept1 = layer(
        rows.astype(F32), qkv1_w, (gains[:, 0], gains[:, 1]), (heads1, rows1), None, bounds, ranges
    )
    middle, rest = join(middle, hops["rest"])
    hops["rest"] = [(column, hop(column, "a"), hop(column, "b")) for column in rest]
    qkv2_w = held["qkv2"]
    result, weights2, kept2 = layer(
        middle, qkv2_w, (gains[:, 2], gains[:, 3]), (heads2, rows2),
        lambda: held["memory"], bounds, ranges,
    )
    cot = hops["cot"]
    output = chunk_hops(result.astype(BF))

    def pair_sum(total):
        half = lax.dynamic_slice_in_dim(total, core * each, each, 0)
        other = hop(lax.dynamic_slice_in_dim(total, (1 - core) * each, each, 0), "core")
        return jnp.where(
            core == 0, jnp.concatenate((half, other), 1), jnp.concatenate((other, half), 1)
        )

    shapes = ((count, 2 * ff), (count, width), pairs.shape)

    def feed_sums(out_g, gate_up_g, down_g):
        return CoreSums((gate_up_g, own(gate_up_g)), (out_g, own(out_g)), (down_g, pairs))

    grad_mixed, grad_att, out_g2, gain_b2, gate_up_g2, down_g2 = ffn_back(
        cot.astype(F32), weights2, kept2
    )
    (grad_out,), sums2 = exchange(
        "back_to_heads_2", 6,
        [Swap([grad_att], True), feed_sums(out_g2, gate_up_g2, down_g2)],
        48,
    )
    sums2 = scatter_second(sums2)
    q, k, v, out, stat = kept2[3:8]
    grads = attend_back(q, k, v, held["memory"], bounds, ranges, out, stat, grad_out)
    ((grad_qkv,),) = exchange("back_to_rows_2", 7, [Swap(list(grads), False)])
    grad_qkv, (sums2, output) = join(grad_qkv, (sums2, output))
    sums2 = scatter_first(sums2)
    grad_middle, gain_a2, qkv_g2 = projections_back(grad_mixed, grad_qkv, weights2, kept2)
    (qkv_s2,) = exchange("projection_sums_2", 12, [CoreSums((qkv_g2, own(qkv_g2)))], 24)
    grad_middle, (sums2, qkv_s2) = join(grad_middle, (sums2, qkv_s2))
    sums2 = scatter_z(sums2)
    qkv_s2 = scatter_second(qkv_s2)

    grad_mixed, grad_att, out_g1, gain_b1, gate_up_g1, down_g1 = ffn_back(
        grad_middle, weights1, kept1
    )
    grad_att, qkv_s2 = join(grad_att, qkv_s2)
    qkv_s2 = scatter_first(qkv_s2)
    (grad_out,), sums1 = exchange(
        "back_to_heads_1", 8,
        [Swap([grad_att], True), feed_sums(out_g1, gate_up_g1, down_g1)],
        48,
    )
    grad_out, (sums2, qkv_s2) = join(grad_out, (sums2, qkv_s2))
    qkv_s2 = scatter_z(qkv_s2)
    sums1 = scatter_second(sums1)
    q, k, v, out, stat = kept1[3:8]
    grads = attend_back(q, k, v, None, bounds, ranges, out, stat, grad_out)
    ((grad_qkv,),) = exchange("back_to_rows_1", 9, [Swap(list(grads), False)])
    grad_qkv, (sums1, qkv_s2) = join(grad_qkv, (sums1, qkv_s2))
    sums1 = scatter_first(sums1)
    grad_rows, gain_a1, qkv_g1 = projections_back(grad_mixed, grad_qkv, weights1, kept1)
    gain_grads = gain_columns((gain_a1, gain_b1, gain_a2, gain_b2)).astype(BF)
    grad_rows, sums1 = join(grad_rows, sums1)
    sums1 = scatter_z(sums1)
    (grad_tokens,), (q_s1,), (k_s1,), (v_s1,), (gain_s,) = exchange(
        "back_to_owners", 10,
        [Chunks(grad_rows.astype(BF))]
        + [Scatter(qkv_g1, ColumnBlocks(count, width, i), i) for i in range(3)]
        + [Scatter(gain_grads, own(gain_grads), 2)],
        40,
    )
    gate_up_s2, out_s2, down_s2 = unpack(scatter_end(sums2), shapes)
    gate_up_s1, out_s1, down_s1 = unpack(scatter_end(sums1), shapes)
    (qkv_s2,) = unpack(scatter_end(qkv_s2), ((count, 3 * width),))
    q_s2, k_s2, v_s2 = columns(qkv_s2, (width,) * 3)
    gate_s1, up_s1 = columns(gate_up_s1, (ff, ff))
    gate_s2, up_s2 = columns(gate_up_s2, (ff, ff))
    return (
        output, grad_tokens.astype(F32),
        gain_s[:, 0], q_s1, k_s1, v_s1, out_s1, gain_s[:, 1], gate_s1, up_s1, pair_sum(down_s1),
        gain_s[:, 2], q_s2, k_s2, v_s2, out_s2, gain_s[:, 3], gate_s2, up_s2, pair_sum(down_s2),
    )


def solution(mesh):
    in_specs = (
        P("grp", "key", None),
        P("grp", "key"),
        P("grp", "key"),
        P("grp"),
        P("grp", "key", None),
        P("grp", "key", None),
        P(("grp", "key")),
        P(("grp", "key"), None),
        P(("grp", "key"), None),
        P(("grp", "key"), None),
        P(("grp", "key"), None),
        P(("grp", "key")),
        P(("grp", "key"), None),
        P(("grp", "key"), None),
        P(("grp", "key"), None),
        P(("grp", "key")),
        P(("grp", "key"), None),
        P(("grp", "key"), None),
        P(("grp", "key"), None),
        P(("grp", "key"), None),
        P(("grp", "key")),
        P(("grp", "key"), None),
        P(("grp", "key"), None),
        P(("grp", "key"), None),
        P("grp", "key", None),
    )
    out_specs = (
        P("grp", "key", None),
        P("grp", "key", None),
        P(("grp", "key")),
        P(("grp", "key"), None),
        P(("grp", "key"), None),
        P(("grp", "key"), None),
        P(("grp", "key"), None),
        P(("grp", "key")),
        P(("grp", "key"), None),
        P(("grp", "key"), None),
        P(("grp", "key"), None),
        P(("grp", "key")),
        P(("grp", "key"), None),
        P(("grp", "key"), None),
        P(("grp", "key"), None),
        P(("grp", "key"), None),
        P(("grp", "key")),
        P(("grp", "key"), None),
        P(("grp", "key"), None),
        P(("grp", "key"), None),
    )
    body = head_local if dict(mesh.shape) == {"grp": 4, "key": HEADS} else gathered_local
    return jax.shard_map(body, mesh=mesh, in_specs=in_specs, out_specs=out_specs, check_vma=False)
```

```python
import functools

import jax
import jax.numpy as jnp
from jax import lax
from jax.experimental import pallas as pl
from jax.experimental.pallas import tpu as pltpu
from jax.sharding import PartitionSpec as P

HEADS = 8


EPS = 1e-05
NEG = -1e30


def norm_forward(values, gain_vec):
    inverse = lax.rsqrt(jnp.mean(values * values, axis=-1, keepdims=True) + EPS)
    return (values * inverse * gain_vec, inverse)


def norm_backward(values, gain_vec, inverse, grad_normed):
    grad_gain = jnp.sum(grad_normed * values * inverse, axis=(0, 1))
    scaled = grad_normed * gain_vec
    grad_values = inverse * scaled - values * inverse**3 * jnp.mean(
        scaled * values, axis=-1, keepdims=True
    )
    return (grad_values, grad_gain)


def project(input_operand, weight_matrix):
    return jnp.dot(input_operand, weight_matrix, preferred_element_type=jnp.float32)


def project_back(gradient_row_block, weight_matrix):
    return jnp.einsum(
        "tzu,ku->tzk", gradient_row_block, weight_matrix, preferred_element_type=jnp.float32
    )


def outer_sum(input_arrays, gradient_reduced_precision):
    return jnp.einsum(
        "zhp,zhv->pv", input_arrays, gradient_reduced_precision, preferred_element_type=jnp.float32
    )


def split_heads(rows):
    return rows.reshape(rows.shape[0], rows.shape[1], HEADS, rows.shape[2] // HEADS)


def fetch_weights(shards):
    return (
        lax.all_gather(shards[0], ("grp", "key"), axis=0, tiled=True),
        lax.all_gather(shards[1], ("grp", "key"), axis=0, tiled=True),
        lax.all_gather(shards[2], ("grp", "key"), axis=0, tiled=True),
        lax.all_gather(shards[3], ("grp", "key"), axis=0, tiled=True),
        lax.all_gather(shards[4], ("grp", "key"), axis=0, tiled=True),
        lax.all_gather(shards[5], ("grp", "key"), axis=0, tiled=True),
        lax.all_gather(shards[6], ("grp", "key"), axis=0, tiled=True),
        lax.all_gather(shards[7], ("grp", "key"), axis=0, tiled=True),
        lax.all_gather(shards[8], ("grp", "key"), axis=0, tiled=True),
    )


def refetch_weights(shards):
    return (
        lax.all_gather(shards[0], ("grp", "key"), axis=0, tiled=True),
        lax.all_gather(shards[1], ("grp", "key"), axis=0, tiled=True),
        lax.all_gather(shards[2], ("grp", "key"), axis=0, tiled=True),
        lax.all_gather(shards[3], ("grp", "key"), axis=0, tiled=True),
        lax.all_gather(shards[4], ("grp", "key"), axis=0, tiled=True),
        lax.all_gather(shards[5], ("grp", "key"), axis=0, tiled=True),
        lax.all_gather(shards[6], ("grp", "key"), axis=0, tiled=True),
        lax.all_gather(shards[7], ("grp", "key"), axis=0, tiled=True),
        lax.all_gather(shards[8], ("grp", "key"), axis=0, tiled=True),
    )


def reduce_gradient_sums(terms):
    return (
        lax.psum_scatter(terms[0], ("grp", "key"), scatter_dimension=0, tiled=True),
        lax.psum_scatter(terms[1], ("grp", "key"), scatter_dimension=0, tiled=True),
        lax.psum_scatter(terms[2], ("grp", "key"), scatter_dimension=0, tiled=True),
        lax.psum_scatter(terms[3], ("grp", "key"), scatter_dimension=0, tiled=True),
        lax.psum_scatter(terms[4], ("grp", "key"), scatter_dimension=0, tiled=True),
        lax.psum_scatter(terms[5], ("grp", "key"), scatter_dimension=0, tiled=True),
        lax.psum_scatter(terms[6], ("grp", "key"), scatter_dimension=0, tiled=True),
        lax.psum_scatter(terms[7], ("grp", "key"), scatter_dimension=0, tiled=True),
        lax.psum_scatter(terms[8], ("grp", "key"), scatter_dimension=0, tiled=True),
    )


def head_scores(query_all, key_block, allowed):
    head_size = query_all.shape[2] // HEADS
    raw_scores = jnp.einsum(
        "sqhd,skhd->shqk",
        split_heads(query_all),
        split_heads(key_block),
        preferred_element_type=jnp.float32,
    ) * head_size ** (-0.5)
    return jnp.where(allowed[:, None], raw_scores, NEG)


def attend_forward(query_all, key_block, value_block, allowed):
    scores = head_scores(query_all, key_block, allowed)
    row_top = lax.pmax(jnp.max(scores, axis=3).astype(jnp.bfloat16), "key").astype(jnp.float32)
    exp_scores = jnp.where(allowed[:, None], jnp.exp(scores - row_top[..., None]), 0.0)
    row_total = lax.psum(jnp.sum(exp_scores, axis=3).astype(jnp.bfloat16), "key").astype(
        jnp.float32
    )
    probability = exp_scores / row_total[..., None]
    partial_value = jnp.einsum(
        "shqk,skhd->sqhd",
        probability.astype(jnp.bfloat16),
        split_heads(value_block),
        preferred_element_type=jnp.float32,
    )
    partial_value = partial_value.reshape(query_all.shape)
    attended = lax.psum_scatter(
        partial_value.astype(jnp.bfloat16), "key", scatter_dimension=1, tiled=True
    ).astype(jnp.float32)
    return (attended, row_top, row_total)


def layer_forward(stream, full_weights, allowed, extra_keys, extra_values):
    gain_a, query_w, key_w, value_w, out_w, gain_b, gate_w, up_w, down_w = full_weights
    normed, first_inverse_factor = norm_forward(stream, gain_a.astype(jnp.float32))
    normed_low = normed.astype(jnp.bfloat16)
    query_low = project(normed_low, query_w).astype(jnp.bfloat16)
    key_low = project(normed_low, key_w).astype(jnp.bfloat16)
    value_low = project(normed_low, value_w).astype(jnp.bfloat16)
    query_all = lax.all_gather(query_low, "key", axis=1, tiled=True)
    if extra_keys is None:
        key_block = key_low
        value_block = value_low
    else:
        key_block = jnp.concatenate((key_low, extra_keys), axis=1)
        value_block = jnp.concatenate((value_low, extra_values), axis=1)
    attended, row_top, row_total = attend_forward(query_all, key_block, value_block, allowed)
    attended_low = attended.astype(jnp.bfloat16)
    mixed_stream = stream + project(attended_low, out_w)
    normed_ff, inverse_b = norm_forward(mixed_stream, gain_b.astype(jnp.float32))
    normed_ff_low = normed_ff.astype(jnp.bfloat16)
    gate_value = project(normed_ff_low, gate_w)
    up_value = project(normed_ff_low, up_w)
    activated_low = (gate_value * jax.nn.sigmoid(gate_value) * up_value).astype(jnp.bfloat16)
    result = mixed_stream + project(activated_low, down_w)
    kept_state = (
        stream,
        first_inverse_factor,
        normed_low,
        key_block,
        value_block,
        query_all,
        row_top,
        row_total,
        attended_low,
        mixed_stream,
        inverse_b,
        normed_ff_low,
        gate_value,
        up_value,
        activated_low,
    )
    return (result, kept_state)


def layer_backward(grad_result, full_weights, kept_state, allowed):
    gain_a, query_w, key_w, value_w, out_w, gain_b, gate_w, up_w, down_w = full_weights
    (
        stream,
        first_inverse_factor,
        normed_low,
        key_block,
        value_block,
        query_all,
        row_top,
        row_total,
        attended_low,
        mixed_stream,
        inverse_b,
        normed_ff_low,
        gate_value,
        up_value,
        activated_low,
    ) = kept_state
    own_rows = stream.shape[1]
    branch_low = grad_result.astype(jnp.bfloat16)
    grad_down = outer_sum(activated_low, branch_low)
    grad_act = project_back(branch_low, down_w)
    sigmoid_gate = jax.nn.sigmoid(gate_value)
    grad_gate = (
        grad_act * up_value * sigmoid_gate * (1.0 + gate_value * (1.0 - sigmoid_gate))
    ).astype(jnp.bfloat16)
    grad_up_low = (grad_act * gate_value * sigmoid_gate).astype(jnp.bfloat16)
    grad_gate_w = outer_sum(normed_ff_low, grad_gate)
    grad_up_w = outer_sum(normed_ff_low, grad_up_low)
    grad_normed_ff = project_back(grad_gate, gate_w) + project_back(grad_up_low, up_w)
    grad_mixed_norm, grad_gain_b = norm_backward(
        mixed_stream, gain_b.astype(jnp.float32), inverse_b, grad_normed_ff
    )
    grad_mixed = grad_result + grad_mixed_norm
    attn_low = grad_mixed.astype(jnp.bfloat16)
    grad_out_w = outer_sum(attended_low, attn_low)
    grad_attended = project_back(attn_low, out_w).astype(jnp.bfloat16)
    grad_all = lax.all_gather(grad_attended, "key", axis=1, tiled=True)
    scores = head_scores(query_all, key_block, allowed)
    probability = (
        jnp.where(allowed[:, None], jnp.exp(scores - row_top[..., None]), 0.0)
        / row_total[..., None]
    )
    grad_heads = split_heads(grad_all)
    grad_probs = jnp.einsum(
        "sqhd,skhd->shqk", grad_heads, split_heads(value_block), preferred_element_type=jnp.float32
    )
    row_delta = lax.psum(
        jnp.sum(probability * grad_probs, axis=3).astype(jnp.bfloat16), "key"
    ).astype(jnp.float32)
    grad_scores = (probability * (grad_probs - row_delta[..., None])).astype(jnp.bfloat16)
    score_scale = (query_all.shape[2] // HEADS) ** (-0.5)
    query_part = (
        jnp.einsum(
            "shqk,skhd->sqhd",
            grad_scores,
            split_heads(key_block),
            preferred_element_type=jnp.float32,
        ).reshape(query_all.shape)
        * score_scale
    )
    grad_query = lax.psum_scatter(
        query_part.astype(jnp.bfloat16), "key", scatter_dimension=1, tiled=True
    )
    own_scores = grad_scores[..., :own_rows]
    grad_key = (
        jnp.einsum(
            "shqk,sqhd->skhd",
            own_scores,
            split_heads(query_all),
            preferred_element_type=jnp.float32,
        ).reshape(stream.shape)
        * score_scale
    ).astype(jnp.bfloat16)
    own_probs = probability.astype(jnp.bfloat16)[..., :own_rows]
    grad_value = (
        jnp.einsum("shqk,sqhd->skhd", own_probs, grad_heads, preferred_element_type=jnp.float32)
        .reshape(stream.shape)
        .astype(jnp.bfloat16)
    )
    grad_query_w = outer_sum(normed_low, grad_query)
    grad_key_w = outer_sum(normed_low, grad_key)
    grad_value_w = outer_sum(normed_low, grad_value)
    grad_normed = (
        project_back(grad_query, query_w)
        + project_back(grad_key, key_w)
        + project_back(grad_value, value_w)
    )
    grad_stream_norm, grad_gain_a = norm_backward(
        stream, gain_a.astype(jnp.float32), first_inverse_factor, grad_normed
    )
    grad_stream = grad_mixed + grad_stream_norm
    terms = (
        grad_gain_a,
        grad_query_w,
        grad_key_w,
        grad_value_w,
        grad_out_w,
        grad_gain_b,
        grad_gate_w,
        grad_up_w,
        grad_down,
    )
    return (grad_stream, terms)


def gathered_local(
    tokens,
    token_docs,
    memory_docs,
    memory_resets,
    memory_keys,
    memory_values,
    attn_gain1,
    query_weight1,
    key_weight1,
    value_weight1,
    out_weight1,
    ffn_gain1,
    gate_weight1,
    up_weight1,
    down_weight1,
    attn_gain2,
    second_query_weight,
    key_weight2,
    value_weight2,
    out_weight2,
    ffn_gain2,
    gate_weight2,
    up_weight2,
    down_weight2,
    cotangent,
):
    first_shards = (
        attn_gain1,
        query_weight1,
        key_weight1,
        value_weight1,
        out_weight1,
        ffn_gain1,
        gate_weight1,
        up_weight1,
        down_weight1,
    )
    second_shards = (
        attn_gain2,
        second_query_weight,
        key_weight2,
        value_weight2,
        out_weight2,
        ffn_gain2,
        gate_weight2,
        up_weight2,
        down_weight2,
    )
    docs_all = lax.all_gather(token_docs, "key", axis=1, tiled=True)
    own_rows = tokens.shape[1]
    query_place = jnp.arange(docs_all.shape[1], dtype=jnp.int32)
    key_place = lax.axis_index("key") * own_rows + jnp.arange(own_rows, dtype=jnp.int32)
    local_allowed = (key_place[None, None, :] <= query_place[None, :, None]) & (
        token_docs[:, None, :] == docs_all[:, :, None]
    )
    memory_allowed = (memory_docs[:, None, :] == docs_all[:, :, None]) & (
        memory_resets[:, None, None] == 0
    )
    both_allowed = jnp.concatenate((local_allowed, memory_allowed), axis=2)
    stream = tokens.astype(jnp.float32)
    first_full = fetch_weights(first_shards)
    middle, first_state = layer_forward(stream, first_full, local_allowed, None, None)
    second_full = fetch_weights(second_shards)
    result, second_state = layer_forward(
        middle, second_full, both_allowed, memory_keys, memory_values
    )
    second_full = refetch_weights(second_shards)
    grad_middle, second_terms = layer_backward(
        cotangent.astype(jnp.float32), second_full, second_state, both_allowed
    )
    second_grads = reduce_gradient_sums(second_terms)
    first_full = refetch_weights(first_shards)
    grad_stream, first_terms = layer_backward(grad_middle, first_full, first_state, local_allowed)
    first_grads = reduce_gradient_sums(first_terms)
    return (
        result.astype(jnp.bfloat16),
        grad_stream,
        first_grads[0],
        first_grads[1],
        first_grads[2],
        first_grads[3],
        first_grads[4],
        first_grads[5],
        first_grads[6],
        first_grads[7],
        first_grads[8],
        second_grads[0],
        second_grads[1],
        second_grads[2],
        second_grads[3],
        second_grads[4],
        second_grads[5],
        second_grads[6],
        second_grads[7],
        second_grads[8],
    )


MESH = pl.DeviceIdType.MESH
ANY = pl.BlockSpec(memory_space=pl.ANY)
VMEM = pl.BlockSpec(memory_space=pltpu.VMEM)
LOG2E = 1.4426950408889634
BLOCK = 512
QUERIES = 512
ROOM = 60 * 2**20
LOCAL = 4
HEAD = 128
PAIR = 2 * HEAD
BF = jnp.bfloat16
F32 = jnp.float32


SEND = pltpu.SemaphoreType.DMA


def flip(value, change):
    return lax.rem(value + change, 2)


class Place:
    def __init__(self):
        self.grp = lax.axis_index("grp")
        self.key = lax.axis_index("key")
        self.y, self.x = self.grp // 2, lax.rem(self.grp, 2)
        self.z, self.core = self.key // 2, lax.rem(self.key, 2)
        self.rank = lax.rem(self.key, LOCAL)
        self.seg = self.key // LOCAL

    def chip(self, da, db, dz, core):
        dx = da * (1 - core) + db * core
        dy = da * core + db * (1 - core)
        z = flip(self.z // 2, dz // 2) * 2 + flip(lax.rem(self.z, 2), lax.rem(dz, 2))
        return flip(self.y, dy) * 2 + flip(self.x, dx), z

    def device(self, da, db, dz):
        grp, z = self.chip(da, db, dz, self.core)
        return grp, z * 2 + self.core

    def sibling(self):
        return self.grp, self.z * 2 + 1 - self.core


def remote(src, dst, send, recv, target):
    return pltpu.make_async_remote_copy(
        src_ref=src, dst_ref=dst, send_sem=send, recv_sem=recv,
        device_id=target, device_id_type=MESH,
    )


def local(src, dst, sem):
    return pltpu.make_async_copy(src, dst, sem)


def span(index, size):
    return pl.ds(pl.multiple_of(index * size, size), size)


class RowBlocks:
    def __init__(self, rows, width):
        self.shape = (rows, width)

    def whole(self, chips):
        return (chips * 2 * self.shape[0], self.shape[1])

    def at(self, ref, chip, core):
        return ref.at[span((chip[0] * LOCAL + chip[1]) * 2 + core, self.shape[0]), :]


class PairBlocks(RowBlocks):
    def whole(self, chips):
        return (chips * self.shape[0], 2 * self.shape[1])

    def at(self, ref, chip, core):
        rows, width = self.shape
        return ref.at[span(chip[0] * LOCAL + chip[1], rows), span(core, width)]


class ColumnBlocks(RowBlocks):
    def __init__(self, rows, width, part):
        self.shape = (rows, width)
        self.part = part

    def at(self, ref, chip, core):
        rows, width = self.shape
        return ref.at[
            span((chip[0] * LOCAL + chip[1]) * 2 + core, rows), pl.ds(self.part * width, width)
        ]


class Swap:
    def __init__(self, arrays, to_heads):
        self.arrays = arrays
        self.to_heads = to_heads
        if to_heads:
            rows, width = arrays[0].shape
            self.parts = width // (LOCAL * PAIR)
            self.outs = [jax.ShapeDtypeStruct((rows * LOCAL, PAIR), BF)] * self.parts
        else:
            rows = arrays[0].shape[0] // LOCAL
            self.parts = len(arrays)
            self.outs = [jax.ShapeDtypeStruct((rows, self.parts * LOCAL * PAIR), BF)]
        self.rows = rows
        self.scratch = [SEND((self.parts, LOCAL)), SEND((self.parts, LOCAL)), SEND((self.parts,))]
        self.out_specs = [ANY] * len(self.outs)

    def run(self, at, ins, outs, scratch):
        send, recv, here = scratch

        def copy(part, k):
            target = lax.rem(at.rank + k, LOCAL)
            if self.to_heads:
                src = ins[0].at[:, span(part * LOCAL + target, PAIR)]
                dst = outs[part].at[span(at.rank, self.rows), :]
            else:
                src = ins[part].at[span(target, self.rows), :]
                dst = outs[0].at[:, span(part * LOCAL + at.rank, PAIR)]
            if k == 0:
                return local(src, dst, here.at[part])
            device = (at.grp, at.seg * LOCAL + target)
            return remote(src, dst, send.at[part, k], recv.at[part, k], device)

        every = [(part, k) for part in range(self.parts) for k in (2, 3, 1, 0)]
        for part, k in every:
            copy(part, k).start()
        yield
        yield "last"
        for part, k in every:
            copy(part, k).wait()


class Rows:
    def __init__(self, array):
        segs, rows, width = array.shape
        self.arrays = [array]
        self.rows = rows
        self.outs = [jax.ShapeDtypeStruct((segs * rows, width), array.dtype)]
        self.out_specs = [ANY]
        self.scratch = [SEND((2,)), SEND((2,)), SEND(())]

    def run(self, at, ins, outs, scratch):
        (src,), (dst,) = ins, outs
        send, recv, here = scratch
        chunk = lax.rem(at.key, 2)

        def part(index):
            return dst.at[span(index, self.rows), :]

        def out(seg):
            target = seg * LOCAL + at.key // 2
            return target, remote(
                src.at[seg], part(chunk), send.at[seg], recv.at[chunk], (at.grp, target)
            )

        for seg in range(2):
            target, copy = out(seg)
            pl.when(target != at.key)(copy.start)
            pl.when(target == at.key)(local(src.at[seg], part(chunk), here).start)
        yield
        yield "last"
        for seg in range(2):
            target, copy = out(seg)
            pl.when(target != at.key)(copy.wait_send)
        for index in range(2):
            owner = 2 * at.rank + index
            copy = remote(src.at[0], part(index), send.at[0], recv.at[index], (at.grp, owner))
            pl.when(owner != at.key)(copy.wait_recv)
            pl.when(owner == at.key)(local(src.at[0], part(index), here).wait)


class Chunks:
    def __init__(self, array):
        rows, width = array.shape
        self.arrays = [array]
        self.rows = rows // 2
        self.outs = [jax.ShapeDtypeStruct((2, rows // 2, width), array.dtype)]
        self.out_specs = [ANY]
        self.scratch = [SEND((2,)), SEND((2,)), SEND(())]

    def run(self, at, ins, outs, scratch):
        (src,), (dst,) = ins, outs
        send, recv, here = scratch

        def part(index):
            return src.at[pl.ds(index * self.rows, self.rows), :]

        def out(index):
            target = 2 * at.rank + index
            return target, remote(
                part(index), dst.at[at.seg], send.at[index], recv.at[at.seg], (at.grp, target)
            )

        for index in range(2):
            target, copy = out(index)
            pl.when(target != at.key)(copy.start)
            pl.when(target == at.key)(local(part(index), dst.at[at.seg], here).start)
        yield
        yield "last"
        for index in range(2):
            target, copy = out(index)
            pl.when(target != at.key)(copy.wait_send)
        for seg in range(2):
            owner = seg * LOCAL + at.key // 2
            copy = remote(part(0), dst.at[seg], send.at[0], recv.at[seg], (at.grp, owner))
            pl.when(owner != at.key)(copy.wait_recv)
            pl.when(owner == at.key)(local(part(0), dst.at[seg], here).wait)


class Memory:
    def __init__(self, array):
        self.arrays = [array]
        self.rows = array.shape[1]
        self.outs = [jax.ShapeDtypeStruct((2 * LOCAL * self.rows, PAIR), BF)]
        self.out_specs = [ANY]
        self.scratch = [SEND((2 * LOCAL,)), SEND((2 * LOCAL,)), SEND(())]

    def run(self, at, ins, outs, scratch):
        send, recv, here = scratch

        def copy(k):
            target = lax.rem(at.key + k, 2 * LOCAL)
            src = ins[0].at[target // LOCAL, :, span(lax.rem(target, LOCAL), PAIR)]
            dst = outs[0].at[span(at.key, self.rows), :]
            if k == 0:
                return local(src, dst, here)
            return remote(src, dst, send.at[k], recv.at[k], (at.grp, target))

        for k in range(2 * LOCAL):
            copy(k).start()
        yield
        yield "last"
        for k in range(2 * LOCAL):
            copy(k).wait()


class Docs:
    def __init__(self, array):
        rows, self.width = array.shape
        self.arrays = [array]
        self.outs = [jax.ShapeDtypeStruct((rows, 2 * LOCAL * self.width), array.dtype)]
        self.out_specs = [ANY]
        self.scratch = [SEND((2 * LOCAL,)), SEND((2 * LOCAL,)), SEND(())]

    def run(self, at, ins, outs, scratch):
        send, recv, here = scratch

        def copy(k):
            target = lax.rem(at.key + k, 2 * LOCAL)
            dst = outs[0].at[:, span(at.key, self.width)]
            if k == 0:
                return local(ins[0], dst, here)
            return remote(ins[0], dst, send.at[k], recv.at[k], (at.grp, target))

        for k in range(2 * LOCAL):
            copy(k).start()
        yield
        yield "last"
        for k in range(2 * LOCAL):
            copy(k).wait()


class Sibling:
    def __init__(self, array):
        self.arrays = [array]
        self.outs = [jax.ShapeDtypeStruct(array.shape, array.dtype)]
        self.out_specs = [ANY]
        self.scratch = [SEND(()), SEND(())]

    def run(self, at, ins, outs, scratch):
        copy = remote(ins[0], outs[0], scratch[0], scratch[1], at.sibling())
        copy.start()
        yield
        yield "last"
        copy.wait()


STEPS = [(da, db, dz) for db in range(2) for da in range(2) for dz in range(4)]


class Gather:
    def __init__(self, shard, blocks):
        self.arrays = [shard]
        self.blocks = blocks
        self.outs = [jax.ShapeDtypeStruct(blocks.whole(4 * LOCAL), shard.dtype)]
        self.out_specs = [ANY]
        self.scratch = [SEND((36,)), SEND((36,)), SEND(())]

    def run(self, at, ins, outs, scratch):
        (shard,), (whole,) = ins, outs
        send, recv, here = scratch
        core = at.core

        def spot(step, of=core):
            return self.blocks.at(whole, at.chip(*step, of), of)

        def copy(step, slot, target):
            mine = isinstance(step[2], int) and step == (0, 0, 0)
            src = shard if mine else spot(step)
            return remote(src, spot(step), send.at[slot], recv.at[slot], target)

        def cross(step):
            da, db, dz = step
            return 20 + 8 * db + 4 * da + dz

        def first(dz):
            return copy((0, 0, dz), 8 + dz, at.device(1, 0, 0))

        def second(da, dz):
            return copy((da, 0, dz), 12 + 4 * da + dz, at.device(0, 1, 0))

        def across(step):
            return copy(step, cross(step), at.sibling())

        def arrived(step, slot):
            dst = spot(step)
            remote(dst, dst, send.at[slot], recv.at[slot], at.sibling()).wait_recv()

        inner = flip(at.z // 2, lax.rem(at.z, 2))
        near, turns = at.device(0, 0, 1), (1, 2 + inner, 3 - inner)
        far = at.device(0, 0, 3)
        inside = pl.when(inner == 1)

        def along_z(index):
            if index == 0:
                return remote(shard, spot((0, 0, 0)), send.at[0], recv.at[1], near)
            if index == 1:
                return remote(shard, spot((0, 0, 0)), send.at[1], recv.at[3], far)
            step, slot, device = {
                2: ((0, 0, 1), 2, far), 3: ((0, 0, 3), 2, near), 4: ((0, 0, 2), 3, near)
            }[index]
            return remote(spot(step), spot(step), send.at[index], recv.at[slot], device)

        mine = local(shard, spot((0, 0, 0)), here)
        mine.start()
        along_z(0).start()
        inside(along_z(1).start)
        first(0).start()
        second(0, 0).start()
        across((0, 0, 0)).start()
        yield
        for turn, dz in enumerate(turns):
            arrived((0, 0, dz), dz)
            inside(along_z((2, 3, 4)[turn]).start)
            first(dz).start()
            second(0, dz).start()
            across((0, 0, dz)).start()
            yield
        for dz in (0,) + turns:
            arrived((1, 0, dz), 8 + dz)
            second(1, dz).start()
            across((1, 0, dz)).start()
        yield
        for da in range(2):
            for dz in (0,) + turns:
                arrived((da, 1, dz), 12 + 4 * da + dz)
                across((da, 1, dz)).start()
        yield "last"
        for step in STEPS:
            dst = spot(step, 1 - core)
            slot = cross(step)
            remote(dst, dst, send.at[slot], recv.at[slot], at.sibling()).wait_recv()
        along_z(0).wait_send()
        for index in range(1, 5):
            inside(along_z(index).wait_send)
        for dz in range(4):
            first(dz).wait_send()
            for da in range(2):
                second(da, dz).wait_send()
        for step in STEPS:
            across(step).wait_send()
        mine.wait()


def tile_of(rows, width):
    sizes = [width // n for n in range(1, width // HEAD + 1) if width % (n * HEAD) == 0]
    return next((size for size in sizes if rows * size <= 32768), HEAD)


def add_into(dst, parts):
    rows, width = dst.shape
    tile = tile_of(rows, width)

    def one(cut):
        total = parts[0][:, cut].astype(F32)
        for part in parts[1:]:
            total += part[:, cut].astype(F32)
        dst[:, cut] = total.astype(dst.dtype)

    if tile == width:
        one(pl.ds(0, width))
    else:

        @pl.loop(0, width // tile)
        def _(t):
            one(pl.ds(pl.multiple_of(t * tile, tile), tile))


class Front:
    def __init__(self, tokens, shard, blocks, gains, gain_blocks, rest):
        self.rest = rest
        self.parts = [Gather(shard, blocks), Gather(gains, gain_blocks), Rows(tokens)]
        (rows,) = self.parts[2].outs
        rows, width = rows.shape
        columns = blocks.shape[1]
        qkv = jax.ShapeDtypeStruct((rows, columns), BF)
        self.swap = Swap([qkv], True)
        self.arrays = [part.arrays[0] for part in self.parts]
        self.outs = [part.outs[0] for part in self.parts]
        self.outs += [jax.ShapeDtypeStruct((rows, width), BF)] + self.swap.outs
        self.out_specs = [ANY] * 3 + [VMEM] + self.swap.out_specs
        self.scratch = [s for part in self.parts for s in part.scratch] + self.swap.scratch
        self.scratch += [
            pltpu.VMEM((width, columns), BF),
            pltpu.VMEM((rows, width), BF),
            pltpu.VMEM(self.parts[1].outs[0].shape, BF),
            pltpu.VMEM((rows, columns), BF),
            SEND((3,)),
        ]

    def run(self, at, ins, outs, scratch):
        stages, rest = [], list(scratch)
        for index, part in enumerate(self.parts):
            held = [rest.pop(0) for _ in part.scratch]
            stages.append(part.run(at, [ins[index]], [outs[index]], held))
        swap_scratch = [rest.pop(0) for _ in self.swap.scratch]
        weights, tokens, gains, qkv, load = rest
        normed, swapped = outs[3], outs[4:]
        gathers, rows = stages[:2], stages[2]

        def step():
            for stage in gathers:
                next(stage)

        step()
        yield
        for _ in range(3):
            step()
        next(rows)
        yield
        step()
        step()
        for stage in stages:
            for _ in stage:
                pass
        copies = [
            local(src, dst, load.at[i])
            for i, (src, dst) in enumerate(zip((outs[2], outs[1], outs[0]), (tokens, gains, weights)))
        ]
        for copy in copies:
            copy.start()
        yield
        for copy in copies:
            copy.wait()
        values = tokens[...].astype(F32)
        gain = gains[...].astype(F32).T[0:1, :]
        normed[...] = (values * inverse_rms(values) * gain).astype(BF)
        tile = 512

        @pl.loop(0, qkv.shape[1] // tile)
        def _(t):
            cut = pl.ds(pl.multiple_of(t * tile, tile), tile)
            qkv[:, cut] = dot_nn(normed[...], weights[:, cut]).astype(BF)

        for _ in range(self.rest):
            yield
        swap = self.swap.run(at, [qkv], swapped, swap_scratch)
        next(swap)
        yield
        yield "last"
        for _ in swap:
            pass


class Assemble:
    def __init__(self, groups, blocks):
        self.arrays = list(groups)
        self.blocks = blocks
        self.outs = [jax.ShapeDtypeStruct(b.whole(4 * LOCAL), groups[0].dtype) for b in blocks]
        self.out_specs = [ANY] * len(blocks)
        n = len(blocks)
        self.scratch = [SEND((n, 16)), SEND((n, 16)), SEND((n, 16)), SEND((16,))]
        self.scratch += [pltpu.VMEM((16,) + groups[0].shape[1:], groups[0].dtype)]

    def run(self, at, ins, outs, scratch):
        send, recv, here, load, held = scratch

        def fetch(slot):
            return local(ins[slot // 4].at[slot % 4], held.at[slot], load.at[slot])

        def each():
            for slot in range(16):
                begin = 0
                for index, blocks in enumerate(self.blocks):
                    yield index, slot, pl.ds(begin, blocks.shape[1])
                    begin += blocks.shape[1]

        def spot(index, slot, core):
            return self.blocks[index].at(outs[index], at.chip(*STEPS[slot], core), core)

        def copies(index, slot, cut):
            src = held.at[slot, :, cut]
            dst = spot(index, slot, at.core)
            return remote(
                src, dst, send.at[index, slot], recv.at[index, slot], at.sibling()
            ), local(src, dst, here.at[index, slot])

        for slot in range(16):
            fetch(slot).start()
        yield
        for index, slot, cut in each():
            if index == 0:
                fetch(slot).wait()
            for copy in copies(index, slot, cut):
                copy.start()
        yield "last"
        for index, slot, cut in each():
            across, own = copies(index, slot, cut)
            across.wait_send()
            own.wait()
            dst = spot(index, slot, 1 - at.core)
            remote(dst, dst, send.at[index, slot], recv.at[index, slot], at.sibling()).wait_recv()


PACK = 16


class CoreSums:
    def __init__(self, *wholes):
        self.arrays = [whole for whole, _ in wholes]
        self.blocks = [blocks for _, blocks in wholes]
        shapes = [blocks.shape for blocks in self.blocks]
        self.width = sum(rows // PACK * width for rows, width in shapes)
        self.outs = [jax.ShapeDtypeStruct((n, PACK, self.width), BF) for n in (4, 4, 8)]
        self.out_specs = [ANY] * 3
        n = len(shapes)
        self.scratch = [pltpu.VMEM((16,) + shape, BF) for shape in shapes] * 2
        self.scratch += [pltpu.VMEM((16, PACK, self.width), BF)]
        self.scratch += [SEND((n, 16)), SEND((n, 16)), SEND((n, 16)), SEND((16,))]

    def run(self, at, ins, outs, scratch):
        n = len(ins)
        own, near, packed = scratch[:n], scratch[n : 2 * n], scratch[2 * n]
        load, send, recv, store = scratch[2 * n + 1 :]

        def chip(slot, core):
            return at.chip(lax.rem(slot // 4, 2), slot // 8, lax.rem(slot, 4), core)

        def fetch(index, slot):
            src = self.blocks[index].at(ins[index], chip(slot, at.core), at.core)
            return local(src, own[index].at[slot], load.at[index, slot])

        def across(index, slot):
            other = 1 - at.core
            src = self.blocks[index].at(ins[index], chip(slot, other), other)
            return remote(
                src, near[index].at[slot], send.at[index, slot], recv.at[index, slot], at.sibling()
            )

        def keep(slot, group, first):
            return local(packed.at[slot], outs[group].at[slot - first], store.at[slot])

        @pl.loop(0, 16)
        def _(turn):
            for index in range(n):
                across(index, 15 - turn).start()
                fetch(index, 15 - turn).start()

        yield
        groups = ((2, 8, 8), (1, 4, 4), (0, 0, 4))
        for group, first, count in groups:

            @pl.loop(0, count)
            def _(turn):
                slot = first + count - 1 - turn
                begin = 0
                for index in range(n):
                    fetch(index, slot).wait()
                    across(index, slot).wait_recv()
                    rows, width = self.blocks[index].shape
                    for part in range(rows // PACK):
                        cut = pl.ds(part * PACK, PACK)
                        add_into(
                            packed.at[slot, :, pl.ds(begin, width)],
                            [own[index].at[slot, cut, :], near[index].at[slot, cut, :]],
                        )
                        begin += width
                keep(slot, group, first).start()

            yield
        yield "last"
        for group, first, count in groups:

            @pl.loop(0, count)
            def _(turn):
                slot = first + count - 1 - turn
                for index in range(n):
                    across(index, slot).wait_send()
                keep(slot, group, first).wait()


def unpack(total, shapes):
    blocks, begin = [], 0
    for rows, width in shapes:
        parts = []
        for _ in range(rows // PACK):
            parts.append(total[:, begin : begin + width])
            begin += width
        blocks.append(jnp.concatenate(parts, axis=0))
    return blocks


class LineSums:
    def __init__(self, terms, shapes, cuts, rest=0):
        self.arrays = list(terms)
        self.rest = rest
        self.shapes = shapes
        self.outs = [jax.ShapeDtypeStruct(shape, F32) for shape in shapes]
        self.out_specs = [VMEM] * len(shapes)
        self.segments, begin = [], 0
        for index, (rows, width) in enumerate(shapes):
            for part in range(rows // PACK):
                self.segments.append((index, part, begin, width))
                begin += width
        self.pieces = []
        for group in cuts:
            held = [s for s in self.segments if s[0] in group]
            first = held[0][2]
            self.pieces.append((first, held[-1][2] + held[-1][3] - first, held))
        n = len(self.pieces)
        box = (PACK, begin)
        self.scratch = [pltpu.VMEM((4,) + box, BF) for _ in terms]
        self.scratch += [pltpu.VMEM((4,) + box, BF), pltpu.VMEM((4,) + box, BF)]
        self.scratch += [pltpu.VMEM((2,) + box, BF), pltpu.VMEM(box, BF)]
        self.scratch += [SEND((len(terms), 4)), SEND((6, n)), SEND((6, n))]

    def run(self, at, ins, outs, scratch):
        n = len(ins)
        terms = scratch[:n]
        low, outer_box, far_box, inner_box, load, send, recv = scratch[n:]
        inner = flip(at.z // 2, lax.rem(at.z, 2))
        inside, outside = pl.when(inner == 1), pl.when(inner == 0)
        near, far = at.device(0, 0, 1), at.device(0, 0, 3)
        pieces = range(len(self.pieces))

        def fetch(index, dz):
            return local(ins[index].at[dz], terms[index].at[dz], load.at[index, dz])

        def columns_of(c):
            first, width, _ = self.pieces[c]
            return pl.ds(first, width)

        def hand(kind, c):
            cut = columns_of(c)
            src, dst, target = {
                1: (low.at[1, :, cut], outer_box.at[1, :, cut], near),
                2: (low.at[2, :, cut], outer_box.at[2, :, cut], near),
                3: (low.at[3, :, cut], outer_box.at[3, :, cut], near),
                0: (low.at[3, :, cut], far_box.at[0, :, cut], far),
                4: (low.at[2, :, cut], far_box.at[1, :, cut], far),
                5: (low.at[1, :, cut], inner_box.at[:, cut], near),
            }[kind]
            return remote(src, dst, send.at[kind, c], recv.at[kind, c], target)

        def settle(c, dz, more):
            for _, _, begin, width in self.pieces[c][2]:
                cut = pl.ds(begin, width)
                parts = [term.at[dz, :, cut] for term in terms] + [m.at[:, cut] for m in more]
                add_into(low.at[dz, :, cut], parts)

        def finish(c, more):
            for index, part, begin, width in self.pieces[c][2]:
                cut = pl.ds(begin, width)
                parts = [term.at[0, :, cut] for term in terms] + [m.at[:, cut] for m in more]
                add_into(outs[index].at[pl.ds(part * PACK, PACK), :], parts)

        for dz in (2, 3, 1, 0):
            for index in range(n):
                fetch(index, dz).start()
        yield
        for dz in (2, 3, 1, 0):
            for index in range(n):
                fetch(index, dz).wait()

        @outside
        def _():
            for c in pieces:
                for dz in (2, 3, 1):
                    settle(c, dz, [])
                    hand(dz, c).start()

        def inwards(c):
            @inside
            def _():
                hand(2, c).wait_recv()
                settle(c, 3, [outer_box.at[2]])
                hand(0, c).start()
                hand(3, c).wait_recv()
                settle(c, 2, [outer_box.at[3]])
                hand(4, c).start()

        def outwards(c):
            @inside
            def _():
                hand(4, c).wait_recv()
                settle(c, 1, [far_box.at[1]])
                hand(5, c).start()
                hand(0, c).wait_recv()
                hand(1, c).wait_recv()
                finish(c, [outer_box.at[1], far_box.at[0]])

            @outside
            def _():
                hand(5, c).wait_recv()
                finish(c, [inner_box])

        for _ in range(1 + self.rest):
            yield
        for c in pieces:
            inwards(c)
            yield
            if c:
                outwards(c - 1)
                yield
        yield "last"
        outwards(len(self.pieces) - 1)
        for c in pieces:

            @outside
            def _():
                for kind in (1, 2, 3):
                    hand(kind, c).wait_send()

            @inside
            def _():
                for kind in (0, 4, 5):
                    hand(kind, c).wait_send()


class Scatter:
    def __init__(self, whole, blocks, turn=0):
        self.arrays = [whole]
        self.blocks = blocks
        self.turn = turn
        shape = blocks.shape
        self.pair = isinstance(blocks, PairBlocks)
        out = (shape[0] // 2, 2 * shape[1]) if self.pair else shape
        self.outs = [jax.ShapeDtypeStruct(out, F32)]
        self.out_specs = [VMEM]
        dma = SEND
        self.scratch = [
            pltpu.VMEM((16,) + shape, BF),
            pltpu.VMEM((16,) + shape, BF),
            pltpu.VMEM((8,) + shape, BF),
            pltpu.VMEM((4,) + shape, BF),
            pltpu.VMEM((4,) + shape, BF),
            dma((16,)),
            dma((32,)),
            dma((32,)),
        ]
        if self.pair:
            self.scratch += [pltpu.VMEM(shape, F32), dma((2,))]

    def run(self, at, ins, outs, scratch):
        (whole,), (out,) = ins, outs
        own, near, from_b, from_a, from_z, load, send, recv = scratch[:8]
        core = at.core
        order = list(reversed(STEPS))

        def fetch(slot):
            src = self.blocks.at(whole, at.chip(*STEPS[slot], core), core)
            return local(src, own.at[slot], load.at[slot])

        def across(slot):
            src = self.blocks.at(whole, at.chip(*STEPS[slot], 1 - core), 1 - core)
            return remote(src, near.at[slot], send.at[slot], recv.at[slot], at.sibling())

        def second(da, dz):
            slot = STEPS.index((da, 1, dz))
            spot = 4 * da + dz
            return remote(
                own.at[slot], from_b.at[spot], send.at[16 + spot], recv.at[16 + spot],
                at.device(0, 1, 0),
            )

        def first(dz):
            slot = STEPS.index((1, 0, dz))
            return remote(
                own.at[slot], from_a.at[dz], send.at[24 + dz], recv.at[24 + dz], at.device(1, 0, 0)
            )

        def along_z(dz):
            slot = STEPS.index((0, 0, dz))
            return remote(
                own.at[slot], from_z.at[dz], send.at[28 + dz], recv.at[28 + dz], at.device(0, 0, dz)
            )

        for step in order:
            slot = STEPS.index(step)
            across(slot).start()
            fetch(slot).start()
        for _ in range(1 + self.turn):
            yield

        def settle(step, more, dst=None):
            slot = STEPS.index(step)
            fetch(slot).wait()
            across(slot).wait_recv()
            parts = [own.at[slot], near.at[slot]] + more
            add_into(own.at[slot] if dst is None else dst, parts)

        for da in (1, 0):
            for dz in (3, 2, 1, 0):
                settle((da, 1, dz), [])
                second(da, dz).start()
        yield
        for dz in (3, 2, 1, 0):
            second(1, dz).wait_recv()
            settle((1, 0, dz), [from_b.at[4 + dz]])
            first(dz).start()
        yield
        for dz in (3, 2, 1):
            second(0, dz).wait_recv()
            first(dz).wait_recv()
            settle((0, 0, dz), [from_b.at[dz], from_a.at[dz]])
            along_z(dz).start()
        yield "last"
        second(0, 0).wait_recv()
        first(0).wait_recv()
        for dz in (1, 2, 3):
            along_z(dz).wait_recv()
        total = scratch[8] if self.pair else out
        more = [from_b.at[0], from_a.at[0]] + [from_z.at[dz] for dz in (1, 2, 3)]
        settle((0, 0, 0), more, total)
        if self.pair:
            rows, width = self.blocks.shape
            half = rows // 2
            columns = span(core, width)
            swap = remote(
                total.at[span(1 - core, half), :], out.at[:, columns],
                scratch[9].at[0], scratch[9].at[1], at.sibling(),
            )
            swap.start()
            out[:, columns] = total[span(core, half), :]
        if self.pair:
            swap.wait()
        for slot in range(16):
            across(slot).wait_send()
        for dz in range(4):
            for da in range(2):
                second(da, dz).wait_send()
            first(dz).wait_send()
            if dz:
                along_z(dz).wait_send()


def later(part, steps=2):
    part.wait = steps
    return part


def staged(part, *refs):
    for _ in range(getattr(part, "wait", 0)):
        yield
    yield from part.run(*refs)


def exchange(name, collective, parts):
    sizes = [(len(p.arrays), len(p.outs), len(p.scratch)) for p in parts]
    n_in = sum(size[0] for size in sizes)
    n_out = sum(size[1] for size in sizes)

    def kernel(*refs):
        at = Place()
        barrier = pltpu.get_barrier_semaphore()
        near = [(at.grp, lax.rem(at.key + k, 2 * LOCAL)) for k in range(1, 2 * LOCAL)]
        near += [at.device(1, 0, 0), at.device(0, 1, 0)]
        for device in near:
            pl.semaphore_signal(barrier, inc=1, device_id=device, device_id_type=MESH)
        pl.semaphore_wait(barrier, len(near))
        ins, outs, scratch = refs[:n_in], refs[n_in : n_in + n_out], refs[n_in + n_out :]
        live = []
        sums = any(isinstance(part, Scatter) for part in parts)
        for part, (i, o, s) in zip(parts, sizes):
            live.append(staged(part, at, ins[:i], outs[:o], scratch[:s]))
            ins, outs, scratch = ins[i:], outs[o:], scratch[s:]
        for stage in live:
            next(stage)
        ending = []
        while live:
            for stage in list(reversed(live) if sums else live):
                if next(stage) == "last":
                    live.remove(stage)
                    ending.append(stage)
        for stage in ending:
            for _ in stage:
                pass

    outs = pl.pallas_call(
        kernel,
        name=name,
        out_shape=[o for p in parts for o in p.outs],
        in_specs=[ANY] * n_in,
        out_specs=[o for p in parts for o in p.out_specs],
        scratch_shapes=[s for p in parts for s in p.scratch],
        compiler_params=pltpu.CompilerParams(
            collective_id=collective, has_side_effects=True, vmem_limit_bytes=ROOM
        ),
    )(*[a for p in parts for a in p.arrays])
    outs = list(outs)
    return [[outs.pop(0) for _ in p.outs] for p in parts]


def hop(values, change):
    pairs = []
    for y in range(2):
        for x in range(2):
            for z in range(LOCAL):
                for core in range(2):
                    to = [y, x, z, core]
                    if change in ("a", "b"):
                        to[1 if (change == "a") == (core == 0) else 0] ^= 1
                    elif change == "core":
                        to[3] ^= 1
                    else:
                        to[2] ^= change
                    number = [((v[0] * 2 + v[1]) * LOCAL + v[2]) * 2 + v[3] for v in ([y, x, z, core], to)]
                    pairs.append(tuple(number))
    return lax.ppermute(values, ("grp", "key"), pairs)


def column_hop(values, pairs):
    size = 2 * LOCAL
    every = [(g * size + s, g * size + t) for g in range(4) for s, t in pairs]
    return lax.ppermute(values, ("grp", "key"), every)


def join(value, others):
    return lax.optimization_barrier((value, others))


def gather_column(shard):
    return jnp.stack([shard] + [hop(shard, dz) for dz in (1, 2, 3)])


def add(*terms):
    return sum(term.astype(F32) for term in terms)


def scatter_second(sums):
    here, first, second = sums
    return here, first, hop(second, "b")


def scatter_first(sums):
    here, first, got = sums
    return here, got, hop(add(first, got[4:]).astype(BF), "a")


def scatter_z(sums):
    here, got, more = sums
    total = add(here, got[:4], more)
    low = total[1:].astype(BF)
    return [total[0]] + [hop(low[dz - 1], dz) for dz in (1, 2, 3)]


def scatter_end(sums):
    return add(*sums)


def rows_hops(chunks):
    odd = lax.rem(lax.axis_index("key"), 2) == 1
    size = 2 * LOCAL
    same = [(j, j // 2 + LOCAL * (j % 2)) for j in range(size)]
    cross = [(j, j // 2 + LOCAL * (1 - j % 2)) for j in range(size)]
    one = column_hop(jnp.where(odd, chunks[1], chunks[0]), same)
    two = column_hop(jnp.where(odd, chunks[0], chunks[1]), cross)
    upper = lax.axis_index("key") >= LOCAL
    return jnp.concatenate((jnp.where(upper, two, one), jnp.where(upper, one, two)))


def chunk_hops(rows):
    half = rows.shape[0] // 2
    odd = lax.rem(lax.axis_index("key"), 2) == 1
    upper = lax.axis_index("key") >= LOCAL
    size = 2 * LOCAL
    same = [(j // 2 + LOCAL * (j % 2), j) for j in range(size)]
    cross = [(j // 2 + LOCAL * (1 - j % 2), j) for j in range(size)]
    one = column_hop(jnp.where(upper, rows[half:], rows[:half]), same)
    two = column_hop(jnp.where(upper, rows[:half], rows[half:]), cross)
    return jnp.stack((jnp.where(odd, two, one), jnp.where(odd, one, two)))


def dot_nt(a, b):
    return lax.dot_general(a, b, (((1,), (1,)), ((), ())), preferred_element_type=F32)


def dot_nn(a, b):
    return lax.dot_general(a, b, (((1,), (0,)), ((), ())), preferred_element_type=F32)


def heads(index):
    return pl.ds(index * HEAD, HEAD)


def block_rows(j):
    return pl.ds(pl.multiple_of(j * BLOCK, BLOCK), BLOCK)


def turned(values):
    return values.astype(F32).T.astype(BF)


def transpose_blocks(src, dst):
    @pl.loop(0, src.shape[0] // BLOCK)
    def _(j):
        dst[j] = turned(src[block_rows(j), :])


def visible(bounds, low, high, j):
    at = lax.broadcasted_iota(jnp.int32, (BLOCK, QUERIES), 0)
    start = j * BLOCK
    return (at >= bounds[low : low + 1, :] - start) & (at < bounds[high : high + 1, :] - start)


def fold(values):
    return values.reshape(values.shape[0] // 8, 8, values.shape[1])


def each_block(ranges, i, with_memory, local_body, memory_body):
    begin, full, diagonal, end = (ranges[i, k] for k in range(4))
    lax.fori_loop(begin, full, local_body(True), 0)
    lax.fori_loop(full, diagonal, local_body(False), 0)
    lax.fori_loop(diagonal, end, local_body(True), 0)
    if with_memory:
        begin, full, rest, end = (ranges[i, k] for k in range(4, 8))
        lax.fori_loop(begin, full, memory_body(True), 0)
        lax.fori_loop(full, rest, memory_body(False), 0)
        lax.fori_loop(rest, end, memory_body(True), 0)


def attend_kernel(with_memory, ranges, *refs):
    if with_memory:
        q, k, v, bounds, mk, mv, out, stat, vt, mvt, scores, acc, top, total = refs
    else:
        q, k, v, bounds, out, stat, vt, scores, acc, top, total = refs
        mk = mvt = None
    i = pl.program_id(0)
    scale = HEAD ** (-0.5) * LOG2E
    blocks = vt.shape[0]

    @pl.when(i == 0)
    def _():
        transpose_blocks(v, vt)
        if with_memory:
            transpose_blocks(mv, mvt)

    acc[...] = jnp.zeros_like(acc)
    top[...] = jnp.full_like(top, NEG)
    total[...] = jnp.zeros_like(total)

    def scan(keys, first, low):
        def run(masked):
            def body(j, _):
                for h in range(2):
                    part = dot_nt(keys[block_rows(j), heads(h)], q[:, heads(h)])
                    if masked:
                        part = jnp.where(visible(bounds, low, low + 1, j), part, NEG)
                    scores[h, first + j] = part
                    top[h] = jnp.maximum(top[h], jnp.max(fold(part), axis=0))
                return 0

            return body

        return run

    each_block(ranges, i, with_memory, scan(k, 0, 0), scan(mk, blocks, 2))
    tops = [jnp.max(top[h], axis=0, keepdims=True) * scale for h in range(2)]

    def take(values_t, first):
        def run(masked):
            def body(j, _):
                for h in range(2):
                    probs = jnp.exp2(scores[h, first + j] * scale - tops[h])
                    total[h] += jnp.sum(fold(probs), axis=0)
                    acc[heads(h), :] += dot_nn(values_t[j, heads(h), :], probs.astype(BF))
                return 0

            return body

        return run

    lax.fori_loop(ranges[i, 0], ranges[i, 3], take(vt, 0)(False), 0)
    if with_memory:
        lax.fori_loop(ranges[i, 4], ranges[i, 7], take(mvt, blocks)(False), 0)
    for h in range(2):
        share = jnp.sum(total[h], axis=0, keepdims=True)
        out[:, heads(h)] = (acc[heads(h), :] / share).T.astype(BF)
        stat[h : h + 1, :] = tops[h] + jnp.log2(share)
    stat[2:, :] = jnp.zeros_like(stat[2:, :])


def attend(q, k, v, memory, bounds, ranges):
    rows = q.shape[0]
    blocks = rows // BLOCK
    row_block = pl.BlockSpec((QUERIES, PAIR), lambda i, *_: (i, 0))
    lane_block = pl.BlockSpec((8, QUERIES), lambda i, *_: (0, i))
    operands = [q, k, v, bounds]
    in_specs = [row_block, VMEM, VMEM, lane_block]
    scratch = [pltpu.VMEM((blocks, PAIR, BLOCK), BF)]
    if memory is not None:
        operands += [memory[0], memory[1]]
        in_specs += [VMEM, VMEM]
        more = memory[1].shape[0] // BLOCK
        scratch += [pltpu.VMEM((more, PAIR, BLOCK), BF)]
        blocks += more
    return pl.pallas_call(
        functools.partial(attend_kernel, memory is not None),
        name="attend",
        grid_spec=pltpu.PrefetchScalarGridSpec(
            num_scalar_prefetch=1,
            grid=(rows // QUERIES,),
            in_specs=in_specs,
            out_specs=(row_block, lane_block),
            scratch_shapes=scratch
            + [
                pltpu.VMEM((2, blocks, BLOCK, QUERIES), F32),
                pltpu.VMEM((PAIR, QUERIES), F32),
                pltpu.VMEM((2, 8, QUERIES), F32),
                pltpu.VMEM((2, 8, QUERIES), F32),
            ],
        ),
        out_shape=(
            jax.ShapeDtypeStruct((rows, PAIR), BF),
            jax.ShapeDtypeStruct((8, rows), F32),
        ),
        compiler_params=pltpu.CompilerParams(vmem_limit_bytes=ROOM),
    )(ranges, *operands)


def attend_back_kernel(with_memory, ranges, *refs):
    if with_memory:
        (q, go, o, stat, bounds, k, v, mk, mv, gq, gk, gv, kt, mkt, delta, gq_t, gk_sum, gv_sum) = refs
    else:
        (q, go, o, stat, bounds, k, v, gq, gk, gv, kt, delta, gq_t, gk_sum, gv_sum) = refs
        mk = mv = mkt = None
    i = pl.program_id(0)
    unit = HEAD ** (-0.5)
    scale = unit * LOG2E

    @pl.when(i == 0)
    def _():
        transpose_blocks(k, kt)
        gk_sum[...] = jnp.zeros_like(gk_sum)
        gv_sum[...] = jnp.zeros_like(gv_sum)
        if with_memory:
            transpose_blocks(mk, mkt)

    for h in range(2):
        both = go[:, heads(h)].astype(F32) * o[:, heads(h)].astype(F32)
        delta[h : h + 1, :] = jnp.sum(both.T, axis=0, keepdims=True)
    gq_t[...] = jnp.zeros_like(gq_t)

    def step(keys, values, keys_t, low, own):
        def run(masked):
            def body(j, _):
                for h in range(2):
                    query, grad = q[:, heads(h)], go[:, heads(h)]
                    scores = dot_nt(keys[block_rows(j), heads(h)], query) * scale
                    probs = jnp.exp2(scores - stat[h : h + 1, :])
                    if masked:
                        probs = jnp.where(visible(bounds, low, low + 1, j), probs, 0.0)
                    grad_probs = dot_nt(values[block_rows(j), heads(h)], grad)
                    grad_scores = (probs * (grad_probs - delta[h : h + 1, :])).astype(BF)
                    gq_t[heads(h), :] += dot_nn(keys_t[j, heads(h), :], grad_scores)
                    if own:
                        gv_sum[block_rows(j), heads(h)] += dot_nn(probs.astype(BF), grad)
                        gk_sum[block_rows(j), heads(h)] += dot_nn(grad_scores, query)
                return 0

            return body

        return run

    each_block(ranges, i, with_memory, step(k, v, kt, 0, True), step(mk, mv, mkt, 2, False))
    gq[...] = (gq_t[...] * unit).T.astype(BF)

    @pl.when(i == pl.num_programs(0) - 1)
    def _():
        gk[...] = (gk_sum[...] * unit).astype(BF)
        gv[...] = gv_sum[...].astype(BF)


def attend_back(q, k, v, memory, bounds, ranges, out, stat, grad):
    rows = q.shape[0]
    blocks = rows // BLOCK
    row_block = pl.BlockSpec((QUERIES, PAIR), lambda i, *_: (i, 0))
    lane_block = pl.BlockSpec((8, QUERIES), lambda i, *_: (0, i))
    operands = [q, grad, out, stat, bounds, k, v]
    in_specs = [row_block, row_block, row_block, lane_block, lane_block, VMEM, VMEM]
    scratch = [pltpu.VMEM((blocks, PAIR, BLOCK), BF)]
    if memory is not None:
        operands += [memory[0], memory[1]]
        in_specs += [VMEM, VMEM]
        scratch += [pltpu.VMEM((memory[0].shape[0] // BLOCK, PAIR, BLOCK), BF)]
    whole = jax.ShapeDtypeStruct((rows, PAIR), BF)
    return pl.pallas_call(
        functools.partial(attend_back_kernel, memory is not None),
        name="attend_back",
        grid_spec=pltpu.PrefetchScalarGridSpec(
            num_scalar_prefetch=1,
            grid=(rows // QUERIES,),
            in_specs=in_specs,
            out_specs=(row_block, VMEM, VMEM),
            scratch_shapes=scratch
            + [
                pltpu.VMEM((8, QUERIES), F32),
                pltpu.VMEM((PAIR, QUERIES), F32),
                pltpu.VMEM((rows, PAIR), F32),
                pltpu.VMEM((rows, PAIR), F32),
            ],
        ),
        out_shape=(whole, whole, whole),
        compiler_params=pltpu.CompilerParams(vmem_limit_bytes=ROOM),
    )(ranges, *operands)


NUMBERS = 8


def members(docs):
    number = jnp.arange(NUMBERS, dtype=jnp.int32)
    return (docs[None, :] == number[:, None]).astype(jnp.int32)


def before(counts):
    at = jnp.arange(counts.shape[-1])
    earlier = at[:, None] < at[None, :]
    return jnp.sum(jnp.where(earlier, counts[..., :, None], 0), axis=-2)


def pick(which, table):
    return jnp.sum(which * table[:, None], axis=0)


def mask_ranges(docs, mem_docs, reset):
    rows = docs.shape[0]
    at = jnp.arange(rows, dtype=jnp.int32)
    own, other = members(docs), members(mem_docs)
    start = pick(own, before(jnp.sum(own, axis=1)))
    counts = jnp.where(reset == 0, jnp.sum(other, axis=1), 0)
    mem_low = pick(own, before(counts))
    mem_high = mem_low + pick(own, counts)
    zero = jnp.zeros_like(start)
    bounds = jnp.stack((start, at + 1, mem_low, mem_high, zero, zero, zero, zero))

    def per_block(values):
        return values.reshape(rows // QUERIES, QUERIES)

    def up(values):
        return (values + BLOCK - 1) // BLOCK

    step = QUERIES // BLOCK
    diagonal = jnp.arange(rows // QUERIES, dtype=jnp.int32) * step
    first = jnp.min(per_block(start), axis=1) // BLOCK
    full = jnp.clip(up(jnp.max(per_block(start), axis=1)), first, diagonal)
    some = mem_high > mem_low
    mem_first = jnp.min(per_block(jnp.where(some, mem_low, mem_docs.shape[0])), axis=1) // BLOCK
    mem_end = jnp.maximum(up(jnp.max(per_block(mem_high), axis=1)), mem_first)
    mem_full = jnp.clip(up(jnp.max(per_block(mem_low), axis=1)), mem_first, mem_end)
    mem_rest = jnp.clip(jnp.min(per_block(mem_high), axis=1) // BLOCK, mem_full, mem_end)
    columns = (first, full, diagonal, diagonal + step, mem_first, mem_full, mem_rest, mem_end)
    return bounds, jnp.stack(columns, axis=1)


def sort_memory(memory, mem_docs):
    entries = mem_docs.shape[0]
    which = members(mem_docs)
    lanes = which.reshape(-1, HEAD)
    at = jnp.arange(HEAD)
    earlier = (at[:, None] < at[None, :]).astype(BF)
    inside = jnp.dot(lanes.astype(BF), earlier, preferred_element_type=F32).astype(jnp.int32)
    totals = jnp.sum(lanes, axis=1).reshape(NUMBERS, -1)
    first = before(jnp.sum(totals, axis=1))[:, None] + before(totals)
    rank = inside.reshape(NUMBERS, -1, HEAD) + first[:, :, None]
    rank = jnp.sum(which * rank.reshape(NUMBERS, entries), axis=0)
    moved = (rank[None, :] == jnp.arange(entries, dtype=jnp.int32)[:, None]).astype(BF)
    return tuple(
        jnp.dot(moved, memory[index], preferred_element_type=F32).astype(BF) for index in range(2)
    )


def columns(matrix, sizes):
    pieces, at = [], 0
    for size in sizes:
        pieces.append(matrix[:, at : at + size])
        at += size
    return pieces


def dot_tn(a, b):
    return lax.dot_general(a, b, (((0,), (0,)), ((), ())), preferred_element_type=F32)


FEED = 256


def inverse_rms(values):
    return lax.rsqrt(jnp.mean(values * values, axis=-1, keepdims=True) + EPS)


def norm_back(values, gain, grad):
    inverse = inverse_rms(values)
    scaled = grad * gain
    mean = jnp.mean(scaled * values, axis=-1, keepdims=True)
    grad_gain = jnp.sum(grad * values * inverse, axis=0, keepdims=True)
    return inverse * scaled - values * (inverse * inverse * inverse) * mean, grad_gain


def feed_kernel(att, stream, out_w, gain, gate_w, up_w, down_w, result, mixed, normed, gate, up):
    step = pl.program_id(0)

    @pl.when(step == 0)
    def _():
        both = stream[...] + dot_nn(att[...], out_w[...])
        mixed[...] = both
        normed[...] = (both * inverse_rms(both) * gain[...]).astype(BF)
        result[...] = both

    gated = dot_nn(normed[...], gate_w[...])
    raised = dot_nn(normed[...], up_w[...])
    gate[...] = gated
    up[...] = raised
    activated = (gated * jax.nn.sigmoid(gated) * raised).astype(BF)
    result[...] += dot_nn(activated, down_w[...])


def feed(attended, stream, out_w, gain, gate_up_w, down_w):
    rows, width = stream.shape
    ff = down_w.shape[0]
    steps = ff // FEED
    part = pl.BlockSpec((rows, FEED), lambda f: (0, f))
    whole = jax.ShapeDtypeStruct((rows, width), F32)
    wide = jax.ShapeDtypeStruct((rows, ff), F32)
    return pl.pallas_call(
        feed_kernel,
        name="feed",
        grid=(steps,),
        in_specs=[
            VMEM, VMEM, VMEM, VMEM,
            pl.BlockSpec((width, FEED), lambda f: (0, f)),
            pl.BlockSpec((width, FEED), lambda f: (0, steps + f)),
            pl.BlockSpec((FEED, width), lambda f: (f, 0)),
        ],
        out_specs=(VMEM, VMEM, VMEM, part, part),
        out_shape=(whole, whole, jax.ShapeDtypeStruct((rows, width), BF), wide, wide),
        compiler_params=pltpu.CompilerParams(vmem_limit_bytes=ROOM),
    )(attended, stream, out_w, gain, gate_up_w, gate_up_w, down_w)


def feed_back_kernel(
    grad_new, gate, up, normed, mixed, gain, att, out_w, gate_w, up_w, down_w,
    gate_g, up_g, down_g, grad_mixed, grad_att, out_g, gain_g, branch, normed_t, total,
):
    step = pl.program_id(0)

    @pl.when(step == 0)
    def _():
        branch[...] = grad_new[...].astype(BF)
        normed_t[...] = turned(normed[...])
        total[...] = jnp.zeros_like(total)

    gated, raised = gate[...], up[...]
    sig = jax.nn.sigmoid(gated)
    swish = gated * sig
    grad_act = dot_nt(branch[...], down_w[...])
    down_g[...] = dot_tn((swish * raised).astype(BF), branch[...]).astype(BF)
    grad_gate = (grad_act * raised * sig * (1.0 + gated * (1.0 - sig))).astype(BF)
    grad_up = (grad_act * swish).astype(BF)
    gate_g[...] = dot_nn(normed_t[...], grad_gate).astype(BF)
    up_g[...] = dot_nn(normed_t[...], grad_up).astype(BF)
    total[...] += dot_nt(grad_gate, gate_w[...]) + dot_nt(grad_up, up_w[...])

    @pl.when(step == pl.num_programs(0) - 1)
    def _():
        back, grad_gain = norm_back(mixed[...], gain[...], total[...])
        both = grad_new[...] + back
        grad_mixed[...] = both
        gain_g[...] = grad_gain
        low = both.astype(BF)
        grad_att[...] = dot_nt(low, out_w[...]).astype(BF)
        out_g[...] = dot_tn(att[...], low).astype(BF)


def feed_back(grad_new, weights, kept):
    gain_a, qkv_w, out_w, gain, gate_up_w, down_w = weights
    attended, mixed, normed, gate, up = kept[7:]
    rows, width = grad_new.shape
    ff = down_w.shape[0]
    steps = ff // FEED
    part = pl.BlockSpec((rows, FEED), lambda f: (0, f))
    columns_of = pl.BlockSpec((width, FEED), lambda f: (0, f))
    rows_of = pl.BlockSpec((FEED, width), lambda f: (f, 0))

    def shape(a, b, kind=BF):
        return jax.ShapeDtypeStruct((a, b), kind)

    return pl.pallas_call(
        feed_back_kernel,
        name="feed_back",
        grid=(steps,),
        in_specs=[
            VMEM, part, part, VMEM, VMEM, VMEM, VMEM, VMEM,
            columns_of, pl.BlockSpec((width, FEED), lambda f: (0, steps + f)), rows_of,
        ],
        out_specs=(columns_of, columns_of, rows_of, VMEM, VMEM, VMEM, VMEM),
        out_shape=(
            shape(width, ff), shape(width, ff), shape(ff, width),
            shape(rows, width, F32), shape(rows, width), shape(width, width), shape(1, width, F32),
        ),
        scratch_shapes=[
            pltpu.VMEM((rows, width), BF), pltpu.VMEM((width, rows), BF), pltpu.VMEM((rows, width), F32),
        ],
        compiler_params=pltpu.CompilerParams(vmem_limit_bytes=ROOM),
    )(grad_new, gate, up, normed, mixed, gain, attended, out_w, gate_up_w, gate_up_w, down_w)


def project_kernel(grad_mixed, stream, gain, normed, grad_qkv, qkv_w, qkv_g, grad_stream, gain_g, normed_t, total):
    step = pl.program_id(0)

    @pl.when(step == 0)
    def _():
        normed_t[...] = turned(normed[...])
        total[...] = jnp.zeros_like(total)

    qkv_g[...] = dot_nn(normed_t[...], grad_qkv[...]).astype(BF)
    total[...] += dot_nt(grad_qkv[...], qkv_w[...])

    @pl.when(step == pl.num_programs(0) - 1)
    def _():
        back, grad_gain = norm_back(stream[...], gain[...], total[...])
        grad_stream[...] = grad_mixed[...] + back
        gain_g[...] = grad_gain


def projections_back(grad_mixed, grad_qkv, weights, kept):
    gain, qkv_w = weights[:2]
    stream, normed = kept[:2]
    rows, width = stream.shape
    size = 512
    part = pl.BlockSpec((width, size), lambda f: (0, f))
    grad_qkv_w, grad_stream, grad_gain = pl.pallas_call(
        project_kernel,
        name="projections_back",
        grid=(grad_qkv.shape[1] // size,),
        in_specs=[VMEM, VMEM, VMEM, VMEM, pl.BlockSpec((rows, size), lambda f: (0, f)), part],
        out_specs=(part, VMEM, VMEM),
        out_shape=(
            jax.ShapeDtypeStruct(qkv_w.shape, BF),
            jax.ShapeDtypeStruct((rows, width), F32),
            jax.ShapeDtypeStruct((1, width), F32),
        ),
        scratch_shapes=[pltpu.VMEM((width, rows), BF), pltpu.VMEM((rows, width), F32)],
        compiler_params=pltpu.CompilerParams(vmem_limit_bytes=ROOM),
    )(grad_mixed, stream, gain, normed, grad_qkv, qkv_w)
    return grad_stream, grad_gain, grad_qkv_w


def layer(stream, normed, heads, qkv_w, gains, to_rows, memory, bounds, ranges):
    gain_a, gain_b = gains
    q, k, v = heads
    out, stat = attend(q, k, v, memory, bounds, ranges)
    attended, out_w, gate_up_w, down_w = to_rows(out)
    result, mixed, normed_ff, gate, up = feed(attended, stream, out_w, gain_b, gate_up_w, down_w)
    weights = (gain_a, qkv_w, out_w, gain_b, gate_up_w, down_w)
    kept = (stream, normed, q, k, v, out, stat, attended, mixed, normed_ff, gate, up)
    return result, weights, kept


def gain_columns(gains):
    stacked = jnp.stack(gains, axis=1)
    return jnp.pad(stacked, ((0, 0), (0, HEAD - len(gains))))


def pair_rows(own, other, core):
    rows, width = own.shape
    both = jnp.where(core == 0, jnp.stack((own, other)), jnp.stack((other, own)))
    return lax.dynamic_slice_in_dim(both.reshape(2 * rows, width), core * (width // 2), width // 2, 1)


def head_local(
    tokens, token_docs, memory_docs, memory_resets, memory_keys, memory_values,
    attn_gain1, query_weight1, key_weight1, value_weight1, out_weight1,
    ffn_gain1, gate_weight1, up_weight1, down_weight1,
    attn_gain2, second_query_weight, key_weight2, value_weight2, out_weight2,
    ffn_gain2, gate_weight2, up_weight2, down_weight2, cotangent,
):
    count, width = query_weight1.shape
    ff = gate_weight1.shape[1]
    each = down_weight1.shape[0]
    core = lax.rem(lax.axis_index("key"), 2)
    seg = lax.axis_index("key") // LOCAL
    gains = gain_columns((attn_gain1, ffn_gain1, attn_gain2, ffn_gain2))
    qkv1 = jnp.concatenate((query_weight1, key_weight1, value_weight1), axis=1)
    qkv2 = jnp.concatenate((second_query_weight, key_weight2, value_weight2), axis=1)
    gate_up1 = jnp.concatenate((gate_weight1, up_weight1), axis=1)
    gate_up2 = jnp.concatenate((gate_weight2, up_weight2), axis=1)
    downs = jnp.concatenate((down_weight1, down_weight2), axis=0)
    docs = jnp.concatenate((token_docs, memory_docs), axis=0)
    pairs = PairBlocks(2 * each, width // 2)

    def own(matrix):
        return RowBlocks(count, matrix.shape[1])

    def gather(matrix):
        return Gather(matrix, own(matrix))

    other = hop(downs, "core")
    down1 = pair_rows(down_weight1, other[:each], core)
    down2 = pair_rows(down_weight2, other[each:], core)
    rest2 = jnp.concatenate((gate_up2, out_weight2), axis=1)
    front, (docs,), (mk,), (mv,), (gu1_w,), (down1_w,), (out1_w,), (qkv2_w,) = exchange(
        "front", 1,
        [Front(tokens, qkv1, own(qkv1), gains, own(gains), 3), Docs(docs),
         later(Memory(memory_keys), 1), later(Memory(memory_values), 7),
         later(gather(gate_up1), 2), later(Gather(down1, pairs), 2),
         later(gather(out_weight1), 2), later(gather(qkv2), 2)],
    )
    qkv1_w, gains, rows, normed1, *heads1 = front
    own_docs = lax.dynamic_index_in_dim(docs, seg, 0, keepdims=False)
    own_mem_docs = lax.dynamic_index_in_dim(docs, seg + 2, 0, keepdims=False)
    reset = lax.dynamic_index_in_dim(memory_resets, seg, 0, keepdims=False)
    bounds, ranges = mask_ranges(own_docs, own_mem_docs, reset)
    gains = [gains[:, i].astype(F32)[None] for i in range(4)]
    hops = {}
    heads1, shards = join(heads1, (rest2, down2))
    hops["rest"] = [gather_column(shard) for shard in shards]

    def rows1(out):
        ((attended,),) = exchange("to_rows_1", 3, [Swap([out], False)])
        return attended, out1_w, gu1_w, down1_w

    def rows2(out):
        out, (rest, down) = join(out, hops["rest"])
        (attended,), (gate_up_w, out_w), (down_w,) = exchange(
            "to_rows_2", 5,
            [Swap([out], False), Assemble(rest, [RowBlocks(count, 2 * ff), RowBlocks(count, width)]),
             Assemble(down, [pairs])],
        )
        attended, cot = join(attended, cotangent)
        hops["cot"] = rows_hops(cot)
        return attended, out_w, gate_up_w, down_w

    middle, weights1, kept1 = layer(
        rows.astype(F32), normed1, heads1, qkv1_w, (gains[0], gains[1]), rows1, None, bounds, ranges
    )
    middle, rest = join(middle, hops["rest"])
    hops["rest"] = [(column, hop(column, "a"), hop(column, "b")) for column in rest]
    normed2 = (middle * inverse_rms(middle) * gains[2]).astype(BF)
    qkv = jnp.dot(normed2, qkv2_w, preferred_element_type=F32).astype(BF)
    (heads2,) = exchange("to_heads_2", 4, [Swap([qkv], True)])
    heads2, firsts = join(heads2, [group[1] for group in hops["rest"]])
    hops["rest"] = [
        (group[0], first, group[2], hop(first, "b")) for group, first in zip(hops["rest"], firsts)
    ]
    memory = sort_memory((mk, mv), own_mem_docs)
    result, weights2, kept2 = layer(
        middle, normed2, heads2, qkv2_w, (gains[2], gains[3]), rows2, memory, bounds, ranges
    )
    cot = hops["cot"]
    output = chunk_hops(result.astype(BF))

    def pair_sum(total):
        half = lax.dynamic_slice_in_dim(total, core * each, each, 0)
        other = hop(lax.dynamic_slice_in_dim(total, (1 - core) * each, each, 0), "core")
        return jnp.where(
            core == 0, jnp.concatenate((half, other), 1), jnp.concatenate((other, half), 1)
        )

    shapes = ((count, ff), (count, ff), (count, width), pairs.shape)

    def feed_sums(gate_g, up_g, down_g, out_g):
        return CoreSums((gate_g, own(gate_g)), (up_g, own(up_g)), (out_g, own(out_g)), (down_g, pairs))

    gate_g2, up_g2, down_g2, grad_mixed, grad_att, out_g2, gain_b2 = feed_back(
        cot.astype(F32), weights2, kept2
    )
    (grad_out,), sums2 = exchange(
        "back_to_heads_2", 6,
        [Swap([grad_att], True), feed_sums(gate_g2, up_g2, down_g2, out_g2)],
    )
    sums2 = scatter_second(sums2)
    q, k, v, out, stat = kept2[2:7]
    grads = attend_back(q, k, v, memory, bounds, ranges, out, stat, grad_out)
    ((grad_qkv,),) = exchange("back_to_rows_2", 7, [Swap(list(grads), False)])
    grad_qkv, (sums2, output) = join(grad_qkv, (sums2, output))
    sums2 = scatter_first(sums2)
    grad_middle, gain_a2, qkv_g2 = projections_back(grad_mixed, grad_qkv, weights2, kept2)
    (qkv_s2,) = exchange("projection_sums_2", 12, [CoreSums((qkv_g2, own(qkv_g2)))])
    grad_middle, (sums2, qkv_s2) = join(grad_middle, (sums2, qkv_s2))
    sums2 = scatter_z(sums2)
    qkv_s2 = scatter_second(qkv_s2)

    gate_g1, up_g1, down_g1, grad_mixed, grad_att, out_g1, gain_b1 = feed_back(
        grad_middle, weights1, kept1
    )
    grad_att, qkv_s2 = join(grad_att, qkv_s2)
    qkv_s2 = scatter_first(qkv_s2)
    (grad_out,), sums1 = exchange(
        "back_to_heads_1", 8,
        [Swap([grad_att], True), feed_sums(gate_g1, up_g1, down_g1, out_g1)],
    )
    grad_out, (sums2, qkv_s2) = join(grad_out, (sums2, qkv_s2))
    qkv_s2 = scatter_z(qkv_s2)
    sums1 = scatter_second(sums1)
    q, k, v, out, stat = kept1[2:7]
    grads = attend_back(q, k, v, None, bounds, ranges, out, stat, grad_out)
    ((grad_qkv,),) = exchange("back_to_rows_1", 9, [Swap(list(grads), False)])
    grad_qkv, (sums1, qkv_s2) = join(grad_qkv, (sums1, qkv_s2))
    sums1 = scatter_first(sums1)
    grad_rows, gain_a1, qkv_g1 = projections_back(grad_mixed, grad_qkv, weights1, kept1)
    gain_grads = gain_columns([g[0] for g in (gain_a1, gain_b1, gain_a2, gain_b2)]).astype(BF)
    here, second, first = sums1
    (grad_tokens,), (gate_s1, up_s1, out_s1, down_s1), (q_s1,), (k_s1,), (v_s1,), (gain_s,) = exchange(
        "back_to_owners", 10,
        [Chunks(grad_rows.astype(BF)), LineSums((here, second, first), shapes, ((0,), (1,), (2, 3)))]
        + [Scatter(qkv_g1, ColumnBlocks(count, width, i), i) for i in range(3)]
        + [Scatter(gain_grads, own(gain_grads))],
    )
    gate_s2, up_s2, out_s2, down_s2 = unpack(scatter_end(sums2), shapes)
    (qkv_s2,) = unpack(scatter_end(qkv_s2), ((count, 3 * width),))
    q_s2, k_s2, v_s2 = columns(qkv_s2, (width,) * 3)
    return (
        output, grad_tokens.astype(F32),
        gain_s[:, 0], q_s1, k_s1, v_s1, out_s1, gain_s[:, 1], gate_s1, up_s1, pair_sum(down_s1),
        gain_s[:, 2], q_s2, k_s2, v_s2, out_s2, gain_s[:, 3], gate_s2, up_s2, pair_sum(down_s2),
    )


def solution(mesh):
    in_specs = (
        P("grp", "key", None),
        P("grp", "key"),
        P("grp", "key"),
        P("grp"),
        P("grp", "key", None),
        P("grp", "key", None),
        P(("grp", "key")),
        P(("grp", "key"), None),
        P(("grp", "key"), None),
        P(("grp", "key"), None),
        P(("grp", "key"), None),
        P(("grp", "key")),
        P(("grp", "key"), None),
        P(("grp", "key"), None),
        P(("grp", "key"), None),
        P(("grp", "key")),
        P(("grp", "key"), None),
        P(("grp", "key"), None),
        P(("grp", "key"), None),
        P(("grp", "key"), None),
        P(("grp", "key")),
        P(("grp", "key"), None),
        P(("grp", "key"), None),
        P(("grp", "key"), None),
        P("grp", "key", None),
    )
    out_specs = (
        P("grp", "key", None),
        P("grp", "key", None),
        P(("grp", "key")),
        P(("grp", "key"), None),
        P(("grp", "key"), None),
        P(("grp", "key"), None),
        P(("grp", "key"), None),
        P(("grp", "key")),
        P(("grp", "key"), None),
        P(("grp", "key"), None),
        P(("grp", "key"), None),
        P(("grp", "key")),
        P(("grp", "key"), None),
        P(("grp", "key"), None),
        P(("grp", "key"), None),
        P(("grp", "key"), None),
        P(("grp", "key")),
        P(("grp", "key"), None),
        P(("grp", "key"), None),
        P(("grp", "key"), None),
    )
    body = head_local if dict(mesh.shape) == {"grp": 4, "key": HEADS} else gathered_local
    return jax.shard_map(body, mesh=mesh, in_specs=in_specs, out_specs=out_specs, check_vma=False)
```

```python
import functools

import jax
import jax.numpy as jnp
from jax import lax
from jax.experimental import pallas as pl
from jax.experimental.pallas import tpu as pltpu
from jax.sharding import PartitionSpec as P

HEADS = 8


EPS = 1e-05
NEG = -1e30


def norm_forward(values, gain_vec):
    inverse = lax.rsqrt(jnp.mean(values * values, axis=-1, keepdims=True) + EPS)
    return (values * inverse * gain_vec, inverse)


def norm_backward(values, gain_vec, inverse, grad_normed):
    grad_gain = jnp.sum(grad_normed * values * inverse, axis=(0, 1))
    scaled = grad_normed * gain_vec
    grad_values = inverse * scaled - values * inverse**3 * jnp.mean(
        scaled * values, axis=-1, keepdims=True
    )
    return (grad_values, grad_gain)


def project(input_operand, weight_matrix):
    return jnp.dot(input_operand, weight_matrix, preferred_element_type=jnp.float32)


def project_back(gradient_row_block, weight_matrix):
    return jnp.einsum(
        "tzu,ku->tzk", gradient_row_block, weight_matrix, preferred_element_type=jnp.float32
    )


def outer_sum(input_arrays, gradient_reduced_precision):
    return jnp.einsum(
        "zhp,zhv->pv", input_arrays, gradient_reduced_precision, preferred_element_type=jnp.float32
    )


def split_heads(rows):
    return rows.reshape(rows.shape[0], rows.shape[1], HEADS, rows.shape[2] // HEADS)


def fetch_weights(shards):
    return (
        lax.all_gather(shards[0], ("grp", "key"), axis=0, tiled=True),
        lax.all_gather(shards[1], ("grp", "key"), axis=0, tiled=True),
        lax.all_gather(shards[2], ("grp", "key"), axis=0, tiled=True),
        lax.all_gather(shards[3], ("grp", "key"), axis=0, tiled=True),
        lax.all_gather(shards[4], ("grp", "key"), axis=0, tiled=True),
        lax.all_gather(shards[5], ("grp", "key"), axis=0, tiled=True),
        lax.all_gather(shards[6], ("grp", "key"), axis=0, tiled=True),
        lax.all_gather(shards[7], ("grp", "key"), axis=0, tiled=True),
        lax.all_gather(shards[8], ("grp", "key"), axis=0, tiled=True),
    )


def refetch_weights(shards):
    return (
        lax.all_gather(shards[0], ("grp", "key"), axis=0, tiled=True),
        lax.all_gather(shards[1], ("grp", "key"), axis=0, tiled=True),
        lax.all_gather(shards[2], ("grp", "key"), axis=0, tiled=True),
        lax.all_gather(shards[3], ("grp", "key"), axis=0, tiled=True),
        lax.all_gather(shards[4], ("grp", "key"), axis=0, tiled=True),
        lax.all_gather(shards[5], ("grp", "key"), axis=0, tiled=True),
        lax.all_gather(shards[6], ("grp", "key"), axis=0, tiled=True),
        lax.all_gather(shards[7], ("grp", "key"), axis=0, tiled=True),
        lax.all_gather(shards[8], ("grp", "key"), axis=0, tiled=True),
    )


def reduce_gradient_sums(terms):
    return (
        lax.psum_scatter(terms[0], ("grp", "key"), scatter_dimension=0, tiled=True),
        lax.psum_scatter(terms[1], ("grp", "key"), scatter_dimension=0, tiled=True),
        lax.psum_scatter(terms[2], ("grp", "key"), scatter_dimension=0, tiled=True),
        lax.psum_scatter(terms[3], ("grp", "key"), scatter_dimension=0, tiled=True),
        lax.psum_scatter(terms[4], ("grp", "key"), scatter_dimension=0, tiled=True),
        lax.psum_scatter(terms[5], ("grp", "key"), scatter_dimension=0, tiled=True),
        lax.psum_scatter(terms[6], ("grp", "key"), scatter_dimension=0, tiled=True),
        lax.psum_scatter(terms[7], ("grp", "key"), scatter_dimension=0, tiled=True),
        lax.psum_scatter(terms[8], ("grp", "key"), scatter_dimension=0, tiled=True),
    )


def head_scores(query_all, key_block, allowed):
    head_size = query_all.shape[2] // HEADS
    raw_scores = jnp.einsum(
        "sqhd,skhd->shqk",
        split_heads(query_all),
        split_heads(key_block),
        preferred_element_type=jnp.float32,
    ) * head_size ** (-0.5)
    return jnp.where(allowed[:, None], raw_scores, NEG)


def attend_forward(query_all, key_block, value_block, allowed):
    scores = head_scores(query_all, key_block, allowed)
    row_top = lax.pmax(jnp.max(scores, axis=3).astype(jnp.bfloat16), "key").astype(jnp.float32)
    exp_scores = jnp.where(allowed[:, None], jnp.exp(scores - row_top[..., None]), 0.0)
    row_total = lax.psum(jnp.sum(exp_scores, axis=3).astype(jnp.bfloat16), "key").astype(
        jnp.float32
    )
    probability = exp_scores / row_total[..., None]
    partial_value = jnp.einsum(
        "shqk,skhd->sqhd",
        probability.astype(jnp.bfloat16),
        split_heads(value_block),
        preferred_element_type=jnp.float32,
    )
    partial_value = partial_value.reshape(query_all.shape)
    attended = lax.psum_scatter(
        partial_value.astype(jnp.bfloat16), "key", scatter_dimension=1, tiled=True
    ).astype(jnp.float32)
    return (attended, row_top, row_total)


def layer_forward(stream, full_weights, allowed, extra_keys, extra_values):
    gain_a, query_w, key_w, value_w, out_w, gain_b, gate_w, up_w, down_w = full_weights
    normed, first_inverse_factor = norm_forward(stream, gain_a.astype(jnp.float32))
    normed_low = normed.astype(jnp.bfloat16)
    query_low = project(normed_low, query_w).astype(jnp.bfloat16)
    key_low = project(normed_low, key_w).astype(jnp.bfloat16)
    value_low = project(normed_low, value_w).astype(jnp.bfloat16)
    query_all = lax.all_gather(query_low, "key", axis=1, tiled=True)
    if extra_keys is None:
        key_block = key_low
        value_block = value_low
    else:
        key_block = jnp.concatenate((key_low, extra_keys), axis=1)
        value_block = jnp.concatenate((value_low, extra_values), axis=1)
    attended, row_top, row_total = attend_forward(query_all, key_block, value_block, allowed)
    attended_low = attended.astype(jnp.bfloat16)
    mixed_stream = stream + project(attended_low, out_w)
    normed_ff, inverse_b = norm_forward(mixed_stream, gain_b.astype(jnp.float32))
    normed_ff_low = normed_ff.astype(jnp.bfloat16)
    gate_value = project(normed_ff_low, gate_w)
    up_value = project(normed_ff_low, up_w)
    activated_low = (gate_value * jax.nn.sigmoid(gate_value) * up_value).astype(jnp.bfloat16)
    result = mixed_stream + project(activated_low, down_w)
    kept_state = (
        stream,
        first_inverse_factor,
        normed_low,
        key_block,
        value_block,
        query_all,
        row_top,
        row_total,
        attended_low,
        mixed_stream,
        inverse_b,
        normed_ff_low,
        gate_value,
        up_value,
        activated_low,
    )
    return (result, kept_state)


def layer_backward(grad_result, full_weights, kept_state, allowed):
    gain_a, query_w, key_w, value_w, out_w, gain_b, gate_w, up_w, down_w = full_weights
    (
        stream,
        first_inverse_factor,
        normed_low,
        key_block,
        value_block,
        query_all,
        row_top,
        row_total,
        attended_low,
        mixed_stream,
        inverse_b,
        normed_ff_low,
        gate_value,
        up_value,
        activated_low,
    ) = kept_state
    own_rows = stream.shape[1]
    branch_low = grad_result.astype(jnp.bfloat16)
    grad_down = outer_sum(activated_low, branch_low)
    grad_act = project_back(branch_low, down_w)
    sigmoid_gate = jax.nn.sigmoid(gate_value)
    grad_gate = (
        grad_act * up_value * sigmoid_gate * (1.0 + gate_value * (1.0 - sigmoid_gate))
    ).astype(jnp.bfloat16)
    grad_up_low = (grad_act * gate_value * sigmoid_gate).astype(jnp.bfloat16)
    grad_gate_w = outer_sum(normed_ff_low, grad_gate)
    grad_up_w = outer_sum(normed_ff_low, grad_up_low)
    grad_normed_ff = project_back(grad_gate, gate_w) + project_back(grad_up_low, up_w)
    grad_mixed_norm, grad_gain_b = norm_backward(
        mixed_stream, gain_b.astype(jnp.float32), inverse_b, grad_normed_ff
    )
    grad_mixed = grad_result + grad_mixed_norm
    attn_low = grad_mixed.astype(jnp.bfloat16)
    grad_out_w = outer_sum(attended_low, attn_low)
    grad_attended = project_back(attn_low, out_w).astype(jnp.bfloat16)
    grad_all = lax.all_gather(grad_attended, "key", axis=1, tiled=True)
    scores = head_scores(query_all, key_block, allowed)
    probability = (
        jnp.where(allowed[:, None], jnp.exp(scores - row_top[..., None]), 0.0)
        / row_total[..., None]
    )
    grad_heads = split_heads(grad_all)
    grad_probs = jnp.einsum(
        "sqhd,skhd->shqk", grad_heads, split_heads(value_block), preferred_element_type=jnp.float32
    )
    row_delta = lax.psum(
        jnp.sum(probability * grad_probs, axis=3).astype(jnp.bfloat16), "key"
    ).astype(jnp.float32)
    grad_scores = (probability * (grad_probs - row_delta[..., None])).astype(jnp.bfloat16)
    score_scale = (query_all.shape[2] // HEADS) ** (-0.5)
    query_part = (
        jnp.einsum(
            "shqk,skhd->sqhd",
            grad_scores,
            split_heads(key_block),
            preferred_element_type=jnp.float32,
        ).reshape(query_all.shape)
        * score_scale
    )
    grad_query = lax.psum_scatter(
        query_part.astype(jnp.bfloat16), "key", scatter_dimension=1, tiled=True
    )
    own_scores = grad_scores[..., :own_rows]
    grad_key = (
        jnp.einsum(
            "shqk,sqhd->skhd",
            own_scores,
            split_heads(query_all),
            preferred_element_type=jnp.float32,
        ).reshape(stream.shape)
        * score_scale
    ).astype(jnp.bfloat16)
    own_probs = probability.astype(jnp.bfloat16)[..., :own_rows]
    grad_value = (
        jnp.einsum("shqk,sqhd->skhd", own_probs, grad_heads, preferred_element_type=jnp.float32)
        .reshape(stream.shape)
        .astype(jnp.bfloat16)
    )
    grad_query_w = outer_sum(normed_low, grad_query)
    grad_key_w = outer_sum(normed_low, grad_key)
    grad_value_w = outer_sum(normed_low, grad_value)
    grad_normed = (
        project_back(grad_query, query_w)
        + project_back(grad_key, key_w)
        + project_back(grad_value, value_w)
    )
    grad_stream_norm, grad_gain_a = norm_backward(
        stream, gain_a.astype(jnp.float32), first_inverse_factor, grad_normed
    )
    grad_stream = grad_mixed + grad_stream_norm
    terms = (
        grad_gain_a,
        grad_query_w,
        grad_key_w,
        grad_value_w,
        grad_out_w,
        grad_gain_b,
        grad_gate_w,
        grad_up_w,
        grad_down,
    )
    return (grad_stream, terms)


def gathered_local(
    tokens,
    token_docs,
    memory_docs,
    memory_resets,
    memory_keys,
    memory_values,
    attn_gain1,
    query_weight1,
    key_weight1,
    value_weight1,
    out_weight1,
    ffn_gain1,
    gate_weight1,
    up_weight1,
    down_weight1,
    attn_gain2,
    second_query_weight,
    key_weight2,
    value_weight2,
    out_weight2,
    ffn_gain2,
    gate_weight2,
    up_weight2,
    down_weight2,
    cotangent,
):
    first_shards = (
        attn_gain1,
        query_weight1,
        key_weight1,
        value_weight1,
        out_weight1,
        ffn_gain1,
        gate_weight1,
        up_weight1,
        down_weight1,
    )
    second_shards = (
        attn_gain2,
        second_query_weight,
        key_weight2,
        value_weight2,
        out_weight2,
        ffn_gain2,
        gate_weight2,
        up_weight2,
        down_weight2,
    )
    docs_all = lax.all_gather(token_docs, "key", axis=1, tiled=True)
    own_rows = tokens.shape[1]
    query_place = jnp.arange(docs_all.shape[1], dtype=jnp.int32)
    key_place = lax.axis_index("key") * own_rows + jnp.arange(own_rows, dtype=jnp.int32)
    local_allowed = (key_place[None, None, :] <= query_place[None, :, None]) & (
        token_docs[:, None, :] == docs_all[:, :, None]
    )
    memory_allowed = (memory_docs[:, None, :] == docs_all[:, :, None]) & (
        memory_resets[:, None, None] == 0
    )
    both_allowed = jnp.concatenate((local_allowed, memory_allowed), axis=2)
    stream = tokens.astype(jnp.float32)
    first_full = fetch_weights(first_shards)
    middle, first_state = layer_forward(stream, first_full, local_allowed, None, None)
    second_full = fetch_weights(second_shards)
    result, second_state = layer_forward(
        middle, second_full, both_allowed, memory_keys, memory_values
    )
    second_full = refetch_weights(second_shards)
    grad_middle, second_terms = layer_backward(
        cotangent.astype(jnp.float32), second_full, second_state, both_allowed
    )
    second_grads = reduce_gradient_sums(second_terms)
    first_full = refetch_weights(first_shards)
    grad_stream, first_terms = layer_backward(grad_middle, first_full, first_state, local_allowed)
    first_grads = reduce_gradient_sums(first_terms)
    return (
        result.astype(jnp.bfloat16),
        grad_stream,
        first_grads[0],
        first_grads[1],
        first_grads[2],
        first_grads[3],
        first_grads[4],
        first_grads[5],
        first_grads[6],
        first_grads[7],
        first_grads[8],
        second_grads[0],
        second_grads[1],
        second_grads[2],
        second_grads[3],
        second_grads[4],
        second_grads[5],
        second_grads[6],
        second_grads[7],
        second_grads[8],
    )


MESH = pl.DeviceIdType.MESH
ANY = pl.BlockSpec(memory_space=pl.ANY)
VMEM = pl.BlockSpec(memory_space=pltpu.VMEM)
LOG2E = 1.4426950408889634
BLOCK = 512
QUERIES = 512
ROOM = 60 * 2**20
LOCAL = 4
HEAD = 128
PAIR = 2 * HEAD
BF = jnp.bfloat16
F32 = jnp.float32


SEND = pltpu.SemaphoreType.DMA


def flip(value, change):
    return lax.rem(value + change, 2)


class Place:
    def __init__(self):
        self.grp = lax.axis_index("grp")
        self.key = lax.axis_index("key")
        self.y, self.x = self.grp // 2, lax.rem(self.grp, 2)
        self.z, self.core = self.key // 2, lax.rem(self.key, 2)
        self.rank = lax.rem(self.key, LOCAL)
        self.seg = self.key // LOCAL

    def chip(self, da, db, dz, core):
        dx = da * (1 - core) + db * core
        dy = da * core + db * (1 - core)
        z = flip(self.z // 2, dz // 2) * 2 + flip(lax.rem(self.z, 2), lax.rem(dz, 2))
        return flip(self.y, dy) * 2 + flip(self.x, dx), z

    def device(self, da, db, dz):
        grp, z = self.chip(da, db, dz, self.core)
        return grp, z * 2 + self.core

    def sibling(self):
        return self.grp, self.z * 2 + 1 - self.core


def remote(src, dst, send, recv, target):
    return pltpu.make_async_remote_copy(
        src_ref=src, dst_ref=dst, send_sem=send, recv_sem=recv,
        device_id=target, device_id_type=MESH,
    )


def local(src, dst, sem):
    return pltpu.make_async_copy(src, dst, sem)


def span(index, size):
    return pl.ds(pl.multiple_of(index * size, size), size)


class RowBlocks:
    def __init__(self, rows, width):
        self.shape = (rows, width)

    def whole(self, chips):
        return (chips * 2 * self.shape[0], self.shape[1])

    def at(self, ref, chip, core):
        return ref.at[span((chip[0] * LOCAL + chip[1]) * 2 + core, self.shape[0]), :]


class PairBlocks(RowBlocks):
    def whole(self, chips):
        return (chips * self.shape[0], 2 * self.shape[1])

    def at(self, ref, chip, core):
        rows, width = self.shape
        return ref.at[span(chip[0] * LOCAL + chip[1], rows), span(core, width)]


class ColumnBlocks(RowBlocks):
    def __init__(self, rows, width, part):
        self.shape = (rows, width)
        self.part = part

    def at(self, ref, chip, core):
        rows, width = self.shape
        return ref.at[
            span((chip[0] * LOCAL + chip[1]) * 2 + core, rows), pl.ds(self.part * width, width)
        ]


class Swap:
    def __init__(self, arrays, to_heads):
        self.arrays = arrays
        self.to_heads = to_heads
        if to_heads:
            rows, width = arrays[0].shape
            self.parts = width // (LOCAL * PAIR)
            self.outs = [jax.ShapeDtypeStruct((rows * LOCAL, PAIR), BF)] * self.parts
        else:
            rows = arrays[0].shape[0] // LOCAL
            self.parts = len(arrays)
            self.outs = [jax.ShapeDtypeStruct((rows, self.parts * LOCAL * PAIR), BF)]
        self.rows = rows
        self.scratch = [SEND((self.parts, LOCAL)), SEND((self.parts, LOCAL)), SEND((self.parts,))]
        self.out_specs = [ANY] * len(self.outs)

    def run(self, at, ins, outs, scratch):
        send, recv, here = scratch

        def copy(part, k):
            target = lax.rem(at.rank + k, LOCAL)
            if self.to_heads:
                src = ins[0].at[:, span(part * LOCAL + target, PAIR)]
                dst = outs[part].at[span(at.rank, self.rows), :]
            else:
                src = ins[part].at[span(target, self.rows), :]
                dst = outs[0].at[:, span(part * LOCAL + at.rank, PAIR)]
            if k == 0:
                return local(src, dst, here.at[part])
            device = (at.grp, at.seg * LOCAL + target)
            return remote(src, dst, send.at[part, k], recv.at[part, k], device)

        every = [(part, k) for part in range(self.parts) for k in (2, 3, 1, 0)]
        for part, k in every:
            copy(part, k).start()
        yield
        yield "last"
        for part, k in every:
            copy(part, k).wait()


class Rows:
    def __init__(self, array):
        segs, rows, width = array.shape
        self.arrays = [array]
        self.rows = rows
        self.outs = [jax.ShapeDtypeStruct((segs * rows, width), array.dtype)]
        self.out_specs = [ANY]
        self.scratch = [SEND((2,)), SEND((2,)), SEND(())]

    def run(self, at, ins, outs, scratch):
        (src,), (dst,) = ins, outs
        send, recv, here = scratch
        chunk = lax.rem(at.key, 2)

        def part(index):
            return dst.at[span(index, self.rows), :]

        def out(seg):
            target = seg * LOCAL + at.key // 2
            return target, remote(
                src.at[seg], part(chunk), send.at[seg], recv.at[chunk], (at.grp, target)
            )

        for seg in range(2):
            target, copy = out(seg)
            pl.when(target != at.key)(copy.start)
            pl.when(target == at.key)(local(src.at[seg], part(chunk), here).start)
        yield
        yield "last"
        for seg in range(2):
            target, copy = out(seg)
            pl.when(target != at.key)(copy.wait_send)
        for index in range(2):
            owner = 2 * at.rank + index
            copy = remote(src.at[0], part(index), send.at[0], recv.at[index], (at.grp, owner))
            pl.when(owner != at.key)(copy.wait_recv)
            pl.when(owner == at.key)(local(src.at[0], part(index), here).wait)


class Chunks:
    def __init__(self, array):
        rows, width = array.shape
        self.arrays = [array]
        self.rows = rows // 2
        self.outs = [jax.ShapeDtypeStruct((2, rows // 2, width), array.dtype)]
        self.out_specs = [ANY]
        self.scratch = [SEND((2,)), SEND((2,)), SEND(())]

    def run(self, at, ins, outs, scratch):
        (src,), (dst,) = ins, outs
        send, recv, here = scratch

        def part(index):
            return src.at[pl.ds(index * self.rows, self.rows), :]

        def out(index):
            target = 2 * at.rank + index
            return target, remote(
                part(index), dst.at[at.seg], send.at[index], recv.at[at.seg], (at.grp, target)
            )

        for index in range(2):
            target, copy = out(index)
            pl.when(target != at.key)(copy.start)
            pl.when(target == at.key)(local(part(index), dst.at[at.seg], here).start)
        yield
        yield "last"
        for index in range(2):
            target, copy = out(index)
            pl.when(target != at.key)(copy.wait_send)
        for seg in range(2):
            owner = seg * LOCAL + at.key // 2
            copy = remote(part(0), dst.at[seg], send.at[0], recv.at[seg], (at.grp, owner))
            pl.when(owner != at.key)(copy.wait_recv)
            pl.when(owner == at.key)(local(part(0), dst.at[seg], here).wait)


class Memory:
    def __init__(self, array):
        self.arrays = [array]
        self.rows = array.shape[1]
        self.outs = [jax.ShapeDtypeStruct((2 * LOCAL * self.rows, PAIR), BF)]
        self.out_specs = [ANY]
        self.scratch = [SEND((2 * LOCAL,)), SEND((2 * LOCAL,)), SEND(())]

    def run(self, at, ins, outs, scratch):
        send, recv, here = scratch

        def copy(k):
            target = lax.rem(at.key + k, 2 * LOCAL)
            src = ins[0].at[target // LOCAL, :, span(lax.rem(target, LOCAL), PAIR)]
            dst = outs[0].at[span(at.key, self.rows), :]
            if k == 0:
                return local(src, dst, here)
            return remote(src, dst, send.at[k], recv.at[k], (at.grp, target))

        for k in range(2 * LOCAL):
            copy(k).start()
        yield
        yield "last"
        for k in range(2 * LOCAL):
            copy(k).wait()


class Docs:
    def __init__(self, array):
        rows, self.width = array.shape
        self.arrays = [array]
        self.outs = [jax.ShapeDtypeStruct((rows, 2 * LOCAL * self.width), array.dtype)]
        self.out_specs = [ANY]
        self.scratch = [SEND((2 * LOCAL,)), SEND((2 * LOCAL,)), SEND(())]

    def run(self, at, ins, outs, scratch):
        send, recv, here = scratch

        def copy(k):
            target = lax.rem(at.key + k, 2 * LOCAL)
            dst = outs[0].at[:, span(at.key, self.width)]
            if k == 0:
                return local(ins[0], dst, here)
            return remote(ins[0], dst, send.at[k], recv.at[k], (at.grp, target))

        for k in range(2 * LOCAL):
            copy(k).start()
        yield
        yield "last"
        for k in range(2 * LOCAL):
            copy(k).wait()


class Sibling:
    def __init__(self, array):
        self.arrays = [array]
        self.outs = [jax.ShapeDtypeStruct(array.shape, array.dtype)]
        self.out_specs = [ANY]
        self.scratch = [SEND(()), SEND(())]

    def run(self, at, ins, outs, scratch):
        copy = remote(ins[0], outs[0], scratch[0], scratch[1], at.sibling())
        copy.start()
        yield
        yield "last"
        copy.wait()


STEPS = [(da, db, dz) for db in range(2) for da in range(2) for dz in range(4)]


class Gather:
    def __init__(self, shards, blocks):
        self.arrays = list(shards)
        self.blocks = blocks
        self.outs = [jax.ShapeDtypeStruct(blocks.whole(4 * LOCAL), BF)]
        self.out_specs = [ANY]
        self.scratch = [SEND((36,)), SEND((36,)), SEND(())]
        self.scratch += [pltpu.VMEM(blocks.shape, BF), SEND((len(shards),))]

    def run(self, at, ins, outs, scratch):
        (whole,) = outs
        send, recv, here, shard, load = scratch
        core = at.core
        copies, begin = [], 0
        for index, src in enumerate(ins):
            cut = pl.ds(begin, src.shape[1])
            copies.append(local(src, shard.at[:, cut], load.at[index]))
            begin += src.shape[1]
        for copy_in in copies:
            copy_in.start()
        for copy_in in copies:
            copy_in.wait()

        def spot(step, of=core):
            return self.blocks.at(whole, at.chip(*step, of), of)

        def copy(step, slot, target):
            mine = isinstance(step[2], int) and step == (0, 0, 0)
            src = shard if mine else spot(step)
            return remote(src, spot(step), send.at[slot], recv.at[slot], target)

        def cross(step):
            da, db, dz = step
            return 20 + 8 * db + 4 * da + dz

        def first(dz):
            return copy((0, 0, dz), 8 + dz, at.device(1, 0, 0))

        def second(da, dz):
            return copy((da, 0, dz), 12 + 4 * da + dz, at.device(0, 1, 0))

        def across(step):
            return copy(step, cross(step), at.sibling())

        def arrived(step, slot):
            dst = spot(step)
            remote(dst, dst, send.at[slot], recv.at[slot], at.sibling()).wait_recv()

        inner = flip(at.z // 2, lax.rem(at.z, 2))
        near, turns = at.device(0, 0, 1), (1, 2 + inner, 3 - inner)
        far = at.device(0, 0, 3)
        inside = pl.when(inner == 1)

        def along_z(index):
            if index == 0:
                return remote(shard, spot((0, 0, 0)), send.at[0], recv.at[1], near)
            if index == 1:
                return remote(shard, spot((0, 0, 0)), send.at[1], recv.at[3], far)
            step, slot, device = {
                2: ((0, 0, 1), 2, far), 3: ((0, 0, 3), 2, near), 4: ((0, 0, 2), 3, near)
            }[index]
            return remote(spot(step), spot(step), send.at[index], recv.at[slot], device)

        mine = local(shard, spot((0, 0, 0)), here)
        mine.start()
        along_z(0).start()
        inside(along_z(1).start)
        first(0).start()
        second(0, 0).start()
        across((0, 0, 0)).start()
        yield
        for turn, dz in enumerate(turns):
            arrived((0, 0, dz), dz)
            inside(along_z((2, 3, 4)[turn]).start)
            first(dz).start()
            second(0, dz).start()
            across((0, 0, dz)).start()
            yield
        for dz in (0,) + turns:
            arrived((1, 0, dz), 8 + dz)
            second(1, dz).start()
            across((1, 0, dz)).start()
        yield
        for da in range(2):
            for dz in (0,) + turns:
                arrived((da, 1, dz), 12 + 4 * da + dz)
                across((da, 1, dz)).start()
        yield "last"
        for step in STEPS:
            dst = spot(step, 1 - core)
            slot = cross(step)
            remote(dst, dst, send.at[slot], recv.at[slot], at.sibling()).wait_recv()
        along_z(0).wait_send()
        for index in range(1, 5):
            inside(along_z(index).wait_send)
        for dz in range(4):
            first(dz).wait_send()
            for da in range(2):
                second(da, dz).wait_send()
        for step in STEPS:
            across(step).wait_send()
        mine.wait()


def tile_of(rows, width):
    sizes = [width // n for n in range(1, width // HEAD + 1) if width % (n * HEAD) == 0]
    return next((size for size in sizes if rows * size <= 32768), HEAD)


def add_into(dst, parts):
    rows, width = dst.shape
    tile = tile_of(rows, width)

    def one(cut):
        total = parts[0][:, cut].astype(F32)
        for part in parts[1:]:
            total += part[:, cut].astype(F32)
        dst[:, cut] = total.astype(dst.dtype)

    if tile == width:
        one(pl.ds(0, width))
    else:

        @pl.loop(0, width // tile)
        def _(t):
            one(pl.ds(pl.multiple_of(t * tile, tile), tile))


class Front:
    def __init__(self, tokens, shards, blocks, gains, gain_blocks, rest):
        self.rest = rest
        self.parts = [Gather(shards, blocks), Gather([gains], gain_blocks), Rows(tokens)]
        (rows,) = self.parts[2].outs
        rows, width = rows.shape
        columns = blocks.shape[1]
        qkv = jax.ShapeDtypeStruct((rows, columns), BF)
        self.swap = Swap([qkv], True)
        self.arrays = [array for part in self.parts for array in part.arrays]
        self.outs = [part.outs[0] for part in self.parts]
        self.outs += [jax.ShapeDtypeStruct((rows, width), BF)] + self.swap.outs
        self.out_specs = [ANY] * 3 + [VMEM] + self.swap.out_specs
        self.scratch = [s for part in self.parts for s in part.scratch] + self.swap.scratch
        self.scratch += [
            pltpu.VMEM((width, columns), BF),
            pltpu.VMEM((rows, width), BF),
            pltpu.VMEM(self.parts[1].outs[0].shape, BF),
            pltpu.VMEM((rows, columns), BF),
            SEND((3,)),
        ]

    def run(self, at, ins, outs, scratch):
        stages, rest, given = [], list(scratch), list(ins)
        for index, part in enumerate(self.parts):
            held = [rest.pop(0) for _ in part.scratch]
            taken = [given.pop(0) for _ in part.arrays]
            stages.append(part.run(at, taken, [outs[index]], held))
        swap_scratch = [rest.pop(0) for _ in self.swap.scratch]
        weights, tokens, gains, qkv, load = rest
        normed, swapped = outs[3], outs[4:]
        gathers, rows = stages[:2], stages[2]

        def step():
            for stage in gathers:
                next(stage)

        step()
        yield
        for _ in range(3):
            step()
        next(rows)
        yield
        step()
        step()
        for stage in stages:
            for _ in stage:
                pass
        copies = [
            local(src, dst, load.at[i])
            for i, (src, dst) in enumerate(zip((outs[2], outs[1], outs[0]), (tokens, gains, weights)))
        ]
        for copy in copies:
            copy.start()
        yield
        for copy in copies:
            copy.wait()
        values = tokens[...].astype(F32)
        gain = gains[...].astype(F32).T[0:1, :]
        normed[...] = (values * inverse_rms(values) * gain).astype(BF)
        tile = 512

        @pl.loop(0, qkv.shape[1] // tile)
        def _(t):
            cut = pl.ds(pl.multiple_of(t * tile, tile), tile)
            qkv[:, cut] = dot_nn(normed[...], weights[:, cut]).astype(BF)

        for _ in range(self.rest):
            yield
        swap = self.swap.run(at, [qkv], swapped, swap_scratch)
        next(swap)
        yield
        yield "last"
        for _ in swap:
            pass


class Assemble:
    def __init__(self, groups, blocks, pieces):
        self.arrays = list(groups)
        self.blocks = blocks
        self.pieces = pieces
        self.outs = [jax.ShapeDtypeStruct(b.whole(4 * LOCAL), groups[0].dtype) for b in blocks]
        self.out_specs = [ANY] * len(blocks)
        n = len(pieces)
        self.scratch = [SEND((n, 16)), SEND((n, 16)), SEND((n, 16)), SEND((16,))]
        self.scratch += [pltpu.VMEM((16,) + groups[0].shape[1:], groups[0].dtype)]

    def run(self, at, ins, outs, scratch):
        send, recv, here, load, held = scratch

        def fetch(group, dz):
            slot = group * 4 + dz
            return local(ins[group].at[dz], held.at[slot], load.at[slot])

        def copies(group, dz, core):
            slot = group * 4 + dz
            chip = at.chip(group % 2, group // 2, dz, core)
            for index, (matrix, row, rows, column, width, down, over) in enumerate(self.pieces):
                block = self.blocks[matrix].at(outs[matrix], chip, core)
                dst = block.at[pl.ds(row, rows), pl.ds(column, width)]
                src = held.at[slot, pl.ds(down, rows), pl.ds(over, width)]
                yield src, dst, index, slot

        def across(src, dst, index, slot):
            return remote(src, dst, send.at[index, slot], recv.at[index, slot], at.sibling())

        def own(src, dst, index, slot):
            return local(src, dst, here.at[index, slot])

        def every(do):
            for group in range(4):

                @pl.loop(0, 4)
                def _(dz):
                    do(group, dz)

        every(lambda group, dz: fetch(group, dz).start())
        yield

        def give(group, dz):
            fetch(group, dz).wait()
            for copy in copies(group, dz, at.core):
                across(*copy).start()
                own(*copy).start()

        every(give)
        yield "last"

        def end(group, dz):
            for copy in copies(group, dz, at.core):
                across(*copy).wait_send()
                own(*copy).wait()
            for copy in copies(group, dz, 1 - at.core):
                across(*copy).wait_recv()

        every(end)


class Sort:
    def __init__(self, rank, *arrays):
        self.arrays = [rank, *arrays]
        self.outs = [jax.ShapeDtypeStruct(array.shape, array.dtype) for array in arrays]
        self.out_specs = [VMEM] * len(arrays)
        self.scratch = [pltpu.VMEM(array.shape, array.dtype) for array in self.arrays]
        self.scratch += [SEND((len(self.arrays),))]

    def run(self, at, ins, outs, scratch):
        held, load = scratch[:-1], scratch[-1]
        copies = [local(src, dst, load.at[i]) for i, (src, dst) in enumerate(zip(ins, held))]
        for copy in copies:
            copy.start()
        yield
        for copy in copies:
            copy.wait()
        rank = held[0]
        entries = rank.shape[1]
        tile = BLOCK

        @pl.loop(0, entries // tile)
        def _(t):
            at_row = lax.broadcasted_iota(jnp.int32, (tile, entries), 0) + t * tile
            moved = jnp.where(rank[...] == at_row, 1.0, 0.0).astype(BF)
            for src, dst in zip(held[1:], outs):
                dst[pl.ds(pl.multiple_of(t * tile, tile), tile), :] = dot_nn(moved, src[...]).astype(BF)

        yield "last"


PACK = 16


class CoreSums:
    def __init__(self, *wholes):
        self.arrays = [whole for whole, _ in wholes]
        self.blocks = [blocks for _, blocks in wholes]
        shapes = [blocks.shape for blocks in self.blocks]
        self.width = sum(rows // PACK * width for rows, width in shapes)
        self.outs = [jax.ShapeDtypeStruct((n, PACK, self.width), BF) for n in (4, 4, 8)]
        self.out_specs = [ANY] * 3
        n = len(shapes)
        self.scratch = [pltpu.VMEM((16,) + shape, BF) for shape in shapes] * 2
        self.scratch += [pltpu.VMEM((16, PACK, self.width), BF)]
        self.scratch += [SEND((n, 16)), SEND((n, 16)), SEND((n, 16)), SEND((16,))]

    def run(self, at, ins, outs, scratch):
        n = len(ins)
        own, near, packed = scratch[:n], scratch[n : 2 * n], scratch[2 * n]
        load, send, recv, store = scratch[2 * n + 1 :]

        def chip(slot, core):
            return at.chip(lax.rem(slot // 4, 2), slot // 8, lax.rem(slot, 4), core)

        def fetch(index, slot):
            src = self.blocks[index].at(ins[index], chip(slot, at.core), at.core)
            return local(src, own[index].at[slot], load.at[index, slot])

        def across(index, slot):
            other = 1 - at.core
            src = self.blocks[index].at(ins[index], chip(slot, other), other)
            return remote(
                src, near[index].at[slot], send.at[index, slot], recv.at[index, slot], at.sibling()
            )

        def keep(slot, group, first):
            return local(packed.at[slot], outs[group].at[slot - first], store.at[slot])

        @pl.loop(0, 16)
        def _(turn):
            for index in range(n):
                across(index, 15 - turn).start()
                fetch(index, 15 - turn).start()

        yield
        groups = ((2, 8, 8), (1, 4, 4), (0, 0, 4))
        for group, first, count in groups:

            @pl.loop(0, count)
            def _(turn):
                slot = first + count - 1 - turn
                begin = 0
                for index in range(n):
                    fetch(index, slot).wait()
                    across(index, slot).wait_recv()
                    rows, width = self.blocks[index].shape
                    for part in range(rows // PACK):
                        cut = pl.ds(part * PACK, PACK)
                        add_into(
                            packed.at[slot, :, pl.ds(begin, width)],
                            [own[index].at[slot, cut, :], near[index].at[slot, cut, :]],
                        )
                        begin += width
                keep(slot, group, first).start()

            yield
        yield "last"
        for group, first, count in groups:

            @pl.loop(0, count)
            def _(turn):
                slot = first + count - 1 - turn
                for index in range(n):
                    across(index, slot).wait_send()
                keep(slot, group, first).wait()


def unpack(total, shapes):
    blocks, begin = [], 0
    for rows, width in shapes:
        parts = []
        for _ in range(rows // PACK):
            parts.append(total[:, begin : begin + width])
            begin += width
        blocks.append(jnp.concatenate(parts, axis=0))
    return blocks


class LineSums:
    def __init__(self, terms, shapes, cuts, rest=0):
        self.arrays = list(terms)
        self.rest = rest
        self.shapes = shapes
        self.outs = [jax.ShapeDtypeStruct(shape, F32) for shape in shapes]
        self.out_specs = [VMEM] * len(shapes)
        self.segments, begin = [], 0
        for index, (rows, width) in enumerate(shapes):
            for part in range(rows // PACK):
                self.segments.append((index, part, begin, width))
                begin += width
        self.pieces = []
        for group in cuts:
            held = [s for s in self.segments if s[0] in group]
            first = held[0][2]
            self.pieces.append((first, held[-1][2] + held[-1][3] - first, held))
        n = len(self.pieces)
        box = (PACK, begin)
        self.scratch = [pltpu.VMEM((4,) + box, BF) for _ in terms]
        self.scratch += [pltpu.VMEM((4,) + box, BF), pltpu.VMEM((4,) + box, BF)]
        self.scratch += [pltpu.VMEM((2,) + box, BF), pltpu.VMEM(box, BF)]
        self.scratch += [SEND((len(terms), 4)), SEND((6, n)), SEND((6, n))]

    def run(self, at, ins, outs, scratch):
        n = len(ins)
        terms = scratch[:n]
        low, outer_box, far_box, inner_box, load, send, recv = scratch[n:]
        inner = flip(at.z // 2, lax.rem(at.z, 2))
        inside, outside = pl.when(inner == 1), pl.when(inner == 0)
        near, far = at.device(0, 0, 1), at.device(0, 0, 3)
        pieces = range(len(self.pieces))

        def fetch(index, dz):
            return local(ins[index].at[dz], terms[index].at[dz], load.at[index, dz])

        def columns_of(c):
            first, width, _ = self.pieces[c]
            return pl.ds(first, width)

        def hand(kind, c):
            cut = columns_of(c)
            src, dst, target = {
                1: (low.at[1, :, cut], outer_box.at[1, :, cut], near),
                2: (low.at[2, :, cut], outer_box.at[2, :, cut], near),
                3: (low.at[3, :, cut], outer_box.at[3, :, cut], near),
                0: (low.at[3, :, cut], far_box.at[0, :, cut], far),
                4: (low.at[2, :, cut], far_box.at[1, :, cut], far),
                5: (low.at[1, :, cut], inner_box.at[:, cut], near),
            }[kind]
            return remote(src, dst, send.at[kind, c], recv.at[kind, c], target)

        def settle(c, dz, more):
            for _, _, begin, width in self.pieces[c][2]:
                cut = pl.ds(begin, width)
                parts = [term.at[dz, :, cut] for term in terms] + [m.at[:, cut] for m in more]
                add_into(low.at[dz, :, cut], parts)

        def finish(c, more):
            for index, part, begin, width in self.pieces[c][2]:
                cut = pl.ds(begin, width)
                parts = [term.at[0, :, cut] for term in terms] + [m.at[:, cut] for m in more]
                add_into(outs[index].at[pl.ds(part * PACK, PACK), :], parts)

        for dz in (2, 3, 1, 0):
            for index in range(n):
                fetch(index, dz).start()
        yield
        for dz in (2, 3, 1, 0):
            for index in range(n):
                fetch(index, dz).wait()

        @outside
        def _():
            for c in pieces:
                for dz in (2, 3, 1):
                    settle(c, dz, [])
                    hand(dz, c).start()

        def inwards(c):
            @inside
            def _():
                hand(2, c).wait_recv()
                settle(c, 3, [outer_box.at[2]])
                hand(0, c).start()
                hand(3, c).wait_recv()
                settle(c, 2, [outer_box.at[3]])
                hand(4, c).start()

        def outwards(c):
            @inside
            def _():
                hand(4, c).wait_recv()
                settle(c, 1, [far_box.at[1]])
                hand(5, c).start()
                hand(0, c).wait_recv()
                hand(1, c).wait_recv()
                finish(c, [outer_box.at[1], far_box.at[0]])

            @outside
            def _():
                hand(5, c).wait_recv()
                finish(c, [inner_box])

        for _ in range(1 + self.rest):
            yield
        for c in pieces:
            inwards(c)
            yield
            if c:
                outwards(c - 1)
                yield
        yield "last"
        outwards(len(self.pieces) - 1)
        for c in pieces:

            @outside
            def _():
                for kind in (1, 2, 3):
                    hand(kind, c).wait_send()

            @inside
            def _():
                for kind in (0, 4, 5):
                    hand(kind, c).wait_send()


class Scatter:
    def __init__(self, whole, blocks, turn=0):
        self.arrays = [whole]
        self.blocks = blocks
        self.turn = turn
        shape = blocks.shape
        self.pair = isinstance(blocks, PairBlocks)
        out = (shape[0] // 2, 2 * shape[1]) if self.pair else shape
        self.outs = [jax.ShapeDtypeStruct(out, F32)]
        self.out_specs = [VMEM]
        dma = SEND
        self.scratch = [
            pltpu.VMEM((16,) + shape, BF),
            pltpu.VMEM((16,) + shape, BF),
            pltpu.VMEM((8,) + shape, BF),
            pltpu.VMEM((4,) + shape, BF),
            pltpu.VMEM((4,) + shape, BF),
            dma((16,)),
            dma((32,)),
            dma((32,)),
        ]
        if self.pair:
            self.scratch += [pltpu.VMEM(shape, F32), dma((2,))]

    def run(self, at, ins, outs, scratch):
        (whole,), (out,) = ins, outs
        own, near, from_b, from_a, from_z, load, send, recv = scratch[:8]
        core = at.core
        order = list(reversed(STEPS))

        def fetch(slot):
            src = self.blocks.at(whole, at.chip(*STEPS[slot], core), core)
            return local(src, own.at[slot], load.at[slot])

        def across(slot):
            src = self.blocks.at(whole, at.chip(*STEPS[slot], 1 - core), 1 - core)
            return remote(src, near.at[slot], send.at[slot], recv.at[slot], at.sibling())

        def second(da, dz):
            slot = STEPS.index((da, 1, dz))
            spot = 4 * da + dz
            return remote(
                own.at[slot], from_b.at[spot], send.at[16 + spot], recv.at[16 + spot],
                at.device(0, 1, 0),
            )

        def first(dz):
            slot = STEPS.index((1, 0, dz))
            return remote(
                own.at[slot], from_a.at[dz], send.at[24 + dz], recv.at[24 + dz], at.device(1, 0, 0)
            )

        def along_z(dz):
            slot = STEPS.index((0, 0, dz))
            return remote(
                own.at[slot], from_z.at[dz], send.at[28 + dz], recv.at[28 + dz], at.device(0, 0, dz)
            )

        for step in order:
            slot = STEPS.index(step)
            across(slot).start()
            fetch(slot).start()
        for _ in range(1 + self.turn):
            yield

        def settle(step, more, dst=None):
            slot = STEPS.index(step)
            fetch(slot).wait()
            across(slot).wait_recv()
            parts = [own.at[slot], near.at[slot]] + more
            add_into(own.at[slot] if dst is None else dst, parts)

        for da in (1, 0):
            for dz in (3, 2, 1, 0):
                settle((da, 1, dz), [])
                second(da, dz).start()
        yield
        for dz in (3, 2, 1, 0):
            second(1, dz).wait_recv()
            settle((1, 0, dz), [from_b.at[4 + dz]])
            first(dz).start()
        yield
        for dz in (3, 2, 1):
            second(0, dz).wait_recv()
            first(dz).wait_recv()
            settle((0, 0, dz), [from_b.at[dz], from_a.at[dz]])
            along_z(dz).start()
        yield "last"
        second(0, 0).wait_recv()
        first(0).wait_recv()
        for dz in (1, 2, 3):
            along_z(dz).wait_recv()
        total = scratch[8] if self.pair else out
        more = [from_b.at[0], from_a.at[0]] + [from_z.at[dz] for dz in (1, 2, 3)]
        settle((0, 0, 0), more, total)
        if self.pair:
            rows, width = self.blocks.shape
            half = rows // 2
            columns = span(core, width)
            swap = remote(
                total.at[span(1 - core, half), :], out.at[:, columns],
                scratch[9].at[0], scratch[9].at[1], at.sibling(),
            )
            swap.start()
            out[:, columns] = total[span(core, half), :]
        if self.pair:
            swap.wait()
        for slot in range(16):
            across(slot).wait_send()
        for dz in range(4):
            for da in range(2):
                second(da, dz).wait_send()
            first(dz).wait_send()
            if dz:
                along_z(dz).wait_send()


def later(part, steps=2):
    part.wait = steps
    return part


def staged(part, *refs):
    for _ in range(getattr(part, "wait", 0)):
        yield
    yield from part.run(*refs)


def exchange(name, collective, parts):
    sizes = [(len(p.arrays), len(p.outs), len(p.scratch)) for p in parts]
    n_in = sum(size[0] for size in sizes)
    n_out = sum(size[1] for size in sizes)

    def kernel(*refs):
        at = Place()
        barrier = pltpu.get_barrier_semaphore()
        near = [(at.grp, lax.rem(at.key + k, 2 * LOCAL)) for k in range(1, 2 * LOCAL)]
        near += [at.device(1, 0, 0), at.device(0, 1, 0)]
        for device in near:
            pl.semaphore_signal(barrier, inc=1, device_id=device, device_id_type=MESH)
        pl.semaphore_wait(barrier, len(near))
        ins, outs, scratch = refs[:n_in], refs[n_in : n_in + n_out], refs[n_in + n_out :]
        live = []
        sums = any(isinstance(part, Scatter) for part in parts)
        for part, (i, o, s) in zip(parts, sizes):
            live.append(staged(part, at, ins[:i], outs[:o], scratch[:s]))
            ins, outs, scratch = ins[i:], outs[o:], scratch[s:]
        for stage in live:
            next(stage)
        ending = []
        while live:
            for stage in list(reversed(live) if sums else live):
                if next(stage) == "last":
                    live.remove(stage)
                    ending.append(stage)
        for stage in ending:
            for _ in stage:
                pass

    outs = pl.pallas_call(
        kernel,
        name=name,
        out_shape=[o for p in parts for o in p.outs],
        in_specs=[ANY] * n_in,
        out_specs=[o for p in parts for o in p.out_specs],
        scratch_shapes=[s for p in parts for s in p.scratch],
        compiler_params=pltpu.CompilerParams(
            collective_id=collective, has_side_effects=True, vmem_limit_bytes=ROOM
        ),
    )(*[a for p in parts for a in p.arrays])
    outs = list(outs)
    return [[outs.pop(0) for _ in p.outs] for p in parts]


def hop(values, change):
    pairs = []
    for y in range(2):
        for x in range(2):
            for z in range(LOCAL):
                for core in range(2):
                    to = [y, x, z, core]
                    if change in ("a", "b"):
                        to[1 if (change == "a") == (core == 0) else 0] ^= 1
                    elif change == "core":
                        to[3] ^= 1
                    else:
                        to[2] ^= change
                    number = [((v[0] * 2 + v[1]) * LOCAL + v[2]) * 2 + v[3] for v in ([y, x, z, core], to)]
                    pairs.append(tuple(number))
    return lax.ppermute(values, ("grp", "key"), pairs)


def column_hop(values, pairs):
    size = 2 * LOCAL
    every = [(g * size + s, g * size + t) for g in range(4) for s, t in pairs]
    return lax.ppermute(values, ("grp", "key"), every)


def join(value, others):
    return lax.optimization_barrier((value, others))


def gather_column(shard):
    return jnp.stack([shard] + [hop(shard, dz) for dz in (1, 2, 3)])


def add(*terms):
    return sum(term.astype(F32) for term in terms)


def scatter_second(sums):
    here, first, second = sums
    return here, first, hop(second, "b")


def scatter_first(sums):
    here, first, got = sums
    return here, got, hop(add(first, got[4:]).astype(BF), "a")


def scatter_z(sums):
    here, got, more = sums
    total = add(here, got[:4], more)
    low = total[1:].astype(BF)
    return [total[0]] + [hop(low[dz - 1], dz) for dz in (1, 2, 3)]


def scatter_end(sums):
    return add(*sums)


def rows_hops(chunks):
    odd = lax.rem(lax.axis_index("key"), 2) == 1
    size = 2 * LOCAL
    same = [(j, j // 2 + LOCAL * (j % 2)) for j in range(size)]
    cross = [(j, j // 2 + LOCAL * (1 - j % 2)) for j in range(size)]
    one = column_hop(jnp.where(odd, chunks[1], chunks[0]), same)
    two = column_hop(jnp.where(odd, chunks[0], chunks[1]), cross)
    upper = lax.axis_index("key") >= LOCAL
    return jnp.concatenate((jnp.where(upper, two, one), jnp.where(upper, one, two)))


def chunk_hops(rows):
    half = rows.shape[0] // 2
    odd = lax.rem(lax.axis_index("key"), 2) == 1
    upper = lax.axis_index("key") >= LOCAL
    size = 2 * LOCAL
    same = [(j // 2 + LOCAL * (j % 2), j) for j in range(size)]
    cross = [(j // 2 + LOCAL * (1 - j % 2), j) for j in range(size)]
    one = column_hop(jnp.where(upper, rows[half:], rows[:half]), same)
    two = column_hop(jnp.where(upper, rows[:half], rows[half:]), cross)
    return jnp.stack((jnp.where(odd, two, one), jnp.where(odd, one, two)))


def dot_nt(a, b):
    return lax.dot_general(a, b, (((1,), (1,)), ((), ())), preferred_element_type=F32)


def dot_nn(a, b):
    return lax.dot_general(a, b, (((1,), (0,)), ((), ())), preferred_element_type=F32)


def heads(index):
    return pl.ds(index * HEAD, HEAD)


def block_rows(j):
    return pl.ds(pl.multiple_of(j * BLOCK, BLOCK), BLOCK)


def turned(values):
    return values.astype(F32).T.astype(BF)


def transpose_blocks(src, dst):
    @pl.loop(0, src.shape[0] // BLOCK)
    def _(j):
        dst[j] = turned(src[block_rows(j), :])


def visible(bounds, low, high, j):
    at = lax.broadcasted_iota(jnp.int32, (BLOCK, QUERIES), 0)
    start = j * BLOCK
    return (at >= bounds[low : low + 1, :] - start) & (at < bounds[high : high + 1, :] - start)


def fold(values):
    return values.reshape(values.shape[0] // 8, 8, values.shape[1])


def each_block(ranges, i, with_memory, local_body, memory_body):
    begin, full, diagonal, end = (ranges[i, k] for k in range(4))
    lax.fori_loop(begin, full, local_body(True), 0)
    lax.fori_loop(full, diagonal, local_body(False), 0)
    lax.fori_loop(diagonal, end, local_body(True), 0)
    if with_memory:
        begin, full, rest, end = (ranges[i, k] for k in range(4, 8))
        lax.fori_loop(begin, full, memory_body(True), 0)
        lax.fori_loop(full, rest, memory_body(False), 0)
        lax.fori_loop(rest, end, memory_body(True), 0)


def attend_kernel(with_memory, ranges, *refs):
    if with_memory:
        q, k, v, bounds, mk, mv, out, stat, vt, mvt, scores, acc, top, total = refs
    else:
        q, k, v, bounds, out, stat, vt, scores, acc, top, total = refs
        mk = mvt = None
    i = pl.program_id(0)
    scale = HEAD ** (-0.5) * LOG2E
    blocks = vt.shape[0]

    @pl.when(i == 0)
    def _():
        transpose_blocks(v, vt)
        if with_memory:
            transpose_blocks(mv, mvt)

    acc[...] = jnp.zeros_like(acc)
    top[...] = jnp.full_like(top, NEG)
    total[...] = jnp.zeros_like(total)

    def scan(keys, first, low):
        def run(masked):
            def body(j, _):
                for h in range(2):
                    part = dot_nt(keys[block_rows(j), heads(h)], q[:, heads(h)])
                    if masked:
                        part = jnp.where(visible(bounds, low, low + 1, j), part, NEG)
                    scores[h, first + j] = part
                    top[h] = jnp.maximum(top[h], jnp.max(fold(part), axis=0))
                return 0

            return body

        return run

    each_block(ranges, i, with_memory, scan(k, 0, 0), scan(mk, blocks, 2))
    tops = [jnp.max(top[h], axis=0, keepdims=True) * scale for h in range(2)]

    def take(values_t, first):
        def run(masked):
            def body(j, _):
                for h in range(2):
                    probs = jnp.exp2(scores[h, first + j] * scale - tops[h])
                    total[h] += jnp.sum(fold(probs), axis=0)
                    acc[heads(h), :] += dot_nn(values_t[j, heads(h), :], probs.astype(BF))
                return 0

            return body

        return run

    lax.fori_loop(ranges[i, 0], ranges[i, 3], take(vt, 0)(False), 0)
    if with_memory:
        lax.fori_loop(ranges[i, 4], ranges[i, 7], take(mvt, blocks)(False), 0)
    for h in range(2):
        share = jnp.sum(total[h], axis=0, keepdims=True)
        out[:, heads(h)] = (acc[heads(h), :] / share).T.astype(BF)
        stat[h : h + 1, :] = tops[h] + jnp.log2(share)
    stat[2:, :] = jnp.zeros_like(stat[2:, :])


def attend(q, k, v, memory, bounds, ranges):
    rows = q.shape[0]
    blocks = rows // BLOCK
    row_block = pl.BlockSpec((QUERIES, PAIR), lambda i, *_: (i, 0))
    lane_block = pl.BlockSpec((8, QUERIES), lambda i, *_: (0, i))
    operands = [q, k, v, bounds]
    in_specs = [row_block, VMEM, VMEM, lane_block]
    scratch = [pltpu.VMEM((blocks, PAIR, BLOCK), BF)]
    if memory is not None:
        operands += [memory[0], memory[1]]
        in_specs += [VMEM, VMEM]
        more = memory[1].shape[0] // BLOCK
        scratch += [pltpu.VMEM((more, PAIR, BLOCK), BF)]
        blocks += more
    return pl.pallas_call(
        functools.partial(attend_kernel, memory is not None),
        name="attend",
        grid_spec=pltpu.PrefetchScalarGridSpec(
            num_scalar_prefetch=1,
            grid=(rows // QUERIES,),
            in_specs=in_specs,
            out_specs=(row_block, lane_block),
            scratch_shapes=scratch
            + [
                pltpu.VMEM((2, blocks, BLOCK, QUERIES), F32),
                pltpu.VMEM((PAIR, QUERIES), F32),
                pltpu.VMEM((2, 8, QUERIES), F32),
                pltpu.VMEM((2, 8, QUERIES), F32),
            ],
        ),
        out_shape=(
            jax.ShapeDtypeStruct((rows, PAIR), BF),
            jax.ShapeDtypeStruct((8, rows), F32),
        ),
        compiler_params=pltpu.CompilerParams(vmem_limit_bytes=ROOM),
    )(ranges, *operands)


def attend_back_kernel(with_memory, ranges, *refs):
    if with_memory:
        (q, go, o, stat, bounds, k, v, mk, mv, gq, gk, gv, kt, mkt, delta, gq_t, gk_sum, gv_sum) = refs
    else:
        (q, go, o, stat, bounds, k, v, gq, gk, gv, kt, delta, gq_t, gk_sum, gv_sum) = refs
        mk = mv = mkt = None
    i = pl.program_id(0)
    unit = HEAD ** (-0.5)
    scale = unit * LOG2E

    @pl.when(i == 0)
    def _():
        transpose_blocks(k, kt)
        gk_sum[...] = jnp.zeros_like(gk_sum)
        gv_sum[...] = jnp.zeros_like(gv_sum)
        if with_memory:
            transpose_blocks(mk, mkt)

    for h in range(2):
        both = go[:, heads(h)].astype(F32) * o[:, heads(h)].astype(F32)
        delta[h : h + 1, :] = jnp.sum(both.T, axis=0, keepdims=True)
    gq_t[...] = jnp.zeros_like(gq_t)

    def step(keys, values, keys_t, low, own):
        def run(masked):
            def body(j, _):
                for h in range(2):
                    query, grad = q[:, heads(h)], go[:, heads(h)]
                    scores = dot_nt(keys[block_rows(j), heads(h)], query) * scale
                    probs = jnp.exp2(scores - stat[h : h + 1, :])
                    if masked:
                        probs = jnp.where(visible(bounds, low, low + 1, j), probs, 0.0)
                    grad_probs = dot_nt(values[block_rows(j), heads(h)], grad)
                    grad_scores = (probs * (grad_probs - delta[h : h + 1, :])).astype(BF)
                    gq_t[heads(h), :] += dot_nn(keys_t[j, heads(h), :], grad_scores)
                    if own:
                        gv_sum[block_rows(j), heads(h)] += dot_nn(probs.astype(BF), grad)
                        gk_sum[block_rows(j), heads(h)] += dot_nn(grad_scores, query)
                return 0

            return body

        return run

    each_block(ranges, i, with_memory, step(k, v, kt, 0, True), step(mk, mv, mkt, 2, False))
    gq[...] = (gq_t[...] * unit).T.astype(BF)

    @pl.when(i == pl.num_programs(0) - 1)
    def _():
        gk[...] = (gk_sum[...] * unit).astype(BF)
        gv[...] = gv_sum[...].astype(BF)


def attend_back(q, k, v, memory, bounds, ranges, out, stat, grad):
    rows = q.shape[0]
    blocks = rows // BLOCK
    row_block = pl.BlockSpec((QUERIES, PAIR), lambda i, *_: (i, 0))
    lane_block = pl.BlockSpec((8, QUERIES), lambda i, *_: (0, i))
    operands = [q, grad, out, stat, bounds, k, v]
    in_specs = [row_block, row_block, row_block, lane_block, lane_block, VMEM, VMEM]
    scratch = [pltpu.VMEM((blocks, PAIR, BLOCK), BF)]
    if memory is not None:
        operands += [memory[0], memory[1]]
        in_specs += [VMEM, VMEM]
        scratch += [pltpu.VMEM((memory[0].shape[0] // BLOCK, PAIR, BLOCK), BF)]
    whole = jax.ShapeDtypeStruct((rows, PAIR), BF)
    return pl.pallas_call(
        functools.partial(attend_back_kernel, memory is not None),
        name="attend_back",
        grid_spec=pltpu.PrefetchScalarGridSpec(
            num_scalar_prefetch=1,
            grid=(rows // QUERIES,),
            in_specs=in_specs,
            out_specs=(row_block, VMEM, VMEM),
            scratch_shapes=scratch
            + [
                pltpu.VMEM((8, QUERIES), F32),
                pltpu.VMEM((PAIR, QUERIES), F32),
                pltpu.VMEM((rows, PAIR), F32),
                pltpu.VMEM((rows, PAIR), F32),
            ],
        ),
        out_shape=(whole, whole, whole),
        compiler_params=pltpu.CompilerParams(vmem_limit_bytes=ROOM),
    )(ranges, *operands)


NUMBERS = 8


def members(docs):
    number = jnp.arange(NUMBERS, dtype=jnp.int32)
    return (docs[None, :] == number[:, None]).astype(jnp.int32)


def before(counts):
    at = jnp.arange(counts.shape[-1])
    earlier = at[:, None] < at[None, :]
    return jnp.sum(jnp.where(earlier, counts[..., :, None], 0), axis=-2)


def pick(which, table):
    return jnp.sum(which * table[:, None], axis=0)


def mask_ranges(docs, mem_docs, reset):
    rows = docs.shape[0]
    at = jnp.arange(rows, dtype=jnp.int32)
    own, other = members(docs), members(mem_docs)
    start = pick(own, before(jnp.sum(own, axis=1)))
    counts = jnp.where(reset == 0, jnp.sum(other, axis=1), 0)
    mem_low = pick(own, before(counts))
    mem_high = mem_low + pick(own, counts)
    zero = jnp.zeros_like(start)
    bounds = jnp.stack((start, at + 1, mem_low, mem_high, zero, zero, zero, zero))

    def per_block(values):
        return values.reshape(rows // QUERIES, QUERIES)

    def up(values):
        return (values + BLOCK - 1) // BLOCK

    place = jnp.arange(rows // QUERIES, dtype=jnp.int32) * QUERIES
    diagonal, end = place // BLOCK, up(place + QUERIES)
    first = jnp.min(per_block(start), axis=1) // BLOCK
    full = jnp.clip(up(jnp.max(per_block(start), axis=1)), first, diagonal)
    some = mem_high > mem_low
    mem_first = jnp.min(per_block(jnp.where(some, mem_low, mem_docs.shape[0])), axis=1) // BLOCK
    mem_end = jnp.maximum(up(jnp.max(per_block(mem_high), axis=1)), mem_first)
    mem_full = jnp.clip(up(jnp.max(per_block(mem_low), axis=1)), mem_first, mem_end)
    mem_rest = jnp.clip(jnp.min(per_block(mem_high), axis=1) // BLOCK, mem_full, mem_end)
    columns = (first, full, diagonal, end, mem_first, mem_full, mem_rest, mem_end)
    return bounds, jnp.stack(columns, axis=1)


def memory_rank(mem_docs):
    entries = mem_docs.shape[0]
    which = members(mem_docs)
    lanes = which.reshape(-1, HEAD)
    at = jnp.arange(HEAD)
    earlier = (at[:, None] < at[None, :]).astype(BF)
    inside = jnp.dot(lanes.astype(BF), earlier, preferred_element_type=F32).astype(jnp.int32)
    totals = jnp.sum(lanes, axis=1).reshape(NUMBERS, -1)
    first = before(jnp.sum(totals, axis=1))[:, None] + before(totals)
    rank = inside.reshape(NUMBERS, -1, HEAD) + first[:, :, None]
    rank = jnp.sum(which * rank.reshape(NUMBERS, entries), axis=0)
    return rank[None]


def columns(matrix, sizes):
    pieces, at = [], 0
    for size in sizes:
        pieces.append(matrix[:, at : at + size])
        at += size
    return pieces


def dot_tn(a, b):
    return lax.dot_general(a, b, (((0,), (0,)), ((), ())), preferred_element_type=F32)


FEED = 256


def inverse_rms(values):
    return lax.rsqrt(jnp.mean(values * values, axis=-1, keepdims=True) + EPS)


def norm_back(values, gain, grad):
    inverse = inverse_rms(values)
    scaled = grad * gain
    mean = jnp.mean(scaled * values, axis=-1, keepdims=True)
    grad_gain = jnp.sum(grad * values * inverse, axis=0, keepdims=True)
    return inverse * scaled - values * (inverse * inverse * inverse) * mean, grad_gain


def feed_kernel(att, stream, out_w, gain, gate_w, up_w, down_w, result, mixed, normed, gate, up):
    step = pl.program_id(0)

    @pl.when(step == 0)
    def _():
        both = stream[...].astype(F32) + dot_nn(att[...], out_w[...])
        mixed[...] = both
        normed[...] = (both * inverse_rms(both) * gain[...]).astype(BF)
        result[...] = both

    gated = dot_nn(normed[...], gate_w[...])
    raised = dot_nn(normed[...], up_w[...])
    gate[...] = gated
    up[...] = raised
    activated = (gated * jax.nn.sigmoid(gated) * raised).astype(BF)
    result[...] += dot_nn(activated, down_w[...])


def feed(attended, stream, out_w, gain, gate_up_w, down_w):
    rows, width = stream.shape
    ff = down_w.shape[0]
    steps = ff // FEED
    part = pl.BlockSpec((rows, FEED), lambda f: (0, f))
    whole = jax.ShapeDtypeStruct((rows, width), F32)
    narrow = jax.ShapeDtypeStruct((rows, width), BF)
    wide = jax.ShapeDtypeStruct((rows, ff), F32)
    return pl.pallas_call(
        feed_kernel,
        name="feed",
        grid=(steps,),
        in_specs=[
            VMEM, VMEM, VMEM, VMEM,
            pl.BlockSpec((width, FEED), lambda f: (0, f)),
            pl.BlockSpec((width, FEED), lambda f: (0, steps + f)),
            pl.BlockSpec((FEED, width), lambda f: (f, 0)),
        ],
        out_specs=(VMEM, VMEM, VMEM, part, part),
        out_shape=(whole, whole, narrow, wide, wide),
        compiler_params=pltpu.CompilerParams(vmem_limit_bytes=ROOM),
    )(attended, stream, out_w, gain, gate_up_w, gate_up_w, down_w)


def feed_back_kernel(
    grad_new, gate, up, normed, mixed, gain, att, out_w, gate_w, up_w, down_w,
    gate_g, up_g, down_g, grad_mixed, grad_att, out_g, gain_g, branch, normed_t, total,
):
    step = pl.program_id(0)

    @pl.when(step == 0)
    def _():
        branch[...] = grad_new[...].astype(BF)
        normed_t[...] = turned(normed[...])
        total[...] = jnp.zeros_like(total)

    gated, raised = gate[...], up[...]
    sig = jax.nn.sigmoid(gated)
    swish = gated * sig
    grad_act = dot_nt(branch[...], down_w[...])
    down_g[...] = dot_tn((swish * raised).astype(BF), branch[...]).astype(BF)
    grad_gate = (grad_act * raised * sig * (1.0 + gated * (1.0 - sig))).astype(BF)
    grad_up = (grad_act * swish).astype(BF)
    gate_g[...] = dot_nn(normed_t[...], grad_gate).astype(BF)
    up_g[...] = dot_nn(normed_t[...], grad_up).astype(BF)
    total[...] += dot_nt(grad_gate, gate_w[...]) + dot_nt(grad_up, up_w[...])

    @pl.when(step == pl.num_programs(0) - 1)
    def _():
        back, grad_gain = norm_back(mixed[...], gain[...], total[...])
        both = grad_new[...].astype(F32) + back
        grad_mixed[...] = both
        gain_g[...] = grad_gain
        low = both.astype(BF)
        grad_att[...] = dot_nt(low, out_w[...]).astype(BF)
        out_g[...] = dot_tn(att[...], low).astype(BF)


def feed_back(grad_new, weights, kept):
    gain_a, qkv_w, out_w, gain, gate_up_w, down_w = weights
    attended, mixed, normed, gate, up = kept[7:]
    rows, width = grad_new.shape
    ff = down_w.shape[0]
    steps = ff // FEED
    part = pl.BlockSpec((rows, FEED), lambda f: (0, f))
    columns_of = pl.BlockSpec((width, FEED), lambda f: (0, f))
    rows_of = pl.BlockSpec((FEED, width), lambda f: (f, 0))

    def shape(a, b, kind=BF):
        return jax.ShapeDtypeStruct((a, b), kind)

    return pl.pallas_call(
        feed_back_kernel,
        name="feed_back",
        grid=(steps,),
        in_specs=[
            VMEM, part, part, VMEM, VMEM, VMEM, VMEM, VMEM,
            columns_of, pl.BlockSpec((width, FEED), lambda f: (0, steps + f)), rows_of,
        ],
        out_specs=(columns_of, columns_of, rows_of, VMEM, VMEM, VMEM, VMEM),
        out_shape=(
            shape(width, ff), shape(width, ff), shape(ff, width),
            shape(rows, width, F32), shape(rows, width), shape(width, width), shape(1, width, F32),
        ),
        scratch_shapes=[
            pltpu.VMEM((rows, width), BF), pltpu.VMEM((width, rows), BF), pltpu.VMEM((rows, width), F32),
        ],
        compiler_params=pltpu.CompilerParams(vmem_limit_bytes=ROOM),
    )(grad_new, gate, up, normed, mixed, gain, attended, out_w, gate_up_w, gate_up_w, down_w)


def project_kernel(grad_mixed, stream, gain, normed, grad_qkv, qkv_w, qkv_g, grad_stream, gain_g, normed_t, total):
    step = pl.program_id(0)

    @pl.when(step == 0)
    def _():
        normed_t[...] = turned(normed[...])
        total[...] = jnp.zeros_like(total)

    qkv_g[...] = dot_nn(normed_t[...], grad_qkv[...]).astype(BF)
    total[...] += dot_nt(grad_qkv[...], qkv_w[...])

    @pl.when(step == pl.num_programs(0) - 1)
    def _():
        back, grad_gain = norm_back(stream[...].astype(F32), gain[...], total[...])
        grad_stream[...] = (grad_mixed[...] + back).astype(grad_stream.dtype)
        gain_g[...] = grad_gain


def projections_back(grad_mixed, grad_qkv, weights, kept, kind):
    gain, qkv_w = weights[:2]
    stream, normed = kept[:2]
    rows, width = stream.shape
    size = 1024
    part = pl.BlockSpec((width, size), lambda f: (0, f))
    grad_qkv_w, grad_stream, grad_gain = pl.pallas_call(
        project_kernel,
        name="projections_back",
        grid=(grad_qkv.shape[1] // size,),
        in_specs=[VMEM, VMEM, VMEM, VMEM, pl.BlockSpec((rows, size), lambda f: (0, f)), part],
        out_specs=(part, VMEM, VMEM),
        out_shape=(
            jax.ShapeDtypeStruct(qkv_w.shape, BF),
            jax.ShapeDtypeStruct((rows, width), kind),
            jax.ShapeDtypeStruct((1, width), F32),
        ),
        scratch_shapes=[pltpu.VMEM((width, rows), BF), pltpu.VMEM((rows, width), F32)],
        compiler_params=pltpu.CompilerParams(vmem_limit_bytes=ROOM),
    )(grad_mixed, stream, gain, normed, grad_qkv, qkv_w)
    return grad_stream, grad_gain, grad_qkv_w


def layer(stream, normed, heads, qkv_w, gains, to_rows, memory, bounds, ranges):
    gain_a, gain_b = gains
    q, k, v = heads
    out, stat = attend(q, k, v, memory, bounds, ranges)
    attended, out_w, gate_up_w, down_w = to_rows(out)
    result, mixed, normed_ff, gate, up = feed(attended, stream, out_w, gain_b, gate_up_w, down_w)
    weights = (gain_a, qkv_w, out_w, gain_b, gate_up_w, down_w)
    kept = (stream, normed, q, k, v, out, stat, attended, mixed, normed_ff, gate, up)
    return result, weights, kept


def gain_columns(gains):
    stacked = jnp.stack(gains, axis=1)
    return jnp.pad(stacked, ((0, 0), (0, HEAD - len(gains))))


def pair_rows(own, other, core):
    rows, width = own.shape
    both = jnp.where(core == 0, jnp.stack((own, other)), jnp.stack((other, own)))
    return lax.dynamic_slice_in_dim(both.reshape(2 * rows, width), core * (width // 2), width // 2, 1)


def head_local(
    tokens, token_docs, memory_docs, memory_resets, memory_keys, memory_values,
    attn_gain1, query_weight1, key_weight1, value_weight1, out_weight1,
    ffn_gain1, gate_weight1, up_weight1, down_weight1,
    attn_gain2, second_query_weight, key_weight2, value_weight2, out_weight2,
    ffn_gain2, gate_weight2, up_weight2, down_weight2, cotangent,
):
    count, width = query_weight1.shape
    ff = gate_weight1.shape[1]
    each = down_weight1.shape[0]
    core = lax.rem(lax.axis_index("key"), 2)
    seg = lax.axis_index("key") // LOCAL
    gains = gain_columns((attn_gain1, ffn_gain1, attn_gain2, ffn_gain2))
    downs = jnp.concatenate((down_weight1, down_weight2), axis=0)
    docs = jnp.concatenate((token_docs, memory_docs), axis=0)
    pairs = PairBlocks(2 * each, width // 2)

    def own(*matrices):
        return RowBlocks(count, sum(matrix.shape[1] for matrix in matrices))

    def gather(*matrices):
        return Gather(matrices, own(*matrices))

    other = hop(downs, "core")
    down1 = pair_rows(down_weight1, other[:each], core)
    down2 = pair_rows(down_weight2, other[each:], core)
    groups = 2 * each // count
    tail = down2[groups * count :]
    half = width // 4
    rest2 = jnp.concatenate(
        [gate_weight2, up_weight2, out_weight2]
        + [down2[g * count : (g + 1) * count] for g in range(groups)]
        + [jnp.concatenate((tail[:, :half], tail[:, half:]))],
        axis=1,
    )
    over = 2 * ff + width
    pieces = [(0, 0, count, 0, 2 * ff, 0, 0), (1, 0, count, 0, width, 0, 2 * ff)]
    pieces += [(2, g * count, count, 0, 2 * half, 0, over + 2 * g * half) for g in range(groups)]
    over += 2 * groups * half
    pieces += [(2, groups * count, count // 2, p * half, half, p * count // 2, over) for p in range(2)]
    first1 = (query_weight1, key_weight1, value_weight1)
    front, (docs,), (mk,), (mv,), (gu1_w,), (down1_w,), (out1_w,), (qkv2_w,) = exchange(
        "front", 1,
        [Front(tokens, first1, own(*first1), gains, own(gains), 3), Docs(docs),
         later(Memory(memory_keys), 1), later(Memory(memory_values), 7),
         later(gather(gate_weight1, up_weight1), 2), later(Gather([down1], pairs), 2),
         later(gather(out_weight1), 2), later(gather(second_query_weight, key_weight2, value_weight2), 2)],
    )
    qkv1_w, gains, rows, normed1, *heads1 = front
    own_docs = lax.dynamic_index_in_dim(docs, seg, 0, keepdims=False)
    own_mem_docs = lax.dynamic_index_in_dim(docs, seg + 2, 0, keepdims=False)
    reset = lax.dynamic_index_in_dim(memory_resets, seg, 0, keepdims=False)
    bounds, ranges = mask_ranges(own_docs, own_mem_docs, reset)
    gains = [gains[:, i].astype(F32)[None] for i in range(4)]
    hops = {}
    heads1, rest2 = join(heads1, rest2)
    hops["rest"] = gather_column(rest2)

    def rows1(out):
        ((attended,),) = exchange("to_rows_1", 3, [Swap([out], False)])
        attended, rest = join(attended, hops["rest"])
        hops["rest"] = rest, hop(rest, "a")
        return attended, out1_w, gu1_w, down1_w

    def rows2(out):
        out, rest = join(out, hops["rest"])
        blocks = (RowBlocks(count, 2 * ff), RowBlocks(count, width), pairs)
        (attended,), (gate_up_w, out_w, down_w) = exchange(
            "to_rows_2", 5, [Swap([out], False), Assemble(rest, blocks, pieces)]
        )
        attended, cot = join(attended, cotangent)
        hops["cot"] = rows_hops(cot)
        return attended, out_w, gate_up_w, down_w

    middle, weights1, kept1 = layer(
        rows, normed1, heads1, qkv1_w, (gains[0], gains[1]), rows1, None, bounds, ranges
    )
    normed2 = (middle * inverse_rms(middle) * gains[2]).astype(BF)
    qkv = jnp.dot(normed2, qkv2_w, preferred_element_type=F32).astype(BF)
    qkv, (column, first) = join(qkv, hops["rest"])
    hops["rest"] = column, first, hop(column, "b"), hop(first, "b")
    heads2, memory = exchange(
        "to_heads_2", 4, [Swap([qkv], True), Sort(memory_rank(own_mem_docs), mk, mv)]
    )
    result, weights2, kept2 = layer(
        middle, normed2, heads2, qkv2_w, (gains[2], gains[3]), rows2, memory, bounds, ranges
    )
    cot = hops["cot"]
    output = chunk_hops(result.astype(BF))

    def pair_sum(total):
        half = lax.dynamic_slice_in_dim(total, core * each, each, 0)
        other = hop(lax.dynamic_slice_in_dim(total, (1 - core) * each, each, 0), "core")
        return jnp.where(
            core == 0, jnp.concatenate((half, other), 1), jnp.concatenate((other, half), 1)
        )

    shapes = ((count, ff), (count, ff), (count, width), pairs.shape)

    def feed_sums(gate_g, up_g, down_g, out_g):
        return CoreSums((gate_g, own(gate_g)), (up_g, own(up_g)), (out_g, own(out_g)), (down_g, pairs))

    gate_g2, up_g2, down_g2, grad_mixed, grad_att, out_g2, gain_b2 = feed_back(
        cot, weights2, kept2
    )
    (grad_out,), sums2 = exchange(
        "back_to_heads_2", 6,
        [Swap([grad_att], True), feed_sums(gate_g2, up_g2, down_g2, out_g2)],
    )
    sums2 = scatter_second(sums2)
    q, k, v, out, stat = kept2[2:7]
    grads = attend_back(q, k, v, memory, bounds, ranges, out, stat, grad_out)
    ((grad_qkv,),) = exchange("back_to_rows_2", 7, [Swap(list(grads), False)])
    grad_qkv, (sums2, output) = join(grad_qkv, (sums2, output))
    sums2 = scatter_first(sums2)
    grad_middle, gain_a2, qkv_g2 = projections_back(grad_mixed, grad_qkv, weights2, kept2, F32)
    (qkv_s2,) = exchange("projection_sums_2", 12, [CoreSums((qkv_g2, own(qkv_g2)))])
    grad_middle, (sums2, qkv_s2) = join(grad_middle, (sums2, qkv_s2))
    sums2 = scatter_z(sums2)
    qkv_s2 = scatter_second(qkv_s2)

    gate_g1, up_g1, down_g1, grad_mixed, grad_att, out_g1, gain_b1 = feed_back(
        grad_middle, weights1, kept1
    )
    grad_att, qkv_s2 = join(grad_att, qkv_s2)
    qkv_s2 = scatter_first(qkv_s2)
    (grad_out,), wide1, rest1 = exchange(
        "back_to_heads_1", 8,
        [Swap([grad_att], True), CoreSums((gate_g1, own(gate_g1)), (up_g1, own(up_g1))),
         CoreSums((out_g1, own(out_g1)), (down_g1, pairs))],
    )
    grad_out, (sums2, qkv_s2) = join(grad_out, (sums2, qkv_s2))
    qkv_s2 = scatter_z(qkv_s2)
    wide1, rest1 = scatter_second(wide1), scatter_second(rest1)
    q, k, v, out, stat = kept1[2:7]
    grads = attend_back(q, k, v, None, bounds, ranges, out, stat, grad_out)
    grads, wide1 = join(grads, wide1)
    wide1 = scatter_first(wide1)
    ((grad_qkv,),) = exchange("back_to_rows_1", 9, [Swap(list(grads), False)])
    grad_qkv, (wide1, rest1, qkv_s2) = join(grad_qkv, (wide1, rest1, qkv_s2))
    rest1 = scatter_first(rest1)
    wide1 = scatter_z(wide1)
    grad_rows, gain_a1, qkv_g1 = projections_back(grad_mixed, grad_qkv, weights1, kept1, BF)
    gain_grads = gain_columns([g[0] for g in (gain_a1, gain_b1, gain_a2, gain_b2)]).astype(BF)
    (grad_tokens,), (out_s1, down_s1), (q_s1,), (k_s1,), (v_s1,), (gain_s,) = exchange(
        "back_to_owners", 10,
        [Chunks(grad_rows), LineSums(rest1, shapes[2:], ((0,), (1,)))]
        + [Scatter(qkv_g1, ColumnBlocks(count, width, i), i) for i in range(3)]
        + [Scatter(gain_grads, own(gain_grads))],
    )
    gate_s1, up_s1 = unpack(scatter_end(wide1), shapes[:2])
    gate_s2, up_s2, out_s2, down_s2 = unpack(scatter_end(sums2), shapes)
    (qkv_s2,) = unpack(scatter_end(qkv_s2), ((count, 3 * width),))
    q_s2, k_s2, v_s2 = columns(qkv_s2, (width,) * 3)
    return (
        output, grad_tokens.astype(F32),
        gain_s[:, 0], q_s1, k_s1, v_s1, out_s1, gain_s[:, 1], gate_s1, up_s1, pair_sum(down_s1),
        gain_s[:, 2], q_s2, k_s2, v_s2, out_s2, gain_s[:, 3], gate_s2, up_s2, pair_sum(down_s2),
    )


def solution(mesh):
    in_specs = (
        P("grp", "key", None),
        P("grp", "key"),
        P("grp", "key"),
        P("grp"),
        P("grp", "key", None),
        P("grp", "key", None),
        P(("grp", "key")),
        P(("grp", "key"), None),
        P(("grp", "key"), None),
        P(("grp", "key"), None),
        P(("grp", "key"), None),
        P(("grp", "key")),
        P(("grp", "key"), None),
        P(("grp", "key"), None),
        P(("grp", "key"), None),
        P(("grp", "key")),
        P(("grp", "key"), None),
        P(("grp", "key"), None),
        P(("grp", "key"), None),
        P(("grp", "key"), None),
        P(("grp", "key")),
        P(("grp", "key"), None),
        P(("grp", "key"), None),
        P(("grp", "key"), None),
        P("grp", "key", None),
    )
    out_specs = (
        P("grp", "key", None),
        P("grp", "key", None),
        P(("grp", "key")),
        P(("grp", "key"), None),
        P(("grp", "key"), None),
        P(("grp", "key"), None),
        P(("grp", "key"), None),
        P(("grp", "key")),
        P(("grp", "key"), None),
        P(("grp", "key"), None),
        P(("grp", "key"), None),
        P(("grp", "key")),
        P(("grp", "key"), None),
        P(("grp", "key"), None),
        P(("grp", "key"), None),
        P(("grp", "key"), None),
        P(("grp", "key")),
        P(("grp", "key"), None),
        P(("grp", "key"), None),
        P(("grp", "key"), None),
    )
    body = head_local if dict(mesh.shape) == {"grp": 4, "key": HEADS} else gathered_local
    return jax.shard_map(body, mesh=mesh, in_specs=in_specs, out_specs=out_specs, check_vma=False)
```

```python
import functools

import jax
import jax.numpy as jnp
from jax import lax
from jax.experimental import pallas as pl
from jax.experimental.pallas import tpu as pltpu
from jax.sharding import PartitionSpec as P

HEADS = 8


EPS = 1e-05
NEG = -1e30


def norm_forward(values, gain_vec):
    inverse = lax.rsqrt(jnp.mean(values * values, axis=-1, keepdims=True) + EPS)
    return (values * inverse * gain_vec, inverse)


def norm_backward(values, gain_vec, inverse, grad_normed):
    grad_gain = jnp.sum(grad_normed * values * inverse, axis=(0, 1))
    scaled = grad_normed * gain_vec
    grad_values = inverse * scaled - values * inverse**3 * jnp.mean(
        scaled * values, axis=-1, keepdims=True
    )
    return (grad_values, grad_gain)


def project(input_operand, weight_matrix):
    return jnp.dot(input_operand, weight_matrix, preferred_element_type=jnp.float32)


def project_back(gradient_row_block, weight_matrix):
    return jnp.einsum(
        "tzu,ku->tzk", gradient_row_block, weight_matrix, preferred_element_type=jnp.float32
    )


def outer_sum(input_arrays, gradient_reduced_precision):
    return jnp.einsum(
        "zhp,zhv->pv", input_arrays, gradient_reduced_precision, preferred_element_type=jnp.float32
    )


def split_heads(rows):
    return rows.reshape(rows.shape[0], rows.shape[1], HEADS, rows.shape[2] // HEADS)


def fetch_weights(shards):
    return (
        lax.all_gather(shards[0], ("grp", "key"), axis=0, tiled=True),
        lax.all_gather(shards[1], ("grp", "key"), axis=0, tiled=True),
        lax.all_gather(shards[2], ("grp", "key"), axis=0, tiled=True),
        lax.all_gather(shards[3], ("grp", "key"), axis=0, tiled=True),
        lax.all_gather(shards[4], ("grp", "key"), axis=0, tiled=True),
        lax.all_gather(shards[5], ("grp", "key"), axis=0, tiled=True),
        lax.all_gather(shards[6], ("grp", "key"), axis=0, tiled=True),
        lax.all_gather(shards[7], ("grp", "key"), axis=0, tiled=True),
        lax.all_gather(shards[8], ("grp", "key"), axis=0, tiled=True),
    )


def refetch_weights(shards):
    return (
        lax.all_gather(shards[0], ("grp", "key"), axis=0, tiled=True),
        lax.all_gather(shards[1], ("grp", "key"), axis=0, tiled=True),
        lax.all_gather(shards[2], ("grp", "key"), axis=0, tiled=True),
        lax.all_gather(shards[3], ("grp", "key"), axis=0, tiled=True),
        lax.all_gather(shards[4], ("grp", "key"), axis=0, tiled=True),
        lax.all_gather(shards[5], ("grp", "key"), axis=0, tiled=True),
        lax.all_gather(shards[6], ("grp", "key"), axis=0, tiled=True),
        lax.all_gather(shards[7], ("grp", "key"), axis=0, tiled=True),
        lax.all_gather(shards[8], ("grp", "key"), axis=0, tiled=True),
    )


def reduce_gradient_sums(terms):
    return (
        lax.psum_scatter(terms[0], ("grp", "key"), scatter_dimension=0, tiled=True),
        lax.psum_scatter(terms[1], ("grp", "key"), scatter_dimension=0, tiled=True),
        lax.psum_scatter(terms[2], ("grp", "key"), scatter_dimension=0, tiled=True),
        lax.psum_scatter(terms[3], ("grp", "key"), scatter_dimension=0, tiled=True),
        lax.psum_scatter(terms[4], ("grp", "key"), scatter_dimension=0, tiled=True),
        lax.psum_scatter(terms[5], ("grp", "key"), scatter_dimension=0, tiled=True),
        lax.psum_scatter(terms[6], ("grp", "key"), scatter_dimension=0, tiled=True),
        lax.psum_scatter(terms[7], ("grp", "key"), scatter_dimension=0, tiled=True),
        lax.psum_scatter(terms[8], ("grp", "key"), scatter_dimension=0, tiled=True),
    )


def head_scores(query_all, key_block, allowed):
    head_size = query_all.shape[2] // HEADS
    raw_scores = jnp.einsum(
        "sqhd,skhd->shqk",
        split_heads(query_all),
        split_heads(key_block),
        preferred_element_type=jnp.float32,
    ) * head_size ** (-0.5)
    return jnp.where(allowed[:, None], raw_scores, NEG)


def attend_forward(query_all, key_block, value_block, allowed):
    scores = head_scores(query_all, key_block, allowed)
    row_top = lax.pmax(jnp.max(scores, axis=3).astype(jnp.bfloat16), "key").astype(jnp.float32)
    exp_scores = jnp.where(allowed[:, None], jnp.exp(scores - row_top[..., None]), 0.0)
    row_total = lax.psum(jnp.sum(exp_scores, axis=3).astype(jnp.bfloat16), "key").astype(
        jnp.float32
    )
    probability = exp_scores / row_total[..., None]
    partial_value = jnp.einsum(
        "shqk,skhd->sqhd",
        probability.astype(jnp.bfloat16),
        split_heads(value_block),
        preferred_element_type=jnp.float32,
    )
    partial_value = partial_value.reshape(query_all.shape)
    attended = lax.psum_scatter(
        partial_value.astype(jnp.bfloat16), "key", scatter_dimension=1, tiled=True
    ).astype(jnp.float32)
    return (attended, row_top, row_total)


def layer_forward(stream, full_weights, allowed, extra_keys, extra_values):
    gain_a, query_w, key_w, value_w, out_w, gain_b, gate_w, up_w, down_w = full_weights
    normed, first_inverse_factor = norm_forward(stream, gain_a.astype(jnp.float32))
    normed_low = normed.astype(jnp.bfloat16)
    query_low = project(normed_low, query_w).astype(jnp.bfloat16)
    key_low = project(normed_low, key_w).astype(jnp.bfloat16)
    value_low = project(normed_low, value_w).astype(jnp.bfloat16)
    query_all = lax.all_gather(query_low, "key", axis=1, tiled=True)
    if extra_keys is None:
        key_block = key_low
        value_block = value_low
    else:
        key_block = jnp.concatenate((key_low, extra_keys), axis=1)
        value_block = jnp.concatenate((value_low, extra_values), axis=1)
    attended, row_top, row_total = attend_forward(query_all, key_block, value_block, allowed)
    attended_low = attended.astype(jnp.bfloat16)
    mixed_stream = stream + project(attended_low, out_w)
    normed_ff, inverse_b = norm_forward(mixed_stream, gain_b.astype(jnp.float32))
    normed_ff_low = normed_ff.astype(jnp.bfloat16)
    gate_value = project(normed_ff_low, gate_w)
    up_value = project(normed_ff_low, up_w)
    activated_low = (gate_value * jax.nn.sigmoid(gate_value) * up_value).astype(jnp.bfloat16)
    result = mixed_stream + project(activated_low, down_w)
    kept_state = (
        stream,
        first_inverse_factor,
        normed_low,
        key_block,
        value_block,
        query_all,
        row_top,
        row_total,
        attended_low,
        mixed_stream,
        inverse_b,
        normed_ff_low,
        gate_value,
        up_value,
        activated_low,
    )
    return (result, kept_state)


def layer_backward(grad_result, full_weights, kept_state, allowed):
    gain_a, query_w, key_w, value_w, out_w, gain_b, gate_w, up_w, down_w = full_weights
    (
        stream,
        first_inverse_factor,
        normed_low,
        key_block,
        value_block,
        query_all,
        row_top,
        row_total,
        attended_low,
        mixed_stream,
        inverse_b,
        normed_ff_low,
        gate_value,
        up_value,
        activated_low,
    ) = kept_state
    own_rows = stream.shape[1]
    branch_low = grad_result.astype(jnp.bfloat16)
    grad_down = outer_sum(activated_low, branch_low)
    grad_act = project_back(branch_low, down_w)
    sigmoid_gate = jax.nn.sigmoid(gate_value)
    grad_gate = (
        grad_act * up_value * sigmoid_gate * (1.0 + gate_value * (1.0 - sigmoid_gate))
    ).astype(jnp.bfloat16)
    grad_up_low = (grad_act * gate_value * sigmoid_gate).astype(jnp.bfloat16)
    grad_gate_w = outer_sum(normed_ff_low, grad_gate)
    grad_up_w = outer_sum(normed_ff_low, grad_up_low)
    grad_normed_ff = project_back(grad_gate, gate_w) + project_back(grad_up_low, up_w)
    grad_mixed_norm, grad_gain_b = norm_backward(
        mixed_stream, gain_b.astype(jnp.float32), inverse_b, grad_normed_ff
    )
    grad_mixed = grad_result + grad_mixed_norm
    attn_low = grad_mixed.astype(jnp.bfloat16)
    grad_out_w = outer_sum(attended_low, attn_low)
    grad_attended = project_back(attn_low, out_w).astype(jnp.bfloat16)
    grad_all = lax.all_gather(grad_attended, "key", axis=1, tiled=True)
    scores = head_scores(query_all, key_block, allowed)
    probability = (
        jnp.where(allowed[:, None], jnp.exp(scores - row_top[..., None]), 0.0)
        / row_total[..., None]
    )
    grad_heads = split_heads(grad_all)
    grad_probs = jnp.einsum(
        "sqhd,skhd->shqk", grad_heads, split_heads(value_block), preferred_element_type=jnp.float32
    )
    row_delta = lax.psum(
        jnp.sum(probability * grad_probs, axis=3).astype(jnp.bfloat16), "key"
    ).astype(jnp.float32)
    grad_scores = (probability * (grad_probs - row_delta[..., None])).astype(jnp.bfloat16)
    score_scale = (query_all.shape[2] // HEADS) ** (-0.5)
    query_part = (
        jnp.einsum(
            "shqk,skhd->sqhd",
            grad_scores,
            split_heads(key_block),
            preferred_element_type=jnp.float32,
        ).reshape(query_all.shape)
        * score_scale
    )
    grad_query = lax.psum_scatter(
        query_part.astype(jnp.bfloat16), "key", scatter_dimension=1, tiled=True
    )
    own_scores = grad_scores[..., :own_rows]
    grad_key = (
        jnp.einsum(
            "shqk,sqhd->skhd",
            own_scores,
            split_heads(query_all),
            preferred_element_type=jnp.float32,
        ).reshape(stream.shape)
        * score_scale
    ).astype(jnp.bfloat16)
    own_probs = probability.astype(jnp.bfloat16)[..., :own_rows]
    grad_value = (
        jnp.einsum("shqk,sqhd->skhd", own_probs, grad_heads, preferred_element_type=jnp.float32)
        .reshape(stream.shape)
        .astype(jnp.bfloat16)
    )
    grad_query_w = outer_sum(normed_low, grad_query)
    grad_key_w = outer_sum(normed_low, grad_key)
    grad_value_w = outer_sum(normed_low, grad_value)
    grad_normed = (
        project_back(grad_query, query_w)
        + project_back(grad_key, key_w)
        + project_back(grad_value, value_w)
    )
    grad_stream_norm, grad_gain_a = norm_backward(
        stream, gain_a.astype(jnp.float32), first_inverse_factor, grad_normed
    )
    grad_stream = grad_mixed + grad_stream_norm
    terms = (
        grad_gain_a,
        grad_query_w,
        grad_key_w,
        grad_value_w,
        grad_out_w,
        grad_gain_b,
        grad_gate_w,
        grad_up_w,
        grad_down,
    )
    return (grad_stream, terms)


def gathered_local(
    tokens,
    token_docs,
    memory_docs,
    memory_resets,
    memory_keys,
    memory_values,
    attn_gain1,
    query_weight1,
    key_weight1,
    value_weight1,
    out_weight1,
    ffn_gain1,
    gate_weight1,
    up_weight1,
    down_weight1,
    attn_gain2,
    second_query_weight,
    key_weight2,
    value_weight2,
    out_weight2,
    ffn_gain2,
    gate_weight2,
    up_weight2,
    down_weight2,
    cotangent,
):
    first_shards = (
        attn_gain1,
        query_weight1,
        key_weight1,
        value_weight1,
        out_weight1,
        ffn_gain1,
        gate_weight1,
        up_weight1,
        down_weight1,
    )
    second_shards = (
        attn_gain2,
        second_query_weight,
        key_weight2,
        value_weight2,
        out_weight2,
        ffn_gain2,
        gate_weight2,
        up_weight2,
        down_weight2,
    )
    docs_all = lax.all_gather(token_docs, "key", axis=1, tiled=True)
    own_rows = tokens.shape[1]
    query_place = jnp.arange(docs_all.shape[1], dtype=jnp.int32)
    key_place = lax.axis_index("key") * own_rows + jnp.arange(own_rows, dtype=jnp.int32)
    local_allowed = (key_place[None, None, :] <= query_place[None, :, None]) & (
        token_docs[:, None, :] == docs_all[:, :, None]
    )
    memory_allowed = (memory_docs[:, None, :] == docs_all[:, :, None]) & (
        memory_resets[:, None, None] == 0
    )
    both_allowed = jnp.concatenate((local_allowed, memory_allowed), axis=2)
    stream = tokens.astype(jnp.float32)
    first_full = fetch_weights(first_shards)
    middle, first_state = layer_forward(stream, first_full, local_allowed, None, None)
    second_full = fetch_weights(second_shards)
    result, second_state = layer_forward(
        middle, second_full, both_allowed, memory_keys, memory_values
    )
    second_full = refetch_weights(second_shards)
    grad_middle, second_terms = layer_backward(
        cotangent.astype(jnp.float32), second_full, second_state, both_allowed
    )
    second_grads = reduce_gradient_sums(second_terms)
    first_full = refetch_weights(first_shards)
    grad_stream, first_terms = layer_backward(grad_middle, first_full, first_state, local_allowed)
    first_grads = reduce_gradient_sums(first_terms)
    return (
        result.astype(jnp.bfloat16),
        grad_stream,
        first_grads[0],
        first_grads[1],
        first_grads[2],
        first_grads[3],
        first_grads[4],
        first_grads[5],
        first_grads[6],
        first_grads[7],
        first_grads[8],
        second_grads[0],
        second_grads[1],
        second_grads[2],
        second_grads[3],
        second_grads[4],
        second_grads[5],
        second_grads[6],
        second_grads[7],
        second_grads[8],
    )


MESH = pl.DeviceIdType.MESH
ANY = pl.BlockSpec(memory_space=pl.ANY)
VMEM = pl.BlockSpec(memory_space=pltpu.VMEM)
LOG2E = 1.4426950408889634
BLOCK = 512
QUERIES = 512
ROOM = 60 * 2**20
LOCAL = 4
HEAD = 128
PAIR = 2 * HEAD
BF = jnp.bfloat16
F32 = jnp.float32


SEND = pltpu.SemaphoreType.DMA


def flip(value, change):
    return lax.rem(value + change, 2)


class Place:
    def __init__(self):
        self.grp = lax.axis_index("grp")
        self.key = lax.axis_index("key")
        self.y, self.x = self.grp // 2, lax.rem(self.grp, 2)
        self.z, self.core = self.key // 2, lax.rem(self.key, 2)
        self.rank = lax.rem(self.key, LOCAL)
        self.seg = self.key // LOCAL

    def chip(self, da, db, dz, core):
        dx = da * (1 - core) + db * core
        dy = da * core + db * (1 - core)
        z = flip(self.z // 2, dz // 2) * 2 + flip(lax.rem(self.z, 2), lax.rem(dz, 2))
        return flip(self.y, dy) * 2 + flip(self.x, dx), z

    def device(self, da, db, dz):
        grp, z = self.chip(da, db, dz, self.core)
        return grp, z * 2 + self.core

    def sibling(self):
        return self.grp, self.z * 2 + 1 - self.core


def remote(src, dst, send, recv, target):
    return pltpu.make_async_remote_copy(
        src_ref=src, dst_ref=dst, send_sem=send, recv_sem=recv,
        device_id=target, device_id_type=MESH,
    )


def local(src, dst, sem):
    return pltpu.make_async_copy(src, dst, sem)


def span(index, size):
    return pl.ds(pl.multiple_of(index * size, size), size)


class RowBlocks:
    def __init__(self, rows, width):
        self.shape = (rows, width)

    def whole(self, chips):
        return (chips * 2 * self.shape[0], self.shape[1])

    def at(self, ref, chip, core):
        return ref.at[span((chip[0] * LOCAL + chip[1]) * 2 + core, self.shape[0]), :]


class PairBlocks(RowBlocks):
    def whole(self, chips):
        return (chips * self.shape[0], 2 * self.shape[1])

    def at(self, ref, chip, core):
        rows, width = self.shape
        return ref.at[span(chip[0] * LOCAL + chip[1], rows), span(core, width)]


class ColumnBlocks(RowBlocks):
    def __init__(self, rows, width, part):
        self.shape = (rows, width)
        self.part = part

    def at(self, ref, chip, core):
        rows, width = self.shape
        return ref.at[
            span((chip[0] * LOCAL + chip[1]) * 2 + core, rows), pl.ds(self.part * width, width)
        ]


class Swap:
    def __init__(self, arrays, to_heads):
        self.arrays = arrays
        self.to_heads = to_heads
        if to_heads:
            rows, width = arrays[0].shape
            self.parts = width // (LOCAL * PAIR)
            self.outs = [jax.ShapeDtypeStruct((rows * LOCAL, PAIR), BF)] * self.parts
        else:
            rows = arrays[0].shape[0] // LOCAL
            self.parts = len(arrays)
            self.outs = [jax.ShapeDtypeStruct((rows, self.parts * LOCAL * PAIR), BF)]
        self.rows = rows
        self.scratch = [SEND((self.parts, LOCAL)), SEND((self.parts, LOCAL)), SEND((self.parts,))]
        self.out_specs = [ANY] * len(self.outs)

    def run(self, at, ins, outs, scratch):
        send, recv, here = scratch

        def copy(part, k):
            target = lax.rem(at.rank + k, LOCAL)
            if self.to_heads:
                src = ins[0].at[:, span(part * LOCAL + target, PAIR)]
                dst = outs[part].at[span(at.rank, self.rows), :]
            else:
                src = ins[part].at[span(target, self.rows), :]
                dst = outs[0].at[:, span(part * LOCAL + at.rank, PAIR)]
            if k == 0:
                return local(src, dst, here.at[part])
            device = (at.grp, at.seg * LOCAL + target)
            return remote(src, dst, send.at[part, k], recv.at[part, k], device)

        every = [(part, k) for part in range(self.parts) for k in (2, 3, 1, 0)]
        for part, k in every:
            copy(part, k).start()
        yield
        yield "last"
        for part, k in every:
            copy(part, k).wait()


class Rows:
    def __init__(self, array):
        segs, rows, width = array.shape
        self.arrays = [array]
        self.rows = rows
        self.outs = [jax.ShapeDtypeStruct((segs * rows, width), array.dtype)]
        self.out_specs = [ANY]
        self.scratch = [SEND((2,)), SEND((2,)), SEND(())]

    def run(self, at, ins, outs, scratch):
        (src,), (dst,) = ins, outs
        send, recv, here = scratch
        chunk = lax.rem(at.key, 2)

        def part(index):
            return dst.at[span(index, self.rows), :]

        def out(seg):
            target = seg * LOCAL + at.key // 2
            return target, remote(
                src.at[seg], part(chunk), send.at[seg], recv.at[chunk], (at.grp, target)
            )

        for seg in range(2):
            target, copy = out(seg)
            pl.when(target != at.key)(copy.start)
            pl.when(target == at.key)(local(src.at[seg], part(chunk), here).start)
        yield
        yield "last"
        for seg in range(2):
            target, copy = out(seg)
            pl.when(target != at.key)(copy.wait_send)
        for index in range(2):
            owner = 2 * at.rank + index
            copy = remote(src.at[0], part(index), send.at[0], recv.at[index], (at.grp, owner))
            pl.when(owner != at.key)(copy.wait_recv)
            pl.when(owner == at.key)(local(src.at[0], part(index), here).wait)


class Chunks:
    def __init__(self, array):
        rows, width = array.shape
        self.arrays = [array]
        self.rows = rows // 2
        self.outs = [jax.ShapeDtypeStruct((2, rows // 2, width), array.dtype)]
        self.out_specs = [ANY]
        self.scratch = [SEND((2,)), SEND((2,)), SEND(())]

    def run(self, at, ins, outs, scratch):
        (src,), (dst,) = ins, outs
        send, recv, here = scratch

        def part(index):
            return src.at[pl.ds(index * self.rows, self.rows), :]

        def out(index):
            target = 2 * at.rank + index
            return target, remote(
                part(index), dst.at[at.seg], send.at[index], recv.at[at.seg], (at.grp, target)
            )

        for index in range(2):
            target, copy = out(index)
            pl.when(target != at.key)(copy.start)
            pl.when(target == at.key)(local(part(index), dst.at[at.seg], here).start)
        yield
        yield "last"
        for index in range(2):
            target, copy = out(index)
            pl.when(target != at.key)(copy.wait_send)
        for seg in range(2):
            owner = seg * LOCAL + at.key // 2
            copy = remote(part(0), dst.at[seg], send.at[0], recv.at[seg], (at.grp, owner))
            pl.when(owner != at.key)(copy.wait_recv)
            pl.when(owner == at.key)(local(part(0), dst.at[seg], here).wait)


class Memory:
    def __init__(self, array):
        self.arrays = [array]
        self.rows = array.shape[1]
        self.outs = [jax.ShapeDtypeStruct((2 * LOCAL * self.rows, PAIR), BF)]
        self.out_specs = [ANY]
        self.scratch = [SEND((2 * LOCAL,)), SEND((2 * LOCAL,)), SEND(())]

    def run(self, at, ins, outs, scratch):
        send, recv, here = scratch

        def copy(k):
            target = lax.rem(at.key + k, 2 * LOCAL)
            src = ins[0].at[target // LOCAL, :, span(lax.rem(target, LOCAL), PAIR)]
            dst = outs[0].at[span(at.key, self.rows), :]
            if k == 0:
                return local(src, dst, here)
            return remote(src, dst, send.at[k], recv.at[k], (at.grp, target))

        for k in range(2 * LOCAL):
            copy(k).start()
        yield
        yield "last"
        for k in range(2 * LOCAL):
            copy(k).wait()


class Docs:
    def __init__(self, array):
        rows, self.width = array.shape
        self.arrays = [array]
        self.outs = [jax.ShapeDtypeStruct((rows, 2 * LOCAL * self.width), array.dtype)]
        self.out_specs = [ANY]
        self.scratch = [SEND((2 * LOCAL,)), SEND((2 * LOCAL,)), SEND(())]

    def run(self, at, ins, outs, scratch):
        send, recv, here = scratch

        def copy(k):
            target = lax.rem(at.key + k, 2 * LOCAL)
            dst = outs[0].at[:, span(at.key, self.width)]
            if k == 0:
                return local(ins[0], dst, here)
            return remote(ins[0], dst, send.at[k], recv.at[k], (at.grp, target))

        for k in range(2 * LOCAL):
            copy(k).start()
        yield
        yield "last"
        for k in range(2 * LOCAL):
            copy(k).wait()


class Sibling:
    def __init__(self, array):
        self.arrays = [array]
        self.outs = [jax.ShapeDtypeStruct(array.shape, array.dtype)]
        self.out_specs = [ANY]
        self.scratch = [SEND(()), SEND(())]

    def run(self, at, ins, outs, scratch):
        copy = remote(ins[0], outs[0], scratch[0], scratch[1], at.sibling())
        copy.start()
        yield
        yield "last"
        copy.wait()


STEPS = [(da, db, dz) for db in range(2) for da in range(2) for dz in range(4)]


class Gather:
    def __init__(self, shards, blocks):
        self.arrays = list(shards)
        self.blocks = blocks
        self.outs = [jax.ShapeDtypeStruct(blocks.whole(4 * LOCAL), BF)]
        self.out_specs = [ANY]
        self.scratch = [SEND((36,)), SEND((36,)), SEND(())]
        self.scratch += [pltpu.VMEM(blocks.shape, BF), SEND((len(shards),))]

    def run(self, at, ins, outs, scratch):
        (whole,) = outs
        send, recv, here, shard, load = scratch
        core = at.core
        copies, begin = [], 0
        for index, src in enumerate(ins):
            cut = pl.ds(begin, src.shape[1])
            copies.append(local(src, shard.at[:, cut], load.at[index]))
            begin += src.shape[1]
        for copy_in in copies:
            copy_in.start()
        for copy_in in copies:
            copy_in.wait()

        def spot(step, of=core):
            return self.blocks.at(whole, at.chip(*step, of), of)

        def copy(step, slot, target):
            mine = isinstance(step[2], int) and step == (0, 0, 0)
            src = shard if mine else spot(step)
            return remote(src, spot(step), send.at[slot], recv.at[slot], target)

        def cross(step):
            da, db, dz = step
            return 20 + 8 * db + 4 * da + dz

        def first(dz):
            return copy((0, 0, dz), 8 + dz, at.device(1, 0, 0))

        def second(da, dz):
            return copy((da, 0, dz), 12 + 4 * da + dz, at.device(0, 1, 0))

        def across(step):
            return copy(step, cross(step), at.sibling())

        def arrived(step, slot):
            dst = spot(step)
            remote(dst, dst, send.at[slot], recv.at[slot], at.sibling()).wait_recv()

        inner = flip(at.z // 2, lax.rem(at.z, 2))
        near, turns = at.device(0, 0, 1), (1, 2 + inner, 3 - inner)
        far = at.device(0, 0, 3)
        inside = pl.when(inner == 1)

        def along_z(index):
            if index == 0:
                return remote(shard, spot((0, 0, 0)), send.at[0], recv.at[1], near)
            if index == 1:
                return remote(shard, spot((0, 0, 0)), send.at[1], recv.at[3], far)
            step, slot, device = {
                2: ((0, 0, 1), 2, far), 3: ((0, 0, 3), 2, near), 4: ((0, 0, 2), 3, near)
            }[index]
            return remote(spot(step), spot(step), send.at[index], recv.at[slot], device)

        mine = local(shard, spot((0, 0, 0)), here)
        mine.start()
        along_z(0).start()
        inside(along_z(1).start)
        first(0).start()
        second(0, 0).start()
        across((0, 0, 0)).start()
        yield
        for turn, dz in enumerate(turns):
            arrived((0, 0, dz), dz)
            inside(along_z((2, 3, 4)[turn]).start)
            first(dz).start()
            second(0, dz).start()
            across((0, 0, dz)).start()
            yield
        for dz in (0,) + turns:
            arrived((1, 0, dz), 8 + dz)
            second(1, dz).start()
            across((1, 0, dz)).start()
        yield
        for da in range(2):
            for dz in (0,) + turns:
                arrived((da, 1, dz), 12 + 4 * da + dz)
                across((da, 1, dz)).start()
        yield "last"
        for step in STEPS:
            dst = spot(step, 1 - core)
            slot = cross(step)
            remote(dst, dst, send.at[slot], recv.at[slot], at.sibling()).wait_recv()
        along_z(0).wait_send()
        for index in range(1, 5):
            inside(along_z(index).wait_send)
        for dz in range(4):
            first(dz).wait_send()
            for da in range(2):
                second(da, dz).wait_send()
        for step in STEPS:
            across(step).wait_send()
        mine.wait()


def tile_of(rows, width):
    sizes = [width // n for n in range(1, width // HEAD + 1) if width % (n * HEAD) == 0]
    return next((size for size in sizes if rows * size <= 32768), HEAD)


def add_into(dst, parts):
    rows, width = dst.shape
    tile = tile_of(rows, width)

    def one(cut):
        total = parts[0][:, cut].astype(F32)
        for part in parts[1:]:
            total += part[:, cut].astype(F32)
        dst[:, cut] = total.astype(dst.dtype)

    if tile == width:
        one(pl.ds(0, width))
    else:

        @pl.loop(0, width // tile)
        def _(t):
            one(pl.ds(pl.multiple_of(t * tile, tile), tile))


class Front:
    def __init__(self, tokens, shards, blocks, gains, gain_blocks, rest):
        self.rest = rest
        self.parts = [Gather(shards, blocks), Gather([gains], gain_blocks), Rows(tokens)]
        (rows,) = self.parts[2].outs
        rows, width = rows.shape
        columns = blocks.shape[1]
        qkv = jax.ShapeDtypeStruct((rows, columns), BF)
        self.swap = Swap([qkv], True)
        self.arrays = [array for part in self.parts for array in part.arrays]
        self.outs = [part.outs[0] for part in self.parts]
        self.outs += [jax.ShapeDtypeStruct((rows, width), BF)] + self.swap.outs
        self.out_specs = [ANY] * 3 + [VMEM] + self.swap.out_specs
        self.scratch = [s for part in self.parts for s in part.scratch] + self.swap.scratch
        self.scratch += [
            pltpu.VMEM((width, columns), BF),
            pltpu.VMEM((rows, width), BF),
            pltpu.VMEM(self.parts[1].outs[0].shape, BF),
            pltpu.VMEM((rows, columns), BF),
            SEND((3,)),
        ]

    def run(self, at, ins, outs, scratch):
        stages, rest, given = [], list(scratch), list(ins)
        for index, part in enumerate(self.parts):
            held = [rest.pop(0) for _ in part.scratch]
            taken = [given.pop(0) for _ in part.arrays]
            stages.append(part.run(at, taken, [outs[index]], held))
        swap_scratch = [rest.pop(0) for _ in self.swap.scratch]
        weights, tokens, gains, qkv, load = rest
        normed, swapped = outs[3], outs[4:]
        gathers, rows = stages[:2], stages[2]

        def step():
            for stage in gathers:
                next(stage)

        step()
        yield
        for _ in range(3):
            step()
        next(rows)
        yield
        step()
        step()
        for stage in stages:
            for _ in stage:
                pass
        copies = [
            local(src, dst, load.at[i])
            for i, (src, dst) in enumerate(zip((outs[2], outs[1], outs[0]), (tokens, gains, weights)))
        ]
        for copy in copies:
            copy.start()
        yield
        for copy in copies:
            copy.wait()
        values = tokens[...].astype(F32)
        gain = gains[...].astype(F32).T[0:1, :]
        normed[...] = (values * inverse_rms(values) * gain).astype(BF)
        tile = 512

        @pl.loop(0, qkv.shape[1] // tile)
        def _(t):
            cut = pl.ds(pl.multiple_of(t * tile, tile), tile)
            qkv[:, cut] = dot_nn(normed[...], weights[:, cut]).astype(BF)

        for _ in range(self.rest):
            yield
        swap = self.swap.run(at, [qkv], swapped, swap_scratch)
        next(swap)
        yield
        yield "last"
        for _ in swap:
            pass


class Assemble:
    def __init__(self, groups, blocks, pieces):
        self.arrays = list(groups)
        self.blocks = blocks
        self.pieces = pieces
        self.outs = [jax.ShapeDtypeStruct(b.whole(4 * LOCAL), groups[0].dtype) for b in blocks]
        self.out_specs = [ANY] * len(blocks)
        n = len(pieces)
        self.scratch = [SEND((n, 16)), SEND((n, 16)), SEND((n, 16)), SEND((16,))]
        self.scratch += [pltpu.VMEM((16,) + groups[0].shape[1:], groups[0].dtype)]

    def run(self, at, ins, outs, scratch):
        send, recv, here, load, held = scratch

        def fetch(group, dz):
            slot = group * 4 + dz
            return local(ins[group].at[dz], held.at[slot], load.at[slot])

        def copies(group, dz, core):
            slot = group * 4 + dz
            chip = at.chip(group % 2, group // 2, dz, core)
            for index, (matrix, row, rows, column, width, down, over) in enumerate(self.pieces):
                block = self.blocks[matrix].at(outs[matrix], chip, core)
                dst = block.at[pl.ds(row, rows), pl.ds(column, width)]
                src = held.at[slot, pl.ds(down, rows), pl.ds(over, width)]
                yield src, dst, index, slot

        def across(src, dst, index, slot):
            return remote(src, dst, send.at[index, slot], recv.at[index, slot], at.sibling())

        def own(src, dst, index, slot):
            return local(src, dst, here.at[index, slot])

        def every(do):
            for group in range(4):

                @pl.loop(0, 4)
                def _(dz):
                    do(group, dz)

        every(lambda group, dz: fetch(group, dz).start())
        yield

        def give(group, dz):
            fetch(group, dz).wait()
            for copy in copies(group, dz, at.core):
                across(*copy).start()
                own(*copy).start()

        every(give)
        yield "last"

        def end(group, dz):
            for copy in copies(group, dz, at.core):
                across(*copy).wait_send()
                own(*copy).wait()
            for copy in copies(group, dz, 1 - at.core):
                across(*copy).wait_recv()

        every(end)


class Sort:
    def __init__(self, rank, *arrays):
        self.arrays = [rank, *arrays]
        self.outs = [jax.ShapeDtypeStruct(array.shape, array.dtype) for array in arrays]
        self.out_specs = [VMEM] * len(arrays)
        self.scratch = [pltpu.VMEM(array.shape, array.dtype) for array in self.arrays]
        self.scratch += [SEND((len(self.arrays),))]

    def run(self, at, ins, outs, scratch):
        held, load = scratch[:-1], scratch[-1]
        copies = [local(src, dst, load.at[i]) for i, (src, dst) in enumerate(zip(ins, held))]
        for copy in copies:
            copy.start()
        yield
        for copy in copies:
            copy.wait()
        rank = held[0]
        entries = rank.shape[1]
        tile = BLOCK

        @pl.loop(0, entries // tile)
        def _(t):
            at_row = lax.broadcasted_iota(jnp.int32, (tile, entries), 0) + t * tile
            moved = jnp.where(rank[...] == at_row, 1.0, 0.0).astype(BF)
            for src, dst in zip(held[1:], outs):
                dst[pl.ds(pl.multiple_of(t * tile, tile), tile), :] = dot_nn(moved, src[...]).astype(BF)

        yield "last"


PACK = 16


class CoreSums:
    def __init__(self, *wholes):
        self.arrays = [whole for whole, _ in wholes]
        self.blocks = [blocks for _, blocks in wholes]
        shapes = [blocks.shape for blocks in self.blocks]
        self.width = sum(rows // PACK * width for rows, width in shapes)
        self.outs = [jax.ShapeDtypeStruct((n, PACK, self.width), BF) for n in (4, 4, 8)]
        self.out_specs = [ANY] * 3
        n = len(shapes)
        self.scratch = [pltpu.VMEM((16,) + shape, BF) for shape in shapes] * 2
        self.scratch += [pltpu.VMEM((16, PACK, self.width), BF)]
        self.scratch += [SEND((n, 16)), SEND((n, 16)), SEND((n, 16)), SEND((16,))]

    def run(self, at, ins, outs, scratch):
        n = len(ins)
        own, near, packed = scratch[:n], scratch[n : 2 * n], scratch[2 * n]
        load, send, recv, store = scratch[2 * n + 1 :]

        def chip(slot, core):
            return at.chip(lax.rem(slot // 4, 2), slot // 8, lax.rem(slot, 4), core)

        def fetch(index, slot):
            src = self.blocks[index].at(ins[index], chip(slot, at.core), at.core)
            return local(src, own[index].at[slot], load.at[index, slot])

        def across(index, slot):
            other = 1 - at.core
            src = self.blocks[index].at(ins[index], chip(slot, other), other)
            return remote(
                src, near[index].at[slot], send.at[index, slot], recv.at[index, slot], at.sibling()
            )

        def keep(slot, group, first):
            return local(packed.at[slot], outs[group].at[slot - first], store.at[slot])

        @pl.loop(0, 16)
        def _(turn):
            for index in range(n):
                across(index, 15 - turn).start()
                fetch(index, 15 - turn).start()

        yield
        groups = ((2, 8, 8), (1, 4, 4), (0, 0, 4))
        for group, first, count in groups:

            @pl.loop(0, count)
            def _(turn):
                slot = first + count - 1 - turn
                begin = 0
                for index in range(n):
                    fetch(index, slot).wait()
                    across(index, slot).wait_recv()
                    rows, width = self.blocks[index].shape
                    for part in range(rows // PACK):
                        cut = pl.ds(part * PACK, PACK)
                        add_into(
                            packed.at[slot, :, pl.ds(begin, width)],
                            [own[index].at[slot, cut, :], near[index].at[slot, cut, :]],
                        )
                        begin += width
                keep(slot, group, first).start()

            yield
        yield "last"
        for group, first, count in groups:

            @pl.loop(0, count)
            def _(turn):
                slot = first + count - 1 - turn
                for index in range(n):
                    across(index, slot).wait_send()
                keep(slot, group, first).wait()


def unpack(total, shapes):
    blocks, begin = [], 0
    for rows, width in shapes:
        parts = []
        for _ in range(rows // PACK):
            parts.append(total[:, begin : begin + width])
            begin += width
        blocks.append(jnp.concatenate(parts, axis=0))
    return blocks


class LineSums:
    def __init__(self, terms, shapes, cuts, rest=0):
        self.arrays = list(terms)
        self.rest = rest
        self.shapes = shapes
        self.outs = [jax.ShapeDtypeStruct(shape, F32) for shape in shapes]
        self.out_specs = [VMEM] * len(shapes)
        self.segments, begin = [], 0
        for index, (rows, width) in enumerate(shapes):
            for part in range(rows // PACK):
                self.segments.append((index, part, begin, width))
                begin += width
        self.pieces = []
        for group in cuts:
            held = [s for s in self.segments if s[0] in group]
            first = held[0][2]
            self.pieces.append((first, held[-1][2] + held[-1][3] - first, held))
        n = len(self.pieces)
        box = (PACK, begin)
        self.scratch = [pltpu.VMEM((4,) + box, BF) for _ in terms]
        self.scratch += [pltpu.VMEM((4,) + box, BF), pltpu.VMEM((4,) + box, BF)]
        self.scratch += [pltpu.VMEM((2,) + box, BF), pltpu.VMEM(box, BF)]
        self.scratch += [SEND((len(terms), 4)), SEND((6, n)), SEND((6, n))]

    def run(self, at, ins, outs, scratch):
        n = len(ins)
        terms = scratch[:n]
        low, outer_box, far_box, inner_box, load, send, recv = scratch[n:]
        inner = flip(at.z // 2, lax.rem(at.z, 2))
        inside, outside = pl.when(inner == 1), pl.when(inner == 0)
        near, far = at.device(0, 0, 1), at.device(0, 0, 3)
        pieces = range(len(self.pieces))

        def fetch(index, dz):
            return local(ins[index].at[dz], terms[index].at[dz], load.at[index, dz])

        def columns_of(c):
            first, width, _ = self.pieces[c]
            return pl.ds(first, width)

        def hand(kind, c):
            cut = columns_of(c)
            src, dst, target = {
                1: (low.at[1, :, cut], outer_box.at[1, :, cut], near),
                2: (low.at[2, :, cut], outer_box.at[2, :, cut], near),
                3: (low.at[3, :, cut], outer_box.at[3, :, cut], near),
                0: (low.at[3, :, cut], far_box.at[0, :, cut], far),
                4: (low.at[2, :, cut], far_box.at[1, :, cut], far),
                5: (low.at[1, :, cut], inner_box.at[:, cut], near),
            }[kind]
            return remote(src, dst, send.at[kind, c], recv.at[kind, c], target)

        def settle(c, dz, more):
            for _, _, begin, width in self.pieces[c][2]:
                cut = pl.ds(begin, width)
                parts = [term.at[dz, :, cut] for term in terms] + [m.at[:, cut] for m in more]
                add_into(low.at[dz, :, cut], parts)

        def finish(c, more):
            for index, part, begin, width in self.pieces[c][2]:
                cut = pl.ds(begin, width)
                parts = [term.at[0, :, cut] for term in terms] + [m.at[:, cut] for m in more]
                add_into(outs[index].at[pl.ds(part * PACK, PACK), :], parts)

        for dz in (2, 3, 1, 0):
            for index in range(n):
                fetch(index, dz).start()
        yield
        for dz in (2, 3, 1, 0):
            for index in range(n):
                fetch(index, dz).wait()

        @outside
        def _():
            for c in pieces:
                for dz in (2, 3, 1):
                    settle(c, dz, [])
                    hand(dz, c).start()

        def inwards(c):
            @inside
            def _():
                hand(2, c).wait_recv()
                settle(c, 3, [outer_box.at[2]])
                hand(0, c).start()
                hand(3, c).wait_recv()
                settle(c, 2, [outer_box.at[3]])
                hand(4, c).start()

        def outwards(c):
            @inside
            def _():
                hand(4, c).wait_recv()
                settle(c, 1, [far_box.at[1]])
                hand(5, c).start()
                hand(0, c).wait_recv()
                hand(1, c).wait_recv()
                finish(c, [outer_box.at[1], far_box.at[0]])

            @outside
            def _():
                hand(5, c).wait_recv()
                finish(c, [inner_box])

        for _ in range(1 + self.rest):
            yield
        for c in pieces:
            inwards(c)
            yield
            if c:
                outwards(c - 1)
                yield
        yield "last"
        outwards(len(self.pieces) - 1)
        for c in pieces:

            @outside
            def _():
                for kind in (1, 2, 3):
                    hand(kind, c).wait_send()

            @inside
            def _():
                for kind in (0, 4, 5):
                    hand(kind, c).wait_send()


class Scatter:
    def __init__(self, whole, blocks, turn=0):
        self.arrays = [whole]
        self.blocks = blocks
        self.turn = turn
        shape = blocks.shape
        self.pair = isinstance(blocks, PairBlocks)
        out = (shape[0] // 2, 2 * shape[1]) if self.pair else shape
        self.outs = [jax.ShapeDtypeStruct(out, F32)]
        self.out_specs = [VMEM]
        dma = SEND
        self.scratch = [
            pltpu.VMEM((16,) + shape, BF),
            pltpu.VMEM((16,) + shape, BF),
            pltpu.VMEM((8,) + shape, BF),
            pltpu.VMEM((4,) + shape, BF),
            pltpu.VMEM((4,) + shape, BF),
            dma((16,)),
            dma((32,)),
            dma((32,)),
        ]
        if self.pair:
            self.scratch += [pltpu.VMEM(shape, F32), dma((2,))]

    def run(self, at, ins, outs, scratch):
        (whole,), (out,) = ins, outs
        own, near, from_b, from_a, from_z, load, send, recv = scratch[:8]
        core = at.core
        order = list(reversed(STEPS))

        def fetch(slot):
            src = self.blocks.at(whole, at.chip(*STEPS[slot], core), core)
            return local(src, own.at[slot], load.at[slot])

        def across(slot):
            src = self.blocks.at(whole, at.chip(*STEPS[slot], 1 - core), 1 - core)
            return remote(src, near.at[slot], send.at[slot], recv.at[slot], at.sibling())

        def second(da, dz):
            slot = STEPS.index((da, 1, dz))
            spot = 4 * da + dz
            return remote(
                own.at[slot], from_b.at[spot], send.at[16 + spot], recv.at[16 + spot],
                at.device(0, 1, 0),
            )

        def first(dz):
            slot = STEPS.index((1, 0, dz))
            return remote(
                own.at[slot], from_a.at[dz], send.at[24 + dz], recv.at[24 + dz], at.device(1, 0, 0)
            )

        def along_z(dz):
            slot = STEPS.index((0, 0, dz))
            return remote(
                own.at[slot], from_z.at[dz], send.at[28 + dz], recv.at[28 + dz], at.device(0, 0, dz)
            )

        for step in order:
            slot = STEPS.index(step)
            across(slot).start()
            fetch(slot).start()
        for _ in range(1 + self.turn):
            yield

        def settle(step, more, dst=None):
            slot = STEPS.index(step)
            fetch(slot).wait()
            across(slot).wait_recv()
            parts = [own.at[slot], near.at[slot]] + more
            add_into(own.at[slot] if dst is None else dst, parts)

        for da in (1, 0):
            for dz in (3, 2, 1, 0):
                settle((da, 1, dz), [])
                second(da, dz).start()
        yield
        for dz in (3, 2, 1, 0):
            second(1, dz).wait_recv()
            settle((1, 0, dz), [from_b.at[4 + dz]])
            first(dz).start()
        yield
        for dz in (3, 2, 1):
            second(0, dz).wait_recv()
            first(dz).wait_recv()
            settle((0, 0, dz), [from_b.at[dz], from_a.at[dz]])
            along_z(dz).start()
        yield "last"
        second(0, 0).wait_recv()
        first(0).wait_recv()
        for dz in (1, 2, 3):
            along_z(dz).wait_recv()
        total = scratch[8] if self.pair else out
        more = [from_b.at[0], from_a.at[0]] + [from_z.at[dz] for dz in (1, 2, 3)]
        settle((0, 0, 0), more, total)
        if self.pair:
            rows, width = self.blocks.shape
            half = rows // 2
            columns = span(core, width)
            swap = remote(
                total.at[span(1 - core, half), :], out.at[:, columns],
                scratch[9].at[0], scratch[9].at[1], at.sibling(),
            )
            swap.start()
            out[:, columns] = total[span(core, half), :]
        if self.pair:
            swap.wait()
        for slot in range(16):
            across(slot).wait_send()
        for dz in range(4):
            for da in range(2):
                second(da, dz).wait_send()
            first(dz).wait_send()
            if dz:
                along_z(dz).wait_send()


def later(part, steps=2):
    part.wait = steps
    return part


def staged(part, *refs):
    for _ in range(getattr(part, "wait", 0)):
        yield
    yield from part.run(*refs)


def exchange(name, collective, parts):
    sizes = [(len(p.arrays), len(p.outs), len(p.scratch)) for p in parts]
    n_in = sum(size[0] for size in sizes)
    n_out = sum(size[1] for size in sizes)

    def kernel(*refs):
        at = Place()
        barrier = pltpu.get_barrier_semaphore()
        near = [(at.grp, lax.rem(at.key + k, 2 * LOCAL)) for k in range(1, 2 * LOCAL)]
        near += [at.device(1, 0, 0), at.device(0, 1, 0)]
        for device in near:
            pl.semaphore_signal(barrier, inc=1, device_id=device, device_id_type=MESH)
        pl.semaphore_wait(barrier, len(near))
        ins, outs, scratch = refs[:n_in], refs[n_in : n_in + n_out], refs[n_in + n_out :]
        live = []
        sums = any(isinstance(part, Scatter) for part in parts)
        for part, (i, o, s) in zip(parts, sizes):
            live.append(staged(part, at, ins[:i], outs[:o], scratch[:s]))
            ins, outs, scratch = ins[i:], outs[o:], scratch[s:]
        for stage in live:
            next(stage)
        ending = []
        while live:
            for stage in list(reversed(live) if sums else live):
                if next(stage) == "last":
                    live.remove(stage)
                    ending.append(stage)
        for stage in ending:
            for _ in stage:
                pass

    outs = pl.pallas_call(
        kernel,
        name=name,
        out_shape=[o for p in parts for o in p.outs],
        in_specs=[ANY] * n_in,
        out_specs=[o for p in parts for o in p.out_specs],
        scratch_shapes=[s for p in parts for s in p.scratch],
        compiler_params=pltpu.CompilerParams(
            collective_id=collective, has_side_effects=True, vmem_limit_bytes=ROOM
        ),
    )(*[a for p in parts for a in p.arrays])
    outs = list(outs)
    return [[outs.pop(0) for _ in p.outs] for p in parts]


def hop(values, change):
    pairs = []
    for y in range(2):
        for x in range(2):
            for z in range(LOCAL):
                for core in range(2):
                    to = [y, x, z, core]
                    if change in ("a", "b"):
                        to[1 if (change == "a") == (core == 0) else 0] ^= 1
                    elif change == "core":
                        to[3] ^= 1
                    else:
                        to[2] ^= change
                    number = [((v[0] * 2 + v[1]) * LOCAL + v[2]) * 2 + v[3] for v in ([y, x, z, core], to)]
                    pairs.append(tuple(number))
    return lax.ppermute(values, ("grp", "key"), pairs)


def column_hop(values, pairs):
    size = 2 * LOCAL
    every = [(g * size + s, g * size + t) for g in range(4) for s, t in pairs]
    return lax.ppermute(values, ("grp", "key"), every)


def join(value, others):
    return lax.optimization_barrier((value, others))


def gather_column(shard):
    return jnp.stack([shard] + [hop(shard, dz) for dz in (1, 2, 3)])


def add(*terms):
    return sum(term.astype(F32) for term in terms)


def scatter_second(sums):
    here, first, second = sums
    return here, first, hop(second, "b")


def scatter_first(sums):
    here, first, got = sums
    return here, got, hop(add(first, got[4:]).astype(BF), "a")


def scatter_z(sums):
    here, got, more = sums
    total = add(here, got[:4], more)
    low = total[1:].astype(BF)
    return [total[0]] + [hop(low[dz - 1], dz) for dz in (1, 2, 3)]


def scatter_end(sums):
    return add(*sums)


def rows_hops(chunks):
    odd = lax.rem(lax.axis_index("key"), 2) == 1
    size = 2 * LOCAL
    same = [(j, j // 2 + LOCAL * (j % 2)) for j in range(size)]
    cross = [(j, j // 2 + LOCAL * (1 - j % 2)) for j in range(size)]
    one = column_hop(jnp.where(odd, chunks[1], chunks[0]), same)
    two = column_hop(jnp.where(odd, chunks[0], chunks[1]), cross)
    upper = lax.axis_index("key") >= LOCAL
    return jnp.concatenate((jnp.where(upper, two, one), jnp.where(upper, one, two)))


def chunk_hops(rows):
    half = rows.shape[0] // 2
    odd = lax.rem(lax.axis_index("key"), 2) == 1
    upper = lax.axis_index("key") >= LOCAL
    size = 2 * LOCAL
    same = [(j // 2 + LOCAL * (j % 2), j) for j in range(size)]
    cross = [(j // 2 + LOCAL * (1 - j % 2), j) for j in range(size)]
    one = column_hop(jnp.where(upper, rows[half:], rows[:half]), same)
    two = column_hop(jnp.where(upper, rows[:half], rows[half:]), cross)
    return jnp.stack((jnp.where(odd, two, one), jnp.where(odd, one, two)))


def dot_nt(a, b):
    return lax.dot_general(a, b, (((1,), (1,)), ((), ())), preferred_element_type=F32)


def dot_nn(a, b):
    return lax.dot_general(a, b, (((1,), (0,)), ((), ())), preferred_element_type=F32)


def heads(index):
    return pl.ds(index * HEAD, HEAD)


def block_rows(j):
    return pl.ds(pl.multiple_of(j * BLOCK, BLOCK), BLOCK)


def turned(values):
    return values.astype(F32).T.astype(BF)


def transpose_blocks(src, dst):
    @pl.loop(0, src.shape[0] // BLOCK)
    def _(j):
        dst[j] = turned(src[block_rows(j), :])


def visible(bounds, low, high, j):
    at = lax.broadcasted_iota(jnp.int32, (BLOCK, QUERIES), 0)
    start = j * BLOCK
    return (at >= bounds[low : low + 1, :] - start) & (at < bounds[high : high + 1, :] - start)


def fold(values):
    return values.reshape(values.shape[0] // 8, 8, values.shape[1])


def each_block(ranges, i, with_memory, local_body, memory_body):
    begin, full, diagonal, end = (ranges[i, k] for k in range(4))
    lax.fori_loop(begin, full, local_body(True), 0)
    lax.fori_loop(full, diagonal, local_body(False), 0)
    lax.fori_loop(diagonal, end, local_body(True), 0)
    if with_memory:
        begin, full, rest, end = (ranges[i, k] for k in range(4, 8))
        lax.fori_loop(begin, full, memory_body(True), 0)
        lax.fori_loop(full, rest, memory_body(False), 0)
        lax.fori_loop(rest, end, memory_body(True), 0)


def attend_kernel(with_memory, ranges, *refs):
    if with_memory:
        q, k, v, bounds, mk, mv, out, stat, vt, mvt, scores, acc, top, total = refs
    else:
        q, k, v, bounds, out, stat, vt, scores, acc, top, total = refs
        mk = mvt = None
    i = pl.program_id(0)
    scale = HEAD ** (-0.5) * LOG2E
    blocks = vt.shape[0]

    @pl.when(i == 0)
    def _():
        transpose_blocks(v, vt)
        if with_memory:
            transpose_blocks(mv, mvt)

    acc[...] = jnp.zeros_like(acc)
    top[...] = jnp.full_like(top, NEG)
    total[...] = jnp.zeros_like(total)

    def scan(keys, first, low):
        def run(masked):
            def body(j, _):
                for h in range(2):
                    part = dot_nt(keys[block_rows(j), heads(h)], q[:, heads(h)])
                    if masked:
                        part = jnp.where(visible(bounds, low, low + 1, j), part, NEG)
                    scores[h, first + j] = part
                    top[h] = jnp.maximum(top[h], jnp.max(fold(part), axis=0))
                return 0

            return body

        return run

    each_block(ranges, i, with_memory, scan(k, 0, 0), scan(mk, blocks, 2))
    tops = [jnp.max(top[h], axis=0, keepdims=True) * scale for h in range(2)]

    def take(values_t, first):
        def run(masked):
            def body(j, _):
                for h in range(2):
                    probs = jnp.exp2(scores[h, first + j] * scale - tops[h])
                    total[h] += jnp.sum(fold(probs), axis=0)
                    acc[heads(h), :] += dot_nn(values_t[j, heads(h), :], probs.astype(BF))
                return 0

            return body

        return run

    lax.fori_loop(ranges[i, 0], ranges[i, 3], take(vt, 0)(False), 0)
    if with_memory:
        lax.fori_loop(ranges[i, 4], ranges[i, 7], take(mvt, blocks)(False), 0)
    for h in range(2):
        share = jnp.sum(total[h], axis=0, keepdims=True)
        out[:, heads(h)] = (acc[heads(h), :] / share).T.astype(BF)
        stat[h : h + 1, :] = tops[h] + jnp.log2(share)
    stat[2:, :] = jnp.zeros_like(stat[2:, :])


def attend(q, k, v, memory, bounds, ranges):
    rows = q.shape[0]
    blocks = rows // BLOCK
    row_block = pl.BlockSpec((QUERIES, PAIR), lambda i, *_: (i, 0))
    lane_block = pl.BlockSpec((8, QUERIES), lambda i, *_: (0, i))
    operands = [q, k, v, bounds]
    in_specs = [row_block, VMEM, VMEM, lane_block]
    scratch = [pltpu.VMEM((blocks, PAIR, BLOCK), BF)]
    if memory is not None:
        operands += [memory[0], memory[1]]
        in_specs += [VMEM, VMEM]
        more = memory[1].shape[0] // BLOCK
        scratch += [pltpu.VMEM((more, PAIR, BLOCK), BF)]
        blocks += more
    return pl.pallas_call(
        functools.partial(attend_kernel, memory is not None),
        name="attend",
        grid_spec=pltpu.PrefetchScalarGridSpec(
            num_scalar_prefetch=1,
            grid=(rows // QUERIES,),
            in_specs=in_specs,
            out_specs=(row_block, lane_block),
            scratch_shapes=scratch
            + [
                pltpu.VMEM((2, blocks, BLOCK, QUERIES), F32),
                pltpu.VMEM((PAIR, QUERIES), F32),
                pltpu.VMEM((2, 8, QUERIES), F32),
                pltpu.VMEM((2, 8, QUERIES), F32),
            ],
        ),
        out_shape=(
            jax.ShapeDtypeStruct((rows, PAIR), BF),
            jax.ShapeDtypeStruct((8, rows), F32),
        ),
        compiler_params=pltpu.CompilerParams(vmem_limit_bytes=ROOM),
    )(ranges, *operands)


def attend_back_kernel(with_memory, ranges, *refs):
    if with_memory:
        (q, go, o, stat, bounds, k, v, mk, mv, gq, gk, gv, kt, mkt, delta, gq_t, gk_sum, gv_sum) = refs
    else:
        (q, go, o, stat, bounds, k, v, gq, gk, gv, kt, delta, gq_t, gk_sum, gv_sum) = refs
        mk = mv = mkt = None
    i = pl.program_id(0)
    unit = HEAD ** (-0.5)
    scale = unit * LOG2E

    @pl.when(i == 0)
    def _():
        transpose_blocks(k, kt)
        gk_sum[...] = jnp.zeros_like(gk_sum)
        gv_sum[...] = jnp.zeros_like(gv_sum)
        if with_memory:
            transpose_blocks(mk, mkt)

    for h in range(2):
        both = go[:, heads(h)].astype(F32) * o[:, heads(h)].astype(F32)
        delta[h : h + 1, :] = jnp.sum(both.T, axis=0, keepdims=True)
    gq_t[...] = jnp.zeros_like(gq_t)

    def step(keys, values, keys_t, low, own):
        def run(masked):
            def body(j, _):
                for h in range(2):
                    query, grad = q[:, heads(h)], go[:, heads(h)]
                    scores = dot_nt(keys[block_rows(j), heads(h)], query) * scale
                    probs = jnp.exp2(scores - stat[h : h + 1, :])
                    if masked:
                        probs = jnp.where(visible(bounds, low, low + 1, j), probs, 0.0)
                    grad_probs = dot_nt(values[block_rows(j), heads(h)], grad)
                    grad_scores = (probs * (grad_probs - delta[h : h + 1, :])).astype(BF)
                    gq_t[heads(h), :] += dot_nn(keys_t[j, heads(h), :], grad_scores)
                    if own:
                        gv_sum[block_rows(j), heads(h)] += dot_nn(probs.astype(BF), grad)
                        gk_sum[block_rows(j), heads(h)] += dot_nn(grad_scores, query)
                return 0

            return body

        return run

    each_block(ranges, i, with_memory, step(k, v, kt, 0, True), step(mk, mv, mkt, 2, False))
    gq[...] = (gq_t[...] * unit).T.astype(BF)

    @pl.when(i == pl.num_programs(0) - 1)
    def _():
        gk[...] = (gk_sum[...] * unit).astype(BF)
        gv[...] = gv_sum[...].astype(BF)


def attend_back(q, k, v, memory, bounds, ranges, out, stat, grad):
    rows = q.shape[0]
    blocks = rows // BLOCK
    row_block = pl.BlockSpec((QUERIES, PAIR), lambda i, *_: (i, 0))
    lane_block = pl.BlockSpec((8, QUERIES), lambda i, *_: (0, i))
    operands = [q, grad, out, stat, bounds, k, v]
    in_specs = [row_block, row_block, row_block, lane_block, lane_block, VMEM, VMEM]
    scratch = [pltpu.VMEM((blocks, PAIR, BLOCK), BF)]
    if memory is not None:
        operands += [memory[0], memory[1]]
        in_specs += [VMEM, VMEM]
        scratch += [pltpu.VMEM((memory[0].shape[0] // BLOCK, PAIR, BLOCK), BF)]
    whole = jax.ShapeDtypeStruct((rows, PAIR), BF)
    return pl.pallas_call(
        functools.partial(attend_back_kernel, memory is not None),
        name="attend_back",
        grid_spec=pltpu.PrefetchScalarGridSpec(
            num_scalar_prefetch=1,
            grid=(rows // QUERIES,),
            in_specs=in_specs,
            out_specs=(row_block, VMEM, VMEM),
            scratch_shapes=scratch
            + [
                pltpu.VMEM((8, QUERIES), F32),
                pltpu.VMEM((PAIR, QUERIES), F32),
                pltpu.VMEM((rows, PAIR), F32),
                pltpu.VMEM((rows, PAIR), F32),
            ],
        ),
        out_shape=(whole, whole, whole),
        compiler_params=pltpu.CompilerParams(vmem_limit_bytes=ROOM),
    )(ranges, *operands)


NUMBERS = 8


def members(docs):
    number = jnp.arange(NUMBERS, dtype=jnp.int32)
    return (docs[None, :] == number[:, None]).astype(jnp.int32)


def before(counts):
    at = jnp.arange(counts.shape[-1])
    earlier = at[:, None] < at[None, :]
    return jnp.sum(jnp.where(earlier, counts[..., :, None], 0), axis=-2)


def pick(which, table):
    return jnp.sum(which * table[:, None], axis=0)


def mask_ranges(docs, mem_docs, reset):
    rows = docs.shape[0]
    at = jnp.arange(rows, dtype=jnp.int32)
    own, other = members(docs), members(mem_docs)
    start = pick(own, before(jnp.sum(own, axis=1)))
    counts = jnp.where(reset == 0, jnp.sum(other, axis=1), 0)
    mem_low = pick(own, before(counts))
    mem_high = mem_low + pick(own, counts)
    zero = jnp.zeros_like(start)
    bounds = jnp.stack((start, at + 1, mem_low, mem_high, zero, zero, zero, zero))

    def per_block(values):
        return values.reshape(rows // QUERIES, QUERIES)

    def up(values):
        return (values + BLOCK - 1) // BLOCK

    place = jnp.arange(rows // QUERIES, dtype=jnp.int32) * QUERIES
    diagonal, end = place // BLOCK, up(place + QUERIES)
    first = jnp.min(per_block(start), axis=1) // BLOCK
    full = jnp.clip(up(jnp.max(per_block(start), axis=1)), first, diagonal)
    some = mem_high > mem_low
    mem_first = jnp.min(per_block(jnp.where(some, mem_low, mem_docs.shape[0])), axis=1) // BLOCK
    mem_end = jnp.maximum(up(jnp.max(per_block(mem_high), axis=1)), mem_first)
    mem_full = jnp.clip(up(jnp.max(per_block(mem_low), axis=1)), mem_first, mem_end)
    mem_rest = jnp.clip(jnp.min(per_block(mem_high), axis=1) // BLOCK, mem_full, mem_end)
    columns = (first, full, diagonal, end, mem_first, mem_full, mem_rest, mem_end)
    return bounds, jnp.stack(columns, axis=1)


def memory_rank(mem_docs):
    entries = mem_docs.shape[0]
    which = members(mem_docs)
    lanes = which.reshape(-1, HEAD)
    at = jnp.arange(HEAD)
    earlier = (at[:, None] < at[None, :]).astype(BF)
    inside = jnp.dot(lanes.astype(BF), earlier, preferred_element_type=F32).astype(jnp.int32)
    totals = jnp.sum(lanes, axis=1).reshape(NUMBERS, -1)
    first = before(jnp.sum(totals, axis=1))[:, None] + before(totals)
    rank = inside.reshape(NUMBERS, -1, HEAD) + first[:, :, None]
    rank = jnp.sum(which * rank.reshape(NUMBERS, entries), axis=0)
    return rank[None]


def columns(matrix, sizes):
    pieces, at = [], 0
    for size in sizes:
        pieces.append(matrix[:, at : at + size])
        at += size
    return pieces


def dot_tn(a, b):
    return lax.dot_general(a, b, (((0,), (0,)), ((), ())), preferred_element_type=F32)


FEED = 256


def inverse_rms(values):
    return lax.rsqrt(jnp.mean(values * values, axis=-1, keepdims=True) + EPS)


def norm_back(values, gain, grad):
    inverse = inverse_rms(values)
    scaled = grad * gain
    mean = jnp.mean(scaled * values, axis=-1, keepdims=True)
    grad_gain = jnp.sum(grad * values * inverse, axis=0, keepdims=True)
    return inverse * scaled - values * (inverse * inverse * inverse) * mean, grad_gain


def feed_kernel(att, stream, out_w, gain, gate_w, up_w, down_w, result, mixed, normed, gate, up):
    step = pl.program_id(0)

    @pl.when(step == 0)
    def _():
        both = stream[...].astype(F32) + dot_nn(att[...], out_w[...])
        mixed[...] = both
        normed[...] = (both * inverse_rms(both) * gain[...]).astype(BF)
        result[...] = both

    gated = dot_nn(normed[...], gate_w[...])
    raised = dot_nn(normed[...], up_w[...])
    gate[...] = gated
    up[...] = raised
    activated = (gated * jax.nn.sigmoid(gated) * raised).astype(BF)
    result[...] += dot_nn(activated, down_w[...])


def feed(attended, stream, out_w, gain, gate_up_w, down_w):
    rows, width = stream.shape
    ff = down_w.shape[0]
    steps = ff // FEED
    part = pl.BlockSpec((rows, FEED), lambda f: (0, f))
    whole = jax.ShapeDtypeStruct((rows, width), F32)
    narrow = jax.ShapeDtypeStruct((rows, width), BF)
    wide = jax.ShapeDtypeStruct((rows, ff), F32)
    return pl.pallas_call(
        feed_kernel,
        name="feed",
        grid=(steps,),
        in_specs=[
            VMEM, VMEM, VMEM, VMEM,
            pl.BlockSpec((width, FEED), lambda f: (0, f)),
            pl.BlockSpec((width, FEED), lambda f: (0, steps + f)),
            pl.BlockSpec((FEED, width), lambda f: (f, 0)),
        ],
        out_specs=(VMEM, VMEM, VMEM, part, part),
        out_shape=(whole, whole, narrow, wide, wide),
        compiler_params=pltpu.CompilerParams(vmem_limit_bytes=ROOM),
    )(attended, stream, out_w, gain, gate_up_w, gate_up_w, down_w)


def feed_back_kernel(
    grad_new, gate, up, normed, mixed, gain, att, out_w, gate_w, up_w, down_w,
    gate_g, up_g, down_g, grad_mixed, grad_att, out_g, gain_g, branch, normed_t, total,
):
    step = pl.program_id(0)

    @pl.when(step == 0)
    def _():
        branch[...] = grad_new[...].astype(BF)
        normed_t[...] = turned(normed[...])
        total[...] = jnp.zeros_like(total)

    gated, raised = gate[...], up[...]
    sig = jax.nn.sigmoid(gated)
    swish = gated * sig
    grad_act = dot_nt(branch[...], down_w[...])
    down_g[...] = dot_tn((swish * raised).astype(BF), branch[...]).astype(BF)
    grad_gate = (grad_act * raised * sig * (1.0 + gated * (1.0 - sig))).astype(BF)
    grad_up = (grad_act * swish).astype(BF)
    gate_g[...] = dot_nn(normed_t[...], grad_gate).astype(BF)
    up_g[...] = dot_nn(normed_t[...], grad_up).astype(BF)
    total[...] += dot_nt(grad_gate, gate_w[...]) + dot_nt(grad_up, up_w[...])

    @pl.when(step == pl.num_programs(0) - 1)
    def _():
        back, grad_gain = norm_back(mixed[...], gain[...], total[...])
        both = grad_new[...].astype(F32) + back
        grad_mixed[...] = both
        gain_g[...] = grad_gain
        low = both.astype(BF)
        grad_att[...] = dot_nt(low, out_w[...]).astype(BF)
        out_g[...] = dot_tn(att[...], low).astype(BF)


def feed_back(grad_new, weights, kept):
    gain_a, qkv_w, out_w, gain, gate_up_w, down_w = weights
    attended, mixed, normed, gate, up = kept[7:]
    rows, width = grad_new.shape
    ff = down_w.shape[0]
    steps = ff // FEED
    part = pl.BlockSpec((rows, FEED), lambda f: (0, f))
    columns_of = pl.BlockSpec((width, FEED), lambda f: (0, f))
    rows_of = pl.BlockSpec((FEED, width), lambda f: (f, 0))

    def shape(a, b, kind=BF):
        return jax.ShapeDtypeStruct((a, b), kind)

    return pl.pallas_call(
        feed_back_kernel,
        name="feed_back",
        grid=(steps,),
        in_specs=[
            VMEM, part, part, VMEM, VMEM, VMEM, VMEM, VMEM,
            columns_of, pl.BlockSpec((width, FEED), lambda f: (0, steps + f)), rows_of,
        ],
        out_specs=(columns_of, columns_of, rows_of, VMEM, VMEM, VMEM, VMEM),
        out_shape=(
            shape(width, ff), shape(width, ff), shape(ff, width),
            shape(rows, width, F32), shape(rows, width), shape(width, width), shape(1, width, F32),
        ),
        scratch_shapes=[
            pltpu.VMEM((rows, width), BF), pltpu.VMEM((width, rows), BF), pltpu.VMEM((rows, width), F32),
        ],
        compiler_params=pltpu.CompilerParams(vmem_limit_bytes=ROOM),
    )(grad_new, gate, up, normed, mixed, gain, attended, out_w, gate_up_w, gate_up_w, down_w)


def project_kernel(grad_mixed, stream, gain, normed, grad_qkv, qkv_w, qkv_g, grad_stream, gain_g, normed_t, total):
    step = pl.program_id(0)

    @pl.when(step == 0)
    def _():
        normed_t[...] = turned(normed[...])
        total[...] = jnp.zeros_like(total)

    qkv_g[...] = dot_nn(normed_t[...], grad_qkv[...]).astype(BF)
    total[...] += dot_nt(grad_qkv[...], qkv_w[...])

    @pl.when(step == pl.num_programs(0) - 1)
    def _():
        back, grad_gain = norm_back(stream[...].astype(F32), gain[...], total[...])
        grad_stream[...] = (grad_mixed[...] + back).astype(grad_stream.dtype)
        gain_g[...] = grad_gain


def projections_back(grad_mixed, grad_qkv, weights, kept, kind):
    gain, qkv_w = weights[:2]
    stream, normed = kept[:2]
    rows, width = stream.shape
    size = 1024
    part = pl.BlockSpec((width, size), lambda f: (0, f))
    grad_qkv_w, grad_stream, grad_gain = pl.pallas_call(
        project_kernel,
        name="projections_back",
        grid=(grad_qkv.shape[1] // size,),
        in_specs=[VMEM, VMEM, VMEM, VMEM, pl.BlockSpec((rows, size), lambda f: (0, f)), part],
        out_specs=(part, VMEM, VMEM),
        out_shape=(
            jax.ShapeDtypeStruct(qkv_w.shape, BF),
            jax.ShapeDtypeStruct((rows, width), kind),
            jax.ShapeDtypeStruct((1, width), F32),
        ),
        scratch_shapes=[pltpu.VMEM((width, rows), BF), pltpu.VMEM((rows, width), F32)],
        cost_estimate=pl.CostEstimate(
            flops=4 * rows * width * grad_qkv.shape[1],
            bytes_accessed=4 * width * grad_qkv.shape[1],
            transcendentals=0,
        ),
        compiler_params=pltpu.CompilerParams(vmem_limit_bytes=ROOM),
    )(grad_mixed, stream, gain, normed, grad_qkv, qkv_w)
    return grad_stream, grad_gain, grad_qkv_w


def layer(stream, normed, heads, qkv_w, gains, to_rows, memory, bounds, ranges):
    gain_a, gain_b = gains
    q, k, v = heads
    out, stat = attend(q, k, v, memory, bounds, ranges)
    attended, out_w, gate_up_w, down_w = to_rows(out)
    result, mixed, normed_ff, gate, up = feed(attended, stream, out_w, gain_b, gate_up_w, down_w)
    weights = (gain_a, qkv_w, out_w, gain_b, gate_up_w, down_w)
    kept = (stream, normed, q, k, v, out, stat, attended, mixed, normed_ff, gate, up)
    return result, weights, kept


def gain_columns(gains):
    stacked = jnp.stack(gains, axis=1)
    return jnp.pad(stacked, ((0, 0), (0, HEAD - len(gains))))


def pair_rows(own, other, core):
    rows, width = own.shape
    both = jnp.where(core == 0, jnp.stack((own, other)), jnp.stack((other, own)))
    return lax.dynamic_slice_in_dim(both.reshape(2 * rows, width), core * (width // 2), width // 2, 1)


def head_local(
    tokens, token_docs, memory_docs, memory_resets, memory_keys, memory_values,
    attn_gain1, query_weight1, key_weight1, value_weight1, out_weight1,
    ffn_gain1, gate_weight1, up_weight1, down_weight1,
    attn_gain2, second_query_weight, key_weight2, value_weight2, out_weight2,
    ffn_gain2, gate_weight2, up_weight2, down_weight2, cotangent,
):
    count, width = query_weight1.shape
    ff = gate_weight1.shape[1]
    each = down_weight1.shape[0]
    core = lax.rem(lax.axis_index("key"), 2)
    seg = lax.axis_index("key") // LOCAL
    gains = gain_columns((attn_gain1, ffn_gain1, attn_gain2, ffn_gain2))
    downs = jnp.concatenate((down_weight1, down_weight2), axis=0)
    docs = jnp.concatenate((token_docs, memory_docs), axis=0)
    pairs = PairBlocks(2 * each, width // 2)

    def own(*matrices):
        return RowBlocks(count, sum(matrix.shape[1] for matrix in matrices))

    def gather(*matrices):
        return Gather(matrices, own(*matrices))

    other = hop(downs, "core")
    down1 = pair_rows(down_weight1, other[:each], core)
    down2 = pair_rows(down_weight2, other[each:], core)
    groups = 2 * each // count
    tail = down2[groups * count :]
    half = width // 4
    rest2 = jnp.concatenate(
        [gate_weight2, up_weight2, out_weight2]
        + [down2[g * count : (g + 1) * count] for g in range(groups)]
        + [jnp.concatenate((tail[:, :half], tail[:, half:]))],
        axis=1,
    )
    over = 2 * ff + width
    pieces = [(0, 0, count, 0, 2 * ff, 0, 0), (1, 0, count, 0, width, 0, 2 * ff)]
    pieces += [(2, g * count, count, 0, 2 * half, 0, over + 2 * g * half) for g in range(groups)]
    over += 2 * groups * half
    pieces += [(2, groups * count, count // 2, p * half, half, p * count // 2, over) for p in range(2)]
    first1 = (query_weight1, key_weight1, value_weight1)
    front, (docs,), (mk,), (mv,), (gu1_w,), (down1_w,), (out1_w,), (qkv2_w,) = exchange(
        "front", 1,
        [Front(tokens, first1, own(*first1), gains, own(gains), 3), Docs(docs),
         later(Memory(memory_keys), 1), later(Memory(memory_values), 7),
         later(gather(gate_weight1, up_weight1), 2), later(Gather([down1], pairs), 2),
         later(gather(out_weight1), 2), later(gather(second_query_weight, key_weight2, value_weight2), 2)],
    )
    qkv1_w, gains, rows, normed1, *heads1 = front
    own_docs = lax.dynamic_index_in_dim(docs, seg, 0, keepdims=False)
    own_mem_docs = lax.dynamic_index_in_dim(docs, seg + 2, 0, keepdims=False)
    reset = lax.dynamic_index_in_dim(memory_resets, seg, 0, keepdims=False)
    bounds, ranges = mask_ranges(own_docs, own_mem_docs, reset)
    gains = [gains[:, i].astype(F32)[None] for i in range(4)]
    hops = {}
    heads1, rest2 = join(heads1, rest2)
    hops["rest"] = gather_column(rest2)

    def rows1(out):
        ((attended,),) = exchange("to_rows_1", 3, [Swap([out], False)])
        attended, rest = join(attended, hops["rest"])
        hops["rest"] = rest, hop(rest, "a")
        return attended, out1_w, gu1_w, down1_w

    def rows2(out):
        out, rest = join(out, hops["rest"])
        blocks = (RowBlocks(count, 2 * ff), RowBlocks(count, width), pairs)
        (attended,), (gate_up_w, out_w, down_w) = exchange(
            "to_rows_2", 5, [Swap([out], False), Assemble(rest, blocks, pieces)]
        )
        attended, cot = join(attended, cotangent)
        hops["cot"] = rows_hops(cot)
        return attended, out_w, gate_up_w, down_w

    middle, weights1, kept1 = layer(
        rows, normed1, heads1, qkv1_w, (gains[0], gains[1]), rows1, None, bounds, ranges
    )
    normed2 = (middle * inverse_rms(middle) * gains[2]).astype(BF)
    qkv = jnp.dot(normed2, qkv2_w, preferred_element_type=F32).astype(BF)
    qkv, (column, first) = join(qkv, hops["rest"])
    hops["rest"] = column, first, hop(column, "b"), hop(first, "b")
    heads2, memory = exchange(
        "to_heads_2", 4, [Swap([qkv], True), Sort(memory_rank(own_mem_docs), mk, mv)]
    )
    result, weights2, kept2 = layer(
        middle, normed2, heads2, qkv2_w, (gains[2], gains[3]), rows2, memory, bounds, ranges
    )
    cot = hops["cot"]
    output = chunk_hops(result.astype(BF))

    def pair_sum(total):
        half = lax.dynamic_slice_in_dim(total, core * each, each, 0)
        other = hop(lax.dynamic_slice_in_dim(total, (1 - core) * each, each, 0), "core")
        return jnp.where(
            core == 0, jnp.concatenate((half, other), 1), jnp.concatenate((other, half), 1)
        )

    shapes = ((count, ff), (count, ff), (count, width), pairs.shape)

    def feed_sums(gate_g, up_g, down_g, out_g):
        return CoreSums((gate_g, own(gate_g)), (up_g, own(up_g)), (out_g, own(out_g)), (down_g, pairs))

    gate_g2, up_g2, down_g2, grad_mixed, grad_att, out_g2, gain_b2 = feed_back(
        cot, weights2, kept2
    )
    (grad_out,), sums2 = exchange(
        "back_to_heads_2", 6,
        [Swap([grad_att], True), feed_sums(gate_g2, up_g2, down_g2, out_g2)],
    )
    sums2 = scatter_second(sums2)
    q, k, v, out, stat = kept2[2:7]
    grads = attend_back(q, k, v, memory, bounds, ranges, out, stat, grad_out)
    ((grad_qkv,),) = exchange("back_to_rows_2", 7, [Swap(list(grads), False)])
    grad_qkv, (sums2, output) = join(grad_qkv, (sums2, output))
    sums2 = scatter_first(sums2)
    grad_middle, gain_a2, qkv_g2 = projections_back(grad_mixed, grad_qkv, weights2, kept2, F32)
    (qkv_s2,) = exchange("projection_sums_2", 12, [CoreSums((qkv_g2, own(qkv_g2)))])
    grad_middle, (sums2, qkv_s2) = join(grad_middle, (sums2, qkv_s2))
    sums2 = scatter_z(sums2)
    qkv_s2 = scatter_second(qkv_s2)

    gate_g1, up_g1, down_g1, grad_mixed, grad_att, out_g1, gain_b1 = feed_back(
        grad_middle, weights1, kept1
    )
    grad_att, qkv_s2 = join(grad_att, qkv_s2)
    qkv_s2 = scatter_first(qkv_s2)
    (grad_out,), wide1, rest1 = exchange(
        "back_to_heads_1", 8,
        [Swap([grad_att], True), CoreSums((gate_g1, own(gate_g1)), (up_g1, own(up_g1))),
         CoreSums((out_g1, own(out_g1)), (down_g1, pairs))],
    )
    grad_out, (sums2, qkv_s2) = join(grad_out, (sums2, qkv_s2))
    qkv_s2 = scatter_z(qkv_s2)
    wide1, rest1 = scatter_second(wide1), scatter_second(rest1)
    q, k, v, out, stat = kept1[2:7]
    grads = attend_back(q, k, v, None, bounds, ranges, out, stat, grad_out)
    grads, wide1 = join(grads, wide1)
    wide1 = scatter_first(wide1)
    ((grad_qkv,),) = exchange("back_to_rows_1", 9, [Swap(list(grads), False)])
    grad_qkv, (wide1, rest1, qkv_s2) = join(grad_qkv, (wide1, rest1, qkv_s2))
    rest1 = scatter_first(rest1)
    wide1 = scatter_z(wide1)
    grad_rows, gain_a1, qkv_g1 = projections_back(grad_mixed, grad_qkv, weights1, kept1, BF)
    gain_grads = gain_columns([g[0] for g in (gain_a1, gain_b1, gain_a2, gain_b2)]).astype(BF)
    (grad_tokens,), (out_s1, down_s1), (q_s1,), (k_s1,), (v_s1,), (gain_s,) = exchange(
        "back_to_owners", 10,
        [Chunks(grad_rows), LineSums(rest1, shapes[2:], ((0,), (1,)))]
        + [Scatter(qkv_g1, ColumnBlocks(count, width, i), i) for i in range(3)]
        + [Scatter(gain_grads, own(gain_grads))],
    )
    grad_tokens, wide1 = join(grad_tokens, wide1)
    gate_s1, up_s1 = unpack(scatter_end(wide1), shapes[:2])
    gate_s2, up_s2, out_s2, down_s2 = unpack(scatter_end(sums2), shapes)
    (qkv_s2,) = unpack(scatter_end(qkv_s2), ((count, 3 * width),))
    q_s2, k_s2, v_s2 = columns(qkv_s2, (width,) * 3)
    return (
        output, grad_tokens.astype(F32),
        gain_s[:, 0], q_s1, k_s1, v_s1, out_s1, gain_s[:, 1], gate_s1, up_s1, pair_sum(down_s1),
        gain_s[:, 2], q_s2, k_s2, v_s2, out_s2, gain_s[:, 3], gate_s2, up_s2, pair_sum(down_s2),
    )


def solution(mesh):
    in_specs = (
        P("grp", "key", None),
        P("grp", "key"),
        P("grp", "key"),
        P("grp"),
        P("grp", "key", None),
        P("grp", "key", None),
        P(("grp", "key")),
        P(("grp", "key"), None),
        P(("grp", "key"), None),
        P(("grp", "key"), None),
        P(("grp", "key"), None),
        P(("grp", "key")),
        P(("grp", "key"), None),
        P(("grp", "key"), None),
        P(("grp", "key"), None),
        P(("grp", "key")),
        P(("grp", "key"), None),
        P(("grp", "key"), None),
        P(("grp", "key"), None),
        P(("grp", "key"), None),
        P(("grp", "key")),
        P(("grp", "key"), None),
        P(("grp", "key"), None),
        P(("grp", "key"), None),
        P("grp", "key", None),
    )
    out_specs = (
        P("grp", "key", None),
        P("grp", "key", None),
        P(("grp", "key")),
        P(("grp", "key"), None),
        P(("grp", "key"), None),
        P(("grp", "key"), None),
        P(("grp", "key"), None),
        P(("grp", "key")),
        P(("grp", "key"), None),
        P(("grp", "key"), None),
        P(("grp", "key"), None),
        P(("grp", "key")),
        P(("grp", "key"), None),
        P(("grp", "key"), None),
        P(("grp", "key"), None),
        P(("grp", "key"), None),
        P(("grp", "key")),
        P(("grp", "key"), None),
        P(("grp", "key"), None),
        P(("grp", "key"), None),
    )
    body = head_local if dict(mesh.shape) == {"grp": 4, "key": HEADS} else gathered_local
    return jax.shard_map(body, mesh=mesh, in_specs=in_specs, out_specs=out_specs, check_vma=False)
```
